32 devices in a mesh: basin: 2 (over x), blk: 16 (over z, y, core).
Axes of the slice: x: 2, y: 2, z: 4, core: 2. Of those that a mesh axis runs over, the one named last changes fastest.
Arguments:
- tracers: bfloat16 [4096, 50, 128], P(('basin', 'blk')), may hold values from -6 to 6
- nbr_cols: int32 [4, 4096], P(None, ('basin', 'blk')), may hold values from 0 to 127
- nbr_wts: float32 [4, 50, 4096], P(None, None, ('basin', 'blk')), may hold values from 0.05 to 0.3
- self_wts: float32 [50, 4096], P(None, ('basin', 'blk')), may hold values from 0.2 to 0.9
- send_cols: int32 [3, 512], P(None, ('basin', 'blk')), may hold values from 0 to 127
- recv_cols: int32 [3, 512], P(None, ('basin', 'blk')), may hold values from 0 to 127
- edge_wts: float32 [3, 50, 512], P(None, None, ('basin', 'blk')), may hold values from 0.1 to 0.4
- wet_levels: int32 [4096], P(('basin', 'blk')), may hold values from 1 to 50
- vert_inv: bfloat16 [50, 50, 4096], P(None, None, ('basin', 'blk')), may hold values from -1 to 2
Outputs:
- advanced: bfloat16 [4096, 50, 128], P(('basin', 'blk'))
The draws below stay inside these ranges and needn't reach their ends.
Inputs may be any that keep to these rules, and one draw needn't show every extreme that they name: `nbr_cols`: local column indices within a block. `send_cols`: local column indices within the sending block. `recv_cols`: local column indices within the receiving block.
All inputs are finite; a program needn't handle non-finite values.
Results may differ from the reference program's by a relative error of at most 0.013.
Values may be sent and summed in bfloat16 or wider, within the bound.
No kernel may reach another device: no remote copies, remote signals or barrier semaphores. Data moves between devices by JAX's collectives and lax.ppermute only.
A program may use at most 64 MiB of HBM per device.

```python
import jax
import jax.numpy as jnp
from jax import lax

L = 50
TR = 128
COLS = 128
NBR = 4
EDGE = 16
NSTEP = 2
NCOLS = 4096
NEDGE = 512
N_BASIN = 2
N_BLK = 16


def draw_vert_inv(key, part):
    key = jax.random.fold_in(key, 11)
    noise = 0.05 * jax.random.normal(key, (L, L, NCOLS), jnp.float32)
    levels = jnp.arange(L)
    eye = (levels[:, None] == levels[None, :]).astype(jnp.float32)
    return (eye[:, :, None] + noise).astype(jnp.bfloat16)


def with_ends(result, stream_key, low, largest):
    index_at = [jax.random.randint(jax.random.fold_in(stream_key, axis), (), 0, length) for axis, length in enumerate(result.shape)]
    widest = result.shape.index(max(result.shape))
    neighbour = index_at[:widest] + [(index_at[widest] + 1) % result.shape[widest]] + index_at[widest + 1:]
    return result.at[tuple(index_at)].set(low).at[tuple(neighbour)].set(largest)


def shard_levels(stream_key, shape, cuts, least, largest):
    factor_of = 1.0
    for dim, blocks in cuts:
        draws = jax.random.uniform(jax.random.fold_in(jax.random.fold_in(stream_key, 6), dim), (blocks,), jnp.float32, least / len(cuts), largest / len(cuts))
        factor_of = factor_of * jnp.repeat(jnp.exp(draws), shape[dim] // blocks).reshape((-1,) + (1,) * (len(shape) - 1 - dim))
    return factor_of


def scatter_about(rng, shape, scale, limit, shards=(), held_as=jnp.bfloat16):
    drawn = jax.random.normal(rng, shape, jnp.float32) * scale
    if len(shards) > 0:
        drawn = shard_levels(rng, shape, shards, -0.22, 0.18) * drawn
    return jnp.clip(drawn, min=-limit, max=limit).astype(held_as)


def setup_inputs(seed: int = 0) -> dict:
    keys = jax.random.split(jax.random.key(seed), 10)
    tracers = scatter_about(keys[0], (NCOLS, L, TR), 1.0, 6.0, ((0, 32),))
    nbr_cols = with_ends(jax.random.randint(keys[1], (NBR, NCOLS), 0, COLS), jax.random.fold_in(keys[1], 1), 0, COLS - 1).astype(jnp.int32)
    nbr_wts = jnp.clip(0.05 + 0.25 * jax.random.uniform(keys[2], (NBR, L, NCOLS), jnp.float32) ** shard_levels(keys[2], (NBR, L, NCOLS), ((2, 32),), -0.2, 0.2), 0.05, 0.3)
    self_wts = jnp.clip(0.2 + 0.7 * jax.random.uniform(keys[3], (L, NCOLS), jnp.float32) ** shard_levels(keys[3], (L, NCOLS), ((1, 32),), -0.2, 0.2), 0.2, 0.9)
    send_cols = with_ends(jax.random.randint(keys[4], (3, NEDGE), 0, COLS), jax.random.fold_in(keys[4], 1), 0, COLS - 1).astype(jnp.int32)
    recv_cols = with_ends(jax.random.randint(keys[5], (3, NEDGE), 0, COLS), jax.random.fold_in(keys[5], 1), 0, COLS - 1).astype(jnp.int32)
    edge_wts = jnp.clip(0.1 + 0.3 * jax.random.uniform(keys[6], (3, L, NEDGE), jnp.float32) ** shard_levels(keys[6], (3, L, NEDGE), ((2, 32),), -0.2, 0.2), 0.1, 0.4)
    wet_levels = with_ends(jax.random.randint(keys[7], (NCOLS,), 1, L + 1), jax.random.fold_in(keys[7], 1), 1, L).astype(jnp.int32)
    vert_inv = draw_vert_inv(jax.random.fold_in(keys[9], 71), 0)
    return dict(tracers=tracers, nbr_cols=nbr_cols, nbr_wts=nbr_wts, self_wts=self_wts, send_cols=send_cols, recv_cols=recv_cols, edge_wts=edge_wts, wet_levels=wet_levels, vert_inv=vert_inv)


def reference(tracers, nbr_cols, nbr_wts, self_wts, send_cols, recv_cols, edge_wts, wet_levels, vert_inv):
    ndev = N_BASIN * N_BLK
    c_all = tracers.reshape(ndev, COLS, L, TR)
    nbr_all = nbr_cols.reshape(NBR, ndev, COLS).transpose(1, 0, 2)
    nw_all = nbr_wts.reshape(NBR, L, ndev, COLS).transpose(2, 0, 1, 3)
    sw_all = self_wts.reshape(L, ndev, COLS).transpose(1, 0, 2)
    snd_all = send_cols.reshape(3, ndev, EDGE).transpose(1, 0, 2)
    rcv_all = recv_cols.reshape(3, ndev, EDGE).transpose(1, 0, 2)
    ew_all = edge_wts.reshape(3, L, ndev, EDGE).transpose(2, 0, 1, 3)
    wet_all = wet_levels.reshape(ndev, COLS)
    vi_all = vert_inv.reshape(L, L, ndev, COLS).transpose(2, 0, 1, 3)
    levels = jnp.arange(L, dtype=jnp.int32)
    positions = jnp.arange(COLS, dtype=jnp.int32)

    def one_device(q, c_now):
        basin_idx = q // N_BLK
        blk_idx = q % N_BLK
        own = c_now[q].astype(jnp.float32)
        total = sw_all[q].T[:, :, None] * own
        onehot = (positions[None, :, None] == nbr_all[q][:, None, :]).astype(jnp.float32)
        nbr_op = jnp.einsum("nji,nli->lji", onehot, nw_all[q], precision=lax.Precision.HIGHEST).astype(jnp.bfloat16)
        total = total + jnp.einsum("lji,ilt->jlt", nbr_op.astype(jnp.float32), own, precision=lax.Precision.HIGHEST)
        sources = [q - 1, q + 1, ((basin_idx - 1 + N_BASIN) % N_BASIN) * N_BLK + blk_idx]
        valid = [blk_idx > 0, blk_idx < N_BLK - 1, blk_idx >= 0]
        for d in range(3):
            src = jnp.clip(sources[d], 0, ndev - 1).astype(jnp.int32)
            rows = c_now[src].astype(jnp.float32)[snd_all[src, d]]
            vals = ew_all[src, d].T[:, :, None] * rows
            seg = jax.ops.segment_sum(vals, rcv_all[src, d], num_segments=COLS)
            total = total + jnp.where(valid[d], seg, jnp.zeros_like(seg))
        mask = (levels[None, :] < wet_all[q][:, None]).astype(jnp.float32)
        explicit = (mask[:, :, None] * total).astype(jnp.bfloat16)
        mixed = jnp.einsum("mlc,cmt->clt", vi_all[q].astype(jnp.float32), explicit.astype(jnp.float32), precision=lax.Precision.HIGHEST)
        return (mask[:, :, None] * mixed).astype(jnp.bfloat16)

    for step in range(NSTEP):
        c_all = lax.map(lambda q: one_device(q, c_all), jnp.arange(ndev, dtype=jnp.int32))
    return c_all.reshape(NCOLS, L, TR)
```

```python
import functools

import jax
import jax.numpy as jnp
from jax import lax
from jax.experimental import pallas as pl
from jax.experimental.pallas import tpu as pltpu
from jax.sharding import PartitionSpec as P

NSTEP = 2
F32 = jnp.float32
BF16 = jnp.bfloat16


def padded(levels):
    return -(-(levels + 1) // 8) * 8


def direction(slot, parity):
    return 2 if slot == 2 else lax.bitwise_xor(parity, jnp.int32(slot))


def edge_tables(parity, edge_ref, recv_ref, wts, tbl):
    nedge, levels = edge_ref.shape[1:]
    wts[...] = jnp.zeros_like(wts)
    tbl[...] = jnp.zeros_like(tbl)
    for slot in range(3):
        d = direction(slot, parity)
        wts[slot * nedge : (slot + 1) * nedge, 0:levels] = edge_ref[d]
        tbl[slot : slot + 1, 0:nedge] = recv_ref[pl.ds(d, 1), :].astype(F32)
    return wts[...].T


def pack_edges(parity, levels, send_ref, weights, tbl, column, outs):
    rows = padded(levels)
    nedge, _, width = outs[0].shape
    is_level = lax.broadcasted_iota(jnp.int32, (rows, width), 0) < levels
    for slot, out in enumerate(outs):
        d = direction(slot, parity)
        table = jnp.broadcast_to(tbl[slot : slot + 1, :], (rows, width))
        for e in range(nedge):
            k = slot * nedge + e
            w = weights[0:rows, k : k + 1]
            out[e] = jnp.where(is_level, column(send_ref[d, e]) * w, table).astype(BF16)


def add_edges(edges, total, tbl_v, tbl_s, sem):
    levels_at = edges[0].shape[1] - 8
    for slot, ref in enumerate(edges):
        tbl_v[slot] = ref[0, levels_at:, :].astype(F32).astype(jnp.int32)
    copy = pltpu.make_async_copy(tbl_v, tbl_s, sem)
    copy.start()
    copy.wait()
    for slot, ref in enumerate(edges):
        for e in range(ref.shape[0]):
            j = tbl_s[slot, 7, e]
            total[j] = total[j] + ref[e].astype(F32)


def vertical(vt_ref, total, out):
    def column(j, _):
        rows = total[j]
        pad = jnp.zeros((64 - rows.shape[0], rows.shape[1]), F32)
        ex = jnp.concatenate([rows, pad], axis=0).astype(BF16)
        out[j] = jnp.dot(vt_ref[j][:, 0:64], ex, preferred_element_type=F32)
        return _
    lax.fori_loop(0, total.shape[0], column, 0, unroll=8)


def gather_kernel(blk, c_ref, send_ref, recv_ref, edge_ref, s0, s1, s2, cf, wts, tbl):
    levels, cols, width = c_ref.shape
    parity = lax.bitwise_and(lax.axis_index(blk), jnp.int32(1))
    weights = edge_tables(parity, edge_ref, recv_ref, wts, tbl)
    for l in range(levels):
        cf[l * cols : (l + 1) * cols, :] = c_ref[l].astype(F32)
    column = lambda s: cf[pl.ds(s, padded(levels), stride=cols), :]
    pack_edges(parity, levels, send_ref, weights, tbl, column, (s0, s1, s2))


def operator_kernel(c_ref, nbr_ref, nw_ref, sw_ref, wet_ref, v_ref, a_ref, ex_ref, vt_ref, exs, merged, vf, vts):
    levels, cols, width = c_ref.shape
    rows = padded(levels)
    nbr = nbr_ref.shape[0]
    lane = lax.broadcasted_iota(jnp.int32, (8, cols), 1)
    sub = lax.broadcasted_iota(jnp.int32, (8, cols), 0)
    target = jnp.where(sub == nbr, lane, -1)
    for n in range(nbr):
        target = jnp.where(sub == n, nbr_ref[n : n + 1, :], target)
    same = [(target == nbr_ref[n : n + 1, :]).astype(F32) for n in range(nbr)]
    same.append((target == lane).astype(F32))
    for l in range(levels):
        total = same[nbr] * sw_ref[l : l + 1, :]
        for n in range(nbr):
            total = total + same[n] * nw_ref[l, n : n + 1, :]
        merged[l] = total
    half = 16
    for jt in range(cols // half):
        j = lax.broadcasted_iota(jnp.int32, (half, cols), 0) + jt * half
        hits = [j == nbr_ref[n : n + 1, :] for n in range(nbr)]
        hits.append(j == lax.broadcasted_iota(jnp.int32, (half, cols), 1))
        def fill(l, _):
            value = jnp.zeros((half, cols), F32)
            for n in range(nbr, -1, -1):
                value = jnp.where(hits[n], merged[l, n : n + 1, :], value)
            a_ref[l, jt * half : (jt + 1) * half, :] = value.astype(BF16)
            return _
        lax.fori_loop(0, levels, fill, 0, unroll=5)
    for l in range(levels):
        exs[pl.ds(l, cols, stride=rows), :] = jnp.dot(a_ref[l], c_ref[l], preferred_element_type=F32)
    for l in range(levels, rows):
        exs[pl.ds(l, cols, stride=rows), :] = jnp.zeros((cols, width), F32)
    ex_ref[...] = exs[...].reshape(cols, rows, width)
    level = lax.broadcasted_iota(jnp.int32, (levels, cols), 0)
    wet = wet_ref[...]
    vf[...] = jnp.zeros_like(vf)
    for m in range(levels):
        keep = jnp.maximum(level, m) < wet
        vf[m * rows : m * rows + levels, :] = jnp.where(keep, v_ref[m].astype(F32), 0.0)
    for l in range(rows):
        block = vf[pl.ds(l, rows, stride=rows), :]
        block = jnp.concatenate([block, jnp.zeros((128 - rows, cols), F32)], axis=0)
        vts[pl.ds(l, cols, stride=rows), :] = block.T
    vt_ref[...] = vts[...].reshape(cols, rows, 128).astype(BF16)


def first_kernel(blk, r0, r1, r2, ex_ref, vt_ref, send_ref, recv_ref, edge_ref, c_ref, s0, s1, s2, exs, wts, tbl, tbl_v, tbl_s, sem):
    levels = edge_ref.shape[2]
    parity = lax.bitwise_and(lax.axis_index(blk), jnp.int32(1))
    weights = edge_tables(parity, edge_ref, recv_ref, wts, tbl)
    exs[...] = ex_ref[...]
    add_edges((r0, r1, r2), exs, tbl_v, tbl_s, sem)
    vertical(vt_ref, exs, c_ref)
    pack_edges(parity, levels, send_ref, weights, tbl, lambda s: c_ref[s], (s0, s1, s2))


def middle_kernel(c_ref, a_ref, ex_ref, cs, exs):
    levels = a_ref.shape[0]
    cols, rows, width = c_ref.shape
    cs[...] = c_ref[...].reshape(cols * rows, width)
    for l in range(levels):
        state = cs[pl.ds(l, cols, stride=rows), :].astype(BF16)
        exs[pl.ds(l, cols, stride=rows), :] = jnp.dot(a_ref[l], state, preferred_element_type=F32)
    for l in range(levels, rows):
        exs[pl.ds(l, cols, stride=rows), :] = jnp.zeros((cols, width), F32)
    ex_ref[...] = exs[...].reshape(cols, rows, width)


def last_kernel(r0, r1, r2, ex_ref, vt_ref, out_ref, exs, cs, tbl_v, tbl_s, sem):
    levels = out_ref.shape[0]
    cols, rows, width = ex_ref.shape
    exs[...] = ex_ref[...]
    add_edges((r0, r1, r2), exs, tbl_v, tbl_s, sem)
    def column(j, _):
        pad = jnp.zeros((64 - rows, width), F32)
        ex = jnp.concatenate([exs[j], pad], axis=0).astype(BF16)
        cs[pl.ds(pl.multiple_of(j * rows, 8), rows), :] = jnp.dot(vt_ref[j][:, 0:64], ex, preferred_element_type=F32)
        return _
    lax.fori_loop(0, cols, column, 0, unroll=8)
    for l in range(levels):
        out_ref[l] = cs[pl.ds(l, cols, stride=rows), :].astype(BF16)


VM = pl.BlockSpec(memory_space=pltpu.VMEM)
SM = pl.BlockSpec(memory_space=pltpu.SMEM)


def call(kernel, ins, specs, outs, scratch, limit, flops=0):
    size = sum(x.size * x.dtype.itemsize for x in (*ins, *outs))
    return pl.pallas_call(
        kernel,
        out_shape=outs,
        in_specs=specs,
        out_specs=[VM] * len(outs),
        scratch_shapes=scratch,
        compiler_params=pltpu.CompilerParams(vmem_limit_bytes=limit * 2**20),
        cost_estimate=pl.CostEstimate(flops=flops, bytes_accessed=size, transcendentals=0),
    )(*ins)


def swapped(values, blk, basin):
    n, b = lax.axis_size(blk), lax.axis_size(basin)
    out = []
    for slot in range(2):
        pairs = []
        for i in range(slot, n - 1, 2):
            pairs += [(i, i + 1), (i + 1, i)]
        out.append(lax.ppermute(values[slot], blk, pairs))
    out.append(lax.ppermute(values[2], basin, [(i, (i + 1) % b) for i in range(b)]))
    return out


def local(tracers, nbr_cols, nbr_wts, self_wts, send_cols, recv_cols, edge_wts, wet_levels, vert_inv):
    cols, levels, width = tracers.shape
    rows = padded(levels)
    nedge = send_cols.shape[1]
    shape = jax.ShapeDtypeStruct
    by_level = jnp.transpose(tracers, (1, 0, 2))
    nbr_by_level = jnp.transpose(nbr_wts, (1, 0, 2))
    edge_by_entry = jnp.transpose(edge_wts, (0, 2, 1))
    wet = wet_levels.reshape(1, cols)
    packed = [shape((nedge, rows, width), BF16)] * 3
    table_scratch = [pltpu.VMEM((128, 128), F32), pltpu.VMEM((8, 128), F32)]
    scatter_scratch = [pltpu.VMEM((3, 8, 128), jnp.int32), pltpu.SMEM((3, 8, 128), jnp.int32), pltpu.SemaphoreType.DMA]
    flat = pltpu.VMEM((cols * rows, width), F32)
    stack = pltpu.VMEM((cols, rows, width), F32)

    sends = call(
        functools.partial(gather_kernel, "blk"),
        (by_level, send_cols, recv_cols, edge_by_entry),
        [VM, SM, VM, VM], packed,
        [pltpu.VMEM((rows * cols, width), F32)] + table_scratch, 16,
    )
    received = swapped(sends, "blk", "basin")
    operator, explicit, vt = call(
        operator_kernel,
        (by_level, nbr_cols, nbr_by_level, self_wts, wet, vert_inv),
        [VM] * 6,
        [shape((levels, cols, cols), BF16), shape((cols, rows, width), F32), shape((cols, rows, 128), BF16)],
        [flat, pltpu.VMEM((levels, 8, cols), F32), pltpu.VMEM((rows * rows, cols), F32), pltpu.VMEM((cols * rows, 128), F32)], 32,
        flops=2 * levels * cols * cols * width,
    )
    state, *sends = call(
        functools.partial(first_kernel, "blk"),
        (*received, explicit, vt, send_cols, recv_cols, edge_by_entry),
        [VM] * 5 + [SM, VM, VM],
        [shape((cols, rows, width), F32)] + packed,
        [stack] + table_scratch + scatter_scratch, 32,
        flops=2 * cols * rows * rows * width,
    )
    received = swapped(sends, "blk", "basin")
    (explicit,) = call(
        middle_kernel, (state, operator), [VM] * 2, [shape((cols, rows, width), F32)], [flat, flat], 32,
        flops=2 * levels * cols * cols * width,
    )
    (out,) = call(
        last_kernel, (*received, explicit, vt), [VM] * 5, [shape((levels, cols, width), BF16)],
        [stack, flat] + scatter_scratch, 32,
        flops=2 * cols * rows * rows * width,
    )
    return jnp.transpose(out, (1, 0, 2))


def solution(mesh):
    in_specs = (
        P(("basin", "blk"), None, None),
        P(None, ("basin", "blk")),
        P(None, None, ("basin", "blk")),
        P(None, ("basin", "blk")),
        P(None, ("basin", "blk")),
        P(None, ("basin", "blk")),
        P(None, None, ("basin", "blk")),
        P(("basin", "blk")),
        P(None, None, ("basin", "blk")),
    )
    out_specs = P(("basin", "blk"), None, None)
    return jax.shard_map(local, mesh=mesh, in_specs=in_specs, out_specs=out_specs, check_vma=False)
```

```python
import functools

import jax
import jax.numpy as jnp
from jax import lax
from jax.experimental import pallas as pl
from jax.experimental.pallas import tpu as pltpu
from jax.sharding import PartitionSpec as P

NSTEP = 2
F32 = jnp.float32
BF16 = jnp.bfloat16


def padded(levels):
    return -(-(levels + 1) // 8) * 8


def direction(slot, parity):
    return 2 if slot == 2 else lax.bitwise_xor(parity, jnp.int32(slot))


def pack_edges(parity, levels, send, weights, tbl, column, outs):
    rows = padded(levels)
    nedge, _, width = outs[0].shape
    is_level = lax.broadcasted_iota(jnp.int32, (rows, width), 0) < levels
    for slot, out in enumerate(outs):
        d = direction(slot, parity)
        table = jnp.broadcast_to(tbl[slot : slot + 1, :], (rows, width))
        for e in range(nedge):
            k = slot * nedge + e
            w = weights[0:rows, k : k + 1]
            out[e] = jnp.where(is_level, column(send[d, e]) * w, table).astype(BF16)


def product(operator, x):
    pad = jnp.zeros((64 - x.shape[0], x.shape[1]), F32)
    x = jnp.concatenate([x.astype(F32), pad], axis=0).astype(BF16)
    return jnp.dot(operator[:, 0:64], x, preferred_element_type=F32)


def vertical(vt_ref, exs, out):
    cols, rows, _ = vt_ref.shape

    def column(j, _):
        out[j] = product(vt_ref[j], exs[pl.ds(pl.multiple_of(j * rows, 8), rows), :])
        return _

    lax.fori_loop(0, cols, column, 0, unroll=16)


def add_edges(edges, vt_ref, total, tbl_v, tbl_s, sem):
    levels_at = edges[0].shape[1] - 8
    for slot, ref in enumerate(edges):
        tbl_v[slot] = ref[0, levels_at:, :].astype(F32).astype(jnp.int32)
    copy = pltpu.make_async_copy(tbl_v, tbl_s, sem)
    copy.start()
    copy.wait()
    group = 4
    for slot, ref in enumerate(edges):
        for first in range(0, ref.shape[0], group):
            at = [tbl_s[slot, 7, e] for e in range(first, first + group)]
            parts = [product(vt_ref[j], ref[first + i]) for i, j in enumerate(at)]
            for j, part in zip(at, parts):
                total[j] = total[j] + part


def gather_kernel(
    blk, c_h, send_h, recv_h, edge_h, nbr_h, nw_h, sw_h, wet_h, v_h,
    s0, s1, s2, c_v, nbr_v, nw_v, sw_v, wet_v, v_v, wts_o, tbl_o,
    cf, wts, recv_v, edge_v, send_s, sems,
):
    levels, cols, width = c_h.shape
    nedge = edge_h.shape[1]
    pitch = cols + 8
    count = 5
    edges = [levels * i // count for i in range(count + 1)]
    pairs = [(send_h, send_s), (recv_h, recv_v), (edge_h, edge_v)]
    pairs += [(c_h.at[pl.ds(lo, hi - lo)], c_v.at[pl.ds(lo, hi - lo)]) for lo, hi in zip(edges, edges[1:])]
    pairs += [(nbr_h, nbr_v), (nw_h, nw_v), (sw_h, sw_v), (wet_h, wet_v), (v_h, v_v)]
    copies = [pltpu.make_async_copy(a, b, sems.at[i]) for i, (a, b) in enumerate(pairs)]
    for copy in copies:
        copy.start()
    parity = lax.bitwise_and(lax.axis_index(blk), jnp.int32(1))
    wts[...] = jnp.zeros_like(wts)
    tbl_o[...] = jnp.zeros_like(tbl_o)
    for copy in copies[:3]:
        copy.wait()
    for slot in range(3):
        d = direction(slot, parity)
        wts[slot * nedge : (slot + 1) * nedge, 0:levels] = edge_v[d]
        tbl_o[slot : slot + 1, 0:nedge] = recv_v[pl.ds(d, 1), :].astype(F32)
    weights = wts[...].T
    wts_o[...] = weights
    for i, (lo, hi) in enumerate(zip(edges, edges[1:])):
        copies[3 + i].wait()
        for l in range(lo, hi):
            cf[l * pitch : l * pitch + cols, :] = c_v[l].astype(F32)
    column = lambda s: cf[pl.ds(s, padded(levels), stride=pitch), :]
    pack_edges(parity, levels, send_s, weights, tbl_o, column, (s0, s1, s2))
    for copy in copies[3 + count :]:
        copy.wait()


def operator_kernel(c_ref, nbr_ref, nw_ref, sw_ref, wet_ref, v_ref, a_ref, state_ref, vt_ref, exs, merged, vf, vts):
    levels, cols, width = c_ref.shape
    rows = padded(levels)
    nbr = nbr_ref.shape[0]
    lane = lax.broadcasted_iota(jnp.int32, (8, cols), 1)
    sub = lax.broadcasted_iota(jnp.int32, (8, cols), 0)
    target = jnp.where(sub == nbr, lane, -1)
    for n in range(nbr):
        target = jnp.where(sub == n, nbr_ref[n : n + 1, :], target)
    same = [(target == nbr_ref[n : n + 1, :]).astype(F32) for n in range(nbr)]
    same.append((target == lane).astype(F32))
    for l in range(levels):
        total = same[nbr] * sw_ref[l : l + 1, :]
        for n in range(nbr):
            total = total + same[n] * nw_ref[l, n : n + 1, :]
        merged[l] = total
    half = 16
    for jt in range(cols // half):
        j = lax.broadcasted_iota(jnp.int32, (half, cols), 0) + jt * half
        hits = [j == nbr_ref[n : n + 1, :] for n in range(nbr)]
        hits.append(j == lax.broadcasted_iota(jnp.int32, (half, cols), 1))

        def fill(l, _):
            value = jnp.zeros((half, cols), F32)
            for n in range(nbr, -1, -1):
                value = jnp.where(hits[n], merged[l, n : n + 1, :], value)
            a_ref[l, jt * half : (jt + 1) * half, :] = value.astype(BF16)
            return _

        lax.fori_loop(0, levels, fill, 0, unroll=5)
    for l in range(levels):
        exs[pl.ds(l, cols, stride=rows), :] = jnp.dot(a_ref[l], c_ref[l], preferred_element_type=F32)
    for l in range(levels, rows):
        exs[pl.ds(l, cols, stride=rows), :] = jnp.zeros((cols, width), F32)
    level = lax.broadcasted_iota(jnp.int32, (levels, cols), 0)
    wet = wet_ref[...]
    vf[...] = jnp.zeros_like(vf)
    for m in range(levels):
        keep = jnp.maximum(level, m) < wet
        vf[m * rows : m * rows + levels, :] = jnp.where(keep, v_ref[m].astype(F32), 0.0)
    for l in range(rows):
        block = vf[pl.ds(l, rows, stride=rows), :]
        block = jnp.concatenate([block, jnp.zeros((128 - rows, cols), F32)], axis=0)
        vts[pl.ds(l, cols, stride=rows), :] = block.T
    vt_ref[...] = vts[...].reshape(cols, rows, 128).astype(BF16)
    vertical(vt_ref, exs, state_ref)


def first_kernel(blk, levels, r0, r1, r2, local_ref, vt_ref, wts_ref, tbl_ref, send_h, state_ref, s0, s1, s2, tbl_v, tbl_s, send_s, sems):
    copy = pltpu.make_async_copy(send_h, send_s, sems.at[1])
    copy.start()
    parity = lax.bitwise_and(lax.axis_index(blk), jnp.int32(1))
    add_edges((r0, r1, r2), vt_ref, state_ref, tbl_v, tbl_s, sems.at[0])
    copy.wait()
    pack_edges(parity, levels, send_s, wts_ref, tbl_ref, lambda s: state_ref[s], (s0, s1, s2))


def middle_kernel(c_ref, a_ref, vt_ref, out_ref, cs, exs):
    levels = a_ref.shape[0]
    cols, rows, width = c_ref.shape
    cs[...] = c_ref[...].reshape(cols * rows, width)
    for l in range(levels):
        state = cs[pl.ds(l, cols, stride=rows), :].astype(BF16)
        exs[pl.ds(l, cols, stride=rows), :] = jnp.dot(a_ref[l], state, preferred_element_type=F32)
    for l in range(levels, rows):
        exs[pl.ds(l, cols, stride=rows), :] = jnp.zeros((cols, width), F32)
    vertical(vt_ref, exs, out_ref)


def last_kernel(r0, r1, r2, local_ref, vt_ref, out_h, total, cs, out_v, tbl_v, tbl_s, sems):
    levels = out_h.shape[0]
    cols, rows, width = total.shape
    add_edges((r0, r1, r2), vt_ref, total, tbl_v, tbl_s, sems.at[0])
    cs[...] = total[...].reshape(cols * rows, width)
    count = 5
    edges = [levels * i // count for i in range(count + 1)]
    copies = []
    for i, (lo, hi) in enumerate(zip(edges, edges[1:])):
        for l in range(lo, hi):
            out_v[l] = cs[pl.ds(l, cols, stride=rows), :].astype(BF16)
        copies.append(pltpu.make_async_copy(out_v.at[pl.ds(lo, hi - lo)], out_h.at[pl.ds(lo, hi - lo)], sems.at[1 + i]))
        copies[-1].start()
    for copy in copies:
        copy.wait()


VM = pl.BlockSpec(memory_space=pltpu.VMEM)
HB = pl.BlockSpec(memory_space=pltpu.HBM)
DMA = pltpu.SemaphoreType.DMA


def call(kernel, ins, specs, outs, out_specs, scratch, limit, flops=0, aliases=None):
    size = sum(x.size * x.dtype.itemsize for x in (*ins, *outs))
    return pl.pallas_call(
        kernel,
        out_shape=outs,
        in_specs=specs,
        out_specs=out_specs,
        scratch_shapes=scratch,
        input_output_aliases=aliases or {},
        compiler_params=pltpu.CompilerParams(vmem_limit_bytes=limit * 2**20),
        cost_estimate=pl.CostEstimate(flops=flops, bytes_accessed=size, transcendentals=0),
    )(*ins)


def swapped(values, blk, basin):
    n, b = lax.axis_size(blk), lax.axis_size(basin)
    third = lax.ppermute(values[2], basin, [(i, (i + 1) % b) for i in range(b)])
    out = []
    for slot in (1, 0):
        pairs = []
        for i in range(slot, n - 1, 2):
            pairs += [(i, i + 1), (i + 1, i)]
        out.append(lax.ppermute(values[slot], blk, pairs))
    return out[1], out[0], third


def local(tracers, nbr_cols, nbr_wts, self_wts, send_cols, recv_cols, edge_wts, wet_levels, vert_inv):
    cols, levels, width = tracers.shape
    rows = padded(levels)
    nedge = send_cols.shape[1]
    shape = jax.ShapeDtypeStruct
    by_level = jnp.transpose(tracers, (1, 0, 2))
    nbr_by_level = jnp.transpose(nbr_wts, (1, 0, 2))
    edge_by_entry = jnp.transpose(edge_wts, (0, 2, 1))
    wet = wet_levels.reshape(1, cols)
    in_hbm = lambda x: pltpu.with_memory_space_constraint(x, pltpu.HBM)
    send_h = in_hbm(send_cols)
    loads = [by_level, nbr_cols, nbr_by_level, self_wts, wet, vert_inv]
    same = lambda x: shape(x.shape, x.dtype)
    packed = [shape((nedge, rows, width), BF16)] * 3
    flat = pltpu.VMEM((cols * rows, width), F32)
    columns = shape((cols, rows, width), F32)
    tables = [pltpu.VMEM((3, 8, 128), jnp.int32), pltpu.SMEM((3, 8, 128), jnp.int32)]

    first = call(
        functools.partial(gather_kernel, "blk"),
        (in_hbm(by_level), send_h, *map(in_hbm, (recv_cols, edge_by_entry, *loads[1:]))),
        [HB] * 9,
        packed + [same(x) for x in loads] + [shape((128, 128), F32), shape((8, 128), F32)],
        [VM] * 11,
        [
            pltpu.VMEM((rows * (cols + 8), width), F32), pltpu.VMEM((128, 128), F32),
            pltpu.VMEM(recv_cols.shape, jnp.int32), pltpu.VMEM(edge_by_entry.shape, F32),
            pltpu.SMEM(send_cols.shape, jnp.int32), DMA((13,)),
        ],
        16,
    )
    sends, loads, (wts, tbl) = first[:3], first[3:9], first[9:]
    received = swapped(sends, "blk", "basin")
    operator, partial, vt = call(
        operator_kernel, loads, [VM] * 6,
        [shape((levels, cols, cols), BF16), columns, shape((cols, rows, 128), BF16)], [VM] * 3,
        [flat, pltpu.VMEM((levels, 8, cols), F32), pltpu.VMEM((rows * rows, cols), F32), pltpu.VMEM((cols * rows, 128), F32)],
        32, flops=2 * levels * cols * cols * width,
    )
    state, *sends = call(
        functools.partial(first_kernel, "blk", levels),
        (*received, partial, vt, wts, tbl, send_h), [VM] * 7 + [HB],
        [columns] + packed, [VM] * 4,
        tables + [pltpu.SMEM(send_cols.shape, jnp.int32), DMA((2,))], 16,
        flops=2 * cols * rows * rows * width, aliases={3: 0},
    )
    received = swapped(sends, "blk", "basin")
    (partial,) = call(
        middle_kernel, (state, operator, vt), [VM] * 3, [columns], [VM], [flat, flat], 32,
        flops=2 * levels * cols * cols * width,
    )
    out, _ = call(
        last_kernel, (*received, partial, vt), [VM] * 5,
        [shape((levels, cols, width), BF16), columns], [HB, VM],
        [flat, pltpu.VMEM((levels, cols, width), BF16)] + tables + [DMA((6,))], 16,
        flops=2 * cols * rows * rows * width, aliases={3: 1},
    )
    return jnp.transpose(out, (1, 0, 2))


def solution(mesh):
    in_specs = (
        P(("basin", "blk"), None, None),
        P(None, ("basin", "blk")),
        P(None, None, ("basin", "blk")),
        P(None, ("basin", "blk")),
        P(None, ("basin", "blk")),
        P(None, ("basin", "blk")),
        P(None, None, ("basin", "blk")),
        P(("basin", "blk")),
        P(None, None, ("basin", "blk")),
    )
    out_specs = P(("basin", "blk"), None, None)
    return jax.shard_map(local, mesh=mesh, in_specs=in_specs, out_specs=out_specs, check_vma=False)
```

```python
import functools

import jax
import jax.numpy as jnp
from jax import lax
from jax.experimental import pallas as pl
from jax.experimental.pallas import tpu as pltpu
from jax.sharding import PartitionSpec as P

NSTEP = 2
F32 = jnp.float32
BF16 = jnp.bfloat16


def padded(levels):
    return -(-(levels + 1) // 8) * 8


def direction(slot, parity):
    return 2 if slot == 1 else lax.bitwise_xor(parity, jnp.int32(1 - slot // 2))


def pack_edges(parity, levels, send, weights, tbl, column, outs):
    rows = padded(levels)
    nedge, _, width = outs[0].shape
    is_level = lax.broadcasted_iota(jnp.int32, (rows, width), 0) < levels
    for slot, out in enumerate(outs):
        d = direction(slot, parity)
        table = jnp.broadcast_to(tbl[slot : slot + 1, :], (rows, width))
        for e in range(nedge):
            k = slot * nedge + e
            w = weights[0:rows, k : k + 1]
            out[e] = jnp.where(is_level, column(send[d, e]) * w, table).astype(BF16)


def product(operator, x):
    pad = jnp.zeros((64 - x.shape[0], x.shape[1]), F32)
    x = jnp.concatenate([x.astype(F32), pad], axis=0).astype(BF16)
    return jnp.dot(operator[:, 0:64], x, preferred_element_type=F32)


def vertical(vt_ref, exs, out):
    cols, rows, _ = vt_ref.shape

    def column(j, _):
        out[j] = product(vt_ref[j], exs[pl.ds(pl.multiple_of(j * rows, 8), rows), :])
        return _

    lax.fori_loop(0, cols, column, 0, unroll=16)


def add_edges(edges, vt_ref, total, tbl_v, tbl_s, sem):
    levels_at = edges[0].shape[1] - 8
    for slot, ref in enumerate(edges):
        tbl_v[slot] = ref[0, levels_at:, :].astype(F32).astype(jnp.int32)
    copy = pltpu.make_async_copy(tbl_v, tbl_s, sem)
    copy.start()
    copy.wait()
    group = 4
    for slot, ref in enumerate(edges):
        for first in range(0, ref.shape[0], group):
            at = [tbl_s[slot, 7, e] for e in range(first, first + group)]
            parts = [product(vt_ref[j], ref[first + i]) for i, j in enumerate(at)]
            for j, part in zip(at, parts):
                total[j] = total[j] + part


def gather_kernel(
    blk, c_h, send_h, recv_h, edge_h, nbr_h, nw_h, sw_h, wet_h, v_h,
    s0, s1, s2, c_v, nbr_v, nw_v, sw_v, wet_v, v_v, wts_o, tbl_o,
    cf, wts, recv_v, edge_v, send_s, sems,
):
    levels, cols, width = c_h.shape
    nedge = edge_h.shape[1]
    pitch = cols + 8
    count = 5
    edges = [levels * i // count for i in range(count + 1)]
    pairs = [(send_h, send_s), (recv_h, recv_v), (edge_h, edge_v)]
    pairs += [(c_h.at[pl.ds(lo, hi - lo)], c_v.at[pl.ds(lo, hi - lo)]) for lo, hi in zip(edges, edges[1:])]
    pairs += [(nbr_h, nbr_v), (nw_h, nw_v), (sw_h, sw_v), (wet_h, wet_v), (v_h, v_v)]
    copies = [pltpu.make_async_copy(a, b, sems.at[i]) for i, (a, b) in enumerate(pairs)]
    for copy in copies:
        copy.start()
    parity = lax.bitwise_and(lax.axis_index(blk), jnp.int32(1))
    wts[...] = jnp.zeros_like(wts)
    tbl_o[...] = jnp.zeros_like(tbl_o)
    for copy in copies[:3]:
        copy.wait()
    for slot in range(3):
        d = direction(slot, parity)
        wts[slot * nedge : (slot + 1) * nedge, 0:levels] = edge_v[d]
        tbl_o[slot : slot + 1, 0:nedge] = recv_v[pl.ds(d, 1), :].astype(F32)
    weights = wts[...].T
    wts_o[...] = weights
    for i, (lo, hi) in enumerate(zip(edges, edges[1:])):
        copies[3 + i].wait()
        for l in range(lo, hi):
            cf[l * pitch : l * pitch + cols, :] = c_v[l].astype(F32)
    column = lambda s: cf[pl.ds(s, padded(levels), stride=pitch), :]
    pack_edges(parity, levels, send_s, weights, tbl_o, column, (s0, s1, s2))
    for copy in copies[3 + count :]:
        copy.wait()


def operator_kernel(c_ref, nbr_ref, nw_ref, sw_ref, wet_ref, v_ref, a_ref, state_ref, vt_ref, exs, merged, vf, vts):
    levels, cols, width = c_ref.shape
    rows = padded(levels)
    nbr = nbr_ref.shape[0]
    lane = lax.broadcasted_iota(jnp.int32, (8, cols), 1)
    sub = lax.broadcasted_iota(jnp.int32, (8, cols), 0)
    target = jnp.where(sub == nbr, lane, -1)
    for n in range(nbr):
        target = jnp.where(sub == n, nbr_ref[n : n + 1, :], target)
    same = [(target == nbr_ref[n : n + 1, :]).astype(F32) for n in range(nbr)]
    same.append((target == lane).astype(F32))
    for l in range(levels):
        total = same[nbr] * sw_ref[l : l + 1, :]
        for n in range(nbr):
            total = total + same[n] * nw_ref[l, n : n + 1, :]
        merged[l] = total
    half = 16
    for jt in range(cols // half):
        j = lax.broadcasted_iota(jnp.int32, (half, cols), 0) + jt * half
        hits = [j == nbr_ref[n : n + 1, :] for n in range(nbr)]
        hits.append(j == lax.broadcasted_iota(jnp.int32, (half, cols), 1))

        def fill(l, _):
            value = jnp.zeros((half, cols), F32)
            for n in range(nbr, -1, -1):
                value = jnp.where(hits[n], merged[l, n : n + 1, :], value)
            a_ref[l, jt * half : (jt + 1) * half, :] = value.astype(BF16)
            return _

        lax.fori_loop(0, levels, fill, 0, unroll=5)
    for l in range(levels):
        exs[pl.ds(l, cols, stride=rows), :] = jnp.dot(a_ref[l], c_ref[l], preferred_element_type=F32)
    for l in range(levels, rows):
        exs[pl.ds(l, cols, stride=rows), :] = jnp.zeros((cols, width), F32)
    level = lax.broadcasted_iota(jnp.int32, (levels, cols), 0)
    wet = wet_ref[...]
    vf[...] = jnp.zeros_like(vf)
    for m in range(levels):
        keep = jnp.maximum(level, m) < wet
        vf[m * rows : m * rows + levels, :] = jnp.where(keep, v_ref[m].astype(F32), 0.0)
    for l in range(rows):
        block = vf[pl.ds(l, rows, stride=rows), :]
        block = jnp.concatenate([block, jnp.zeros((128 - rows, cols), F32)], axis=0)
        vts[pl.ds(l, cols, stride=rows), :] = block.T
    vt_ref[...] = vts[...].reshape(cols, rows, 128).astype(BF16)
    vertical(vt_ref, exs, state_ref)


def first_kernel(blk, levels, r0, r1, r2, local_ref, vt_ref, wts_ref, tbl_ref, send_h, state_ref, s0, s1, s2, tbl_v, tbl_s, send_s, sems):
    copy = pltpu.make_async_copy(send_h, send_s, sems.at[1])
    copy.start()
    parity = lax.bitwise_and(lax.axis_index(blk), jnp.int32(1))
    add_edges((r0, r1, r2), vt_ref, state_ref, tbl_v, tbl_s, sems.at[0])
    copy.wait()
    pack_edges(parity, levels, send_s, wts_ref, tbl_ref, lambda s: state_ref[s], (s0, s1, s2))


def middle_kernel(c_ref, a_ref, vt_ref, out_ref, cs, exs):
    levels = a_ref.shape[0]
    cols, rows, width = c_ref.shape
    cs[...] = c_ref[...].reshape(cols * rows, width)
    for l in range(levels):
        state = cs[pl.ds(l, cols, stride=rows), :].astype(BF16)
        exs[pl.ds(l, cols, stride=rows), :] = jnp.dot(a_ref[l], state, preferred_element_type=F32)
    for l in range(levels, rows):
        exs[pl.ds(l, cols, stride=rows), :] = jnp.zeros((cols, width), F32)
    vertical(vt_ref, exs, out_ref)


def last_kernel(r0, r1, r2, local_ref, vt_ref, out_h, total, cs, out_v, tbl_v, tbl_s, sems):
    levels = out_h.shape[0]
    cols, rows, width = total.shape
    add_edges((r0, r1, r2), vt_ref, total, tbl_v, tbl_s, sems.at[0])
    cs[...] = total[...].reshape(cols * rows, width)
    count = 5
    edges = [levels * i // count for i in range(count + 1)]
    copies = []
    for i, (lo, hi) in enumerate(zip(edges, edges[1:])):
        for l in range(lo, hi):
            out_v[l] = cs[pl.ds(l, cols, stride=rows), :].astype(BF16)
        copies.append(pltpu.make_async_copy(out_v.at[pl.ds(lo, hi - lo)], out_h.at[pl.ds(lo, hi - lo)], sems.at[1 + i]))
        copies[-1].start()
    for copy in copies:
        copy.wait()


VM = pl.BlockSpec(memory_space=pltpu.VMEM)
HB = pl.BlockSpec(memory_space=pltpu.HBM)
DMA = pltpu.SemaphoreType.DMA


def call(kernel, ins, specs, outs, out_specs, scratch, limit, flops=0, aliases=None):
    size = sum(x.size * x.dtype.itemsize for x in (*ins, *outs))
    return pl.pallas_call(
        kernel,
        out_shape=outs,
        in_specs=specs,
        out_specs=out_specs,
        scratch_shapes=scratch,
        input_output_aliases=aliases or {},
        compiler_params=pltpu.CompilerParams(vmem_limit_bytes=limit * 2**20),
        cost_estimate=pl.CostEstimate(flops=flops, bytes_accessed=size, transcendentals=0),
    )(*ins)


def swapped(values, blk, basin):
    n, b = lax.axis_size(blk), lax.axis_size(basin)
    pairs = lambda first: [pair for i in range(first, n - 1, 2) for pair in ((i, i + 1), (i + 1, i))]
    return (
        lax.ppermute(values[0], blk, pairs(1)),
        lax.ppermute(values[1], basin, [(i, (i + 1) % b) for i in range(b)]),
        lax.ppermute(values[2], blk, pairs(0)),
    )


def local(tracers, nbr_cols, nbr_wts, self_wts, send_cols, recv_cols, edge_wts, wet_levels, vert_inv):
    cols, levels, width = tracers.shape
    rows = padded(levels)
    nedge = send_cols.shape[1]
    shape = jax.ShapeDtypeStruct
    by_level = jnp.transpose(tracers, (1, 0, 2))
    nbr_by_level = jnp.transpose(nbr_wts, (1, 0, 2))
    edge_by_entry = jnp.transpose(edge_wts, (0, 2, 1))
    wet = wet_levels.reshape(1, cols)
    in_hbm = lambda x: pltpu.with_memory_space_constraint(x, pltpu.HBM)
    send_h = in_hbm(send_cols)
    loads = [by_level, nbr_cols, nbr_by_level, self_wts, wet, vert_inv]
    same = lambda x: shape(x.shape, x.dtype)
    packed = [shape((nedge, rows, width), BF16)] * 3
    flat = pltpu.VMEM((cols * rows, width), F32)
    columns = shape((cols, rows, width), F32)
    tables = [pltpu.VMEM((3, 8, 128), jnp.int32), pltpu.SMEM((3, 8, 128), jnp.int32)]

    first = call(
        functools.partial(gather_kernel, "blk"),
        (in_hbm(by_level), send_h, *map(in_hbm, (recv_cols, edge_by_entry, *loads[1:]))),
        [HB] * 9,
        packed + [same(x) for x in loads] + [shape((128, 128), F32), shape((8, 128), F32)],
        [VM] * 11,
        [
            pltpu.VMEM((rows * (cols + 8), width), F32), pltpu.VMEM((128, 128), F32),
            pltpu.VMEM(recv_cols.shape, jnp.int32), pltpu.VMEM(edge_by_entry.shape, F32),
            pltpu.SMEM(send_cols.shape, jnp.int32), DMA((13,)),
        ],
        16,
    )
    sends, loads, (wts, tbl) = first[:3], first[3:9], first[9:]
    received = swapped(sends, "blk", "basin")
    operator, partial, vt = call(
        operator_kernel, loads, [VM] * 6,
        [shape((levels, cols, cols), BF16), columns, shape((cols, rows, 128), BF16)], [VM] * 3,
        [flat, pltpu.VMEM((levels, 8, cols), F32), pltpu.VMEM((rows * rows, cols), F32), pltpu.VMEM((cols * rows, 128), F32)],
        32, flops=2 * levels * cols * cols * width,
    )
    state, *sends = call(
        functools.partial(first_kernel, "blk", levels),
        (*received, partial, vt, wts, tbl, send_h), [VM] * 7 + [HB],
        [columns] + packed, [VM] * 4,
        tables + [pltpu.SMEM(send_cols.shape, jnp.int32), DMA((2,))], 16,
        flops=2 * cols * rows * rows * width, aliases={3: 0},
    )
    received = swapped(sends, "blk", "basin")
    (partial,) = call(
        middle_kernel, (state, operator, vt), [VM] * 3, [columns], [VM], [flat, flat], 32,
        flops=2 * levels * cols * cols * width,
    )
    out, _ = call(
        last_kernel, (*received, partial, vt), [VM] * 5,
        [shape((levels, cols, width), BF16), columns], [HB, VM],
        [flat, pltpu.VMEM((levels, cols, width), BF16)] + tables + [DMA((6,))], 16,
        flops=2 * cols * rows * rows * width, aliases={3: 1},
    )
    return jnp.transpose(out, (1, 0, 2))


def solution(mesh):
    in_specs = (
        P(("basin", "blk"), None, None),
        P(None, ("basin", "blk")),
        P(None, None, ("basin", "blk")),
        P(None, ("basin", "blk")),
        P(None, ("basin", "blk")),
        P(None, ("basin", "blk")),
        P(None, None, ("basin", "blk")),
        P(("basin", "blk")),
        P(None, None, ("basin", "blk")),
    )
    out_specs = P(("basin", "blk"), None, None)
    return jax.shard_map(local, mesh=mesh, in_specs=in_specs, out_specs=out_specs, check_vma=False)
```

```python
import functools

import jax
import jax.numpy as jnp
from jax import lax
from jax.experimental import pallas as pl
from jax.experimental.pallas import tpu as pltpu
from jax.sharding import PartitionSpec as P

NSTEP = 2
F32 = jnp.float32
BF16 = jnp.bfloat16


def padded(levels):
    return -(-(levels + 1) // 8) * 8


def direction(slot, parity):
    return 2 if slot == 1 else lax.bitwise_xor(parity, jnp.int32(1 - slot // 2))


def has_partner(slot, at, count):
    first = lax.bitwise_and(at + slot // 2, jnp.int32(1)) == 1
    return jnp.where(first, at + 1 < count, at > 0)


def pack_edges(parity, levels, send, weights, tbl, column, outs):
    rows = padded(levels)
    nedge, _, width = outs[0].shape
    is_level = lax.broadcasted_iota(jnp.int32, (rows, width), 0) < levels
    for slot, out in enumerate(outs):
        d = direction(slot, parity)
        table = jnp.broadcast_to(tbl[slot : slot + 1, :], (rows, width))
        for e in range(nedge):
            k = slot * nedge + e
            w = weights[0:rows, k : k + 1]
            out[e] = jnp.where(is_level, column(send[d, e]) * w, table).astype(BF16)


def product(operator, x):
    pad = jnp.zeros((64 - x.shape[0], x.shape[1]), F32)
    x = jnp.concatenate([x.astype(F32), pad], axis=0).astype(BF16)
    return jnp.dot(operator[:, 0:64], x, preferred_element_type=F32)


def vertical(vt_ref, exs, out):
    cols, rows, _ = vt_ref.shape

    def column(j, _):
        out[j] = product(vt_ref[j], exs[pl.ds(pl.multiple_of(j * rows, 8), rows), :])
        return _

    lax.fori_loop(0, cols, column, 0, unroll=16)


def add_edges(edges, vt_ref, total, tbl_v, tbl_s, sem):
    levels_at = edges[0].shape[1] - 8
    for slot, ref in enumerate(edges):
        tbl_v[slot] = ref[0, levels_at:, :].astype(F32).astype(jnp.int32)
    copy = pltpu.make_async_copy(tbl_v, tbl_s, sem)
    copy.start()
    copy.wait()
    group = 4
    for slot, ref in enumerate(edges):
        for first in range(0, ref.shape[0], group):
            at = [tbl_s[slot, 7, e] for e in range(first, first + group)]
            parts = [product(vt_ref[j], ref[first + i]) for i, j in enumerate(at)]
            for j, part in zip(at, parts):
                total[j] = total[j] + part


def gather_kernel(
    blk, c_h, send_h, recv_h, edge_h, nbr_h, nw_h, sw_h, wet_h, v_h,
    s0, s1, s2, c_v, nbr_v, nw_v, sw_v, wet_v, v_v, wts_o, tbl_o,
    cf, wts, recv_v, edge_v, send_s, sems,
):
    levels, cols, width = c_h.shape
    nedge = edge_h.shape[1]
    pitch = cols + 8
    count = 5
    edges = [levels * i // count for i in range(count + 1)]
    pairs = [(send_h, send_s), (recv_h, recv_v), (edge_h, edge_v)]
    pairs += [(c_h.at[pl.ds(lo, hi - lo)], c_v.at[pl.ds(lo, hi - lo)]) for lo, hi in zip(edges, edges[1:])]
    pairs += [(nbr_h, nbr_v), (nw_h, nw_v), (sw_h, sw_v), (wet_h, wet_v), (v_h, v_v)]
    copies = [pltpu.make_async_copy(a, b, sems.at[i]) for i, (a, b) in enumerate(pairs)]
    for copy in copies:
        copy.start()
    parity = lax.bitwise_and(lax.axis_index(blk), jnp.int32(1))
    wts[...] = jnp.zeros_like(wts)
    tbl_o[...] = jnp.zeros_like(tbl_o)
    for copy in copies[:3]:
        copy.wait()
    for slot in range(3):
        d = direction(slot, parity)
        weight = edge_v[d]
        if slot != 1:
            weight = jnp.where(has_partner(slot, lax.axis_index(blk), lax.axis_size(blk)), weight, 0.0)
        wts[slot * nedge : (slot + 1) * nedge, 0:levels] = weight
        tbl_o[slot : slot + 1, 0:nedge] = recv_v[pl.ds(d, 1), :].astype(F32)
    weights = wts[...].T
    wts_o[...] = weights
    for i, (lo, hi) in enumerate(zip(edges, edges[1:])):
        copies[3 + i].wait()
        for l in range(lo, hi):
            cf[l * pitch : l * pitch + cols, :] = c_v[l].astype(F32)
    column = lambda s: cf[pl.ds(s, padded(levels), stride=pitch), :]
    pack_edges(parity, levels, send_s, weights, tbl_o, column, (s0, s1, s2))
    for copy in copies[3 + count :]:
        copy.wait()


def operator_kernel(c_ref, nbr_ref, nw_ref, sw_ref, wet_ref, v_ref, a_ref, state_ref, vt_ref, exs, merged, vf, vts):
    levels, cols, width = c_ref.shape
    rows = padded(levels)
    nbr = nbr_ref.shape[0]
    lane = lax.broadcasted_iota(jnp.int32, (8, cols), 1)
    sub = lax.broadcasted_iota(jnp.int32, (8, cols), 0)
    target = jnp.where(sub == nbr, lane, -1)
    for n in range(nbr):
        target = jnp.where(sub == n, nbr_ref[n : n + 1, :], target)
    same = [(target == nbr_ref[n : n + 1, :]).astype(F32) for n in range(nbr)]
    same.append((target == lane).astype(F32))
    for l in range(levels):
        total = same[nbr] * sw_ref[l : l + 1, :]
        for n in range(nbr):
            total = total + same[n] * nw_ref[l, n : n + 1, :]
        merged[l] = total
    half = 16
    for jt in range(cols // half):
        j = lax.broadcasted_iota(jnp.int32, (half, cols), 0) + jt * half
        hits = [j == nbr_ref[n : n + 1, :] for n in range(nbr)]
        hits.append(j == lax.broadcasted_iota(jnp.int32, (half, cols), 1))

        def fill(l, _):
            value = jnp.zeros((half, cols), F32)
            for n in range(nbr, -1, -1):
                value = jnp.where(hits[n], merged[l, n : n + 1, :], value)
            a_ref[l, jt * half : (jt + 1) * half, :] = value.astype(BF16)
            return _

        lax.fori_loop(0, levels, fill, 0, unroll=5)
    for l in range(levels):
        exs[pl.ds(l, cols, stride=rows), :] = jnp.dot(a_ref[l], c_ref[l], preferred_element_type=F32)
    for l in range(levels, rows):
        exs[pl.ds(l, cols, stride=rows), :] = jnp.zeros((cols, width), F32)
    level = lax.broadcasted_iota(jnp.int32, (levels, cols), 0)
    wet = wet_ref[...]
    vf[...] = jnp.zeros_like(vf)
    for m in range(levels):
        keep = jnp.maximum(level, m) < wet
        vf[m * rows : m * rows + levels, :] = jnp.where(keep, v_ref[m].astype(F32), 0.0)
    for l in range(rows):
        block = vf[pl.ds(l, rows, stride=rows), :]
        block = jnp.concatenate([block, jnp.zeros((128 - rows, cols), F32)], axis=0)
        vts[pl.ds(l, cols, stride=rows), :] = block.T
    vt_ref[...] = vts[...].reshape(cols, rows, 128).astype(BF16)
    vertical(vt_ref, exs, state_ref)


def first_kernel(blk, levels, r0, r1, r2, local_ref, vt_ref, wts_ref, tbl_ref, send_h, state_ref, s0, s1, s2, tbl_v, tbl_s, send_s, sems):
    copy = pltpu.make_async_copy(send_h, send_s, sems.at[1])
    copy.start()
    parity = lax.bitwise_and(lax.axis_index(blk), jnp.int32(1))
    add_edges((r0, r1, r2), vt_ref, state_ref, tbl_v, tbl_s, sems.at[0])
    copy.wait()
    pack_edges(parity, levels, send_s, wts_ref, tbl_ref, lambda s: state_ref[s], (s0, s1, s2))


def middle_kernel(c_ref, a_ref, vt_ref, out_ref, cs, exs):
    levels = a_ref.shape[0]
    cols, rows, width = c_ref.shape
    cs[...] = c_ref[...].reshape(cols * rows, width)
    for l in range(levels):
        state = cs[pl.ds(l, cols, stride=rows), :].astype(BF16)
        exs[pl.ds(l, cols, stride=rows), :] = jnp.dot(a_ref[l], state, preferred_element_type=F32)
    for l in range(levels, rows):
        exs[pl.ds(l, cols, stride=rows), :] = jnp.zeros((cols, width), F32)
    vertical(vt_ref, exs, out_ref)


def last_kernel(r0, r1, r2, local_ref, vt_ref, out_h, total, cs, out_v, tbl_v, tbl_s, sems):
    levels = out_h.shape[0]
    cols, rows, width = total.shape
    add_edges((r0, r1, r2), vt_ref, total, tbl_v, tbl_s, sems.at[0])
    cs[...] = total[...].reshape(cols * rows, width)
    count = 5
    edges = [levels * i // count for i in range(count + 1)]
    copies = []
    for i, (lo, hi) in enumerate(zip(edges, edges[1:])):
        for l in range(lo, hi):
            out_v[l] = cs[pl.ds(l, cols, stride=rows), :].astype(BF16)
        copies.append(pltpu.make_async_copy(out_v.at[pl.ds(lo, hi - lo)], out_h.at[pl.ds(lo, hi - lo)], sems.at[1 + i]))
        copies[-1].start()
    for copy in copies:
        copy.wait()


VM = pl.BlockSpec(memory_space=pltpu.VMEM)
HB = pl.BlockSpec(memory_space=pltpu.HBM)
DMA = pltpu.SemaphoreType.DMA


def call(kernel, ins, specs, outs, out_specs, scratch, limit, flops=0, aliases=None):
    size = sum(x.size * x.dtype.itemsize for x in (*ins, *outs))
    return pl.pallas_call(
        kernel,
        out_shape=outs,
        in_specs=specs,
        out_specs=out_specs,
        scratch_shapes=scratch,
        input_output_aliases=aliases or {},
        compiler_params=pltpu.CompilerParams(vmem_limit_bytes=limit * 2**20),
        cost_estimate=pl.CostEstimate(flops=flops, bytes_accessed=size, transcendentals=0),
    )(*ins)


def swapped(values, blk, basin):
    n, b = lax.axis_size(blk), lax.axis_size(basin)

    def pairs(first):
        partner = {i: i + 1 for i in range(first, n - 1, 2)}
        partner |= {j: i for i, j in partner.items()}
        return [(i, partner.get(i, i)) for i in range(n)]

    return (
        lax.ppermute(values[0], blk, pairs(1)),
        lax.ppermute(values[1], basin, [(i, (i + 1) % b) for i in range(b)]),
        lax.ppermute(values[2], blk, pairs(0)),
    )


def local(tracers, nbr_cols, nbr_wts, self_wts, send_cols, recv_cols, edge_wts, wet_levels, vert_inv):
    cols, levels, width = tracers.shape
    rows = padded(levels)
    nedge = send_cols.shape[1]
    shape = jax.ShapeDtypeStruct
    by_level = jnp.transpose(tracers, (1, 0, 2))
    nbr_by_level = jnp.transpose(nbr_wts, (1, 0, 2))
    edge_by_entry = jnp.transpose(edge_wts, (0, 2, 1))
    wet = wet_levels.reshape(1, cols)
    in_hbm = lambda x: pltpu.with_memory_space_constraint(x, pltpu.HBM)
    send_h = in_hbm(send_cols)
    loads = [by_level, nbr_cols, nbr_by_level, self_wts, wet, vert_inv]
    same = lambda x: shape(x.shape, x.dtype)
    packed = [shape((nedge, rows, width), BF16)] * 3
    flat = pltpu.VMEM((cols * rows, width), F32)
    columns = shape((cols, rows, width), F32)
    tables = [pltpu.VMEM((3, 8, 128), jnp.int32), pltpu.SMEM((3, 8, 128), jnp.int32)]

    first = call(
        functools.partial(gather_kernel, "blk"),
        (in_hbm(by_level), send_h, *map(in_hbm, (recv_cols, edge_by_entry, *loads[1:]))),
        [HB] * 9,
        packed + [same(x) for x in loads] + [shape((128, 128), F32), shape((8, 128), F32)],
        [VM] * 11,
        [
            pltpu.VMEM((rows * (cols + 8), width), F32), pltpu.VMEM((128, 128), F32),
            pltpu.VMEM(recv_cols.shape, jnp.int32), pltpu.VMEM(edge_by_entry.shape, F32),
            pltpu.SMEM(send_cols.shape, jnp.int32), DMA((13,)),
        ],
        16,
    )
    sends, loads, (wts, tbl) = first[:3], first[3:9], first[9:]
    received = swapped(sends, "blk", "basin")
    operator, partial, vt = call(
        operator_kernel, loads, [VM] * 6,
        [shape((levels, cols, cols), BF16), columns, shape((cols, rows, 128), BF16)], [VM] * 3,
        [flat, pltpu.VMEM((levels, 8, cols), F32), pltpu.VMEM((rows * rows, cols), F32), pltpu.VMEM((cols * rows, 128), F32)],
        32, flops=2 * levels * cols * cols * width,
    )
    state, *sends = call(
        functools.partial(first_kernel, "blk", levels),
        (*received, partial, vt, wts, tbl, send_h), [VM] * 7 + [HB],
        [columns] + packed, [VM] * 4,
        tables + [pltpu.SMEM(send_cols.shape, jnp.int32), DMA((2,))], 16,
        flops=2 * cols * rows * rows * width, aliases={3: 0},
    )
    received = swapped(sends, "blk", "basin")
    (partial,) = call(
        middle_kernel, (state, operator, vt), [VM] * 3, [columns], [VM], [flat, flat], 32,
        flops=2 * levels * cols * cols * width,
    )
    out, _ = call(
        last_kernel, (*received, partial, vt), [VM] * 5,
        [shape((levels, cols, width), BF16), columns], [HB, VM],
        [flat, pltpu.VMEM((levels, cols, width), BF16)] + tables + [DMA((6,))], 16,
        flops=2 * cols * rows * rows * width, aliases={3: 1},
    )
    return jnp.transpose(out, (1, 0, 2))


def solution(mesh):
    in_specs = (
        P(("basin", "blk"), None, None),
        P(None, ("basin", "blk")),
        P(None, None, ("basin", "blk")),
        P(None, ("basin", "blk")),
        P(None, ("basin", "blk")),
        P(None, ("basin", "blk")),
        P(None, None, ("basin", "blk")),
        P(("basin", "blk")),
        P(None, None, ("basin", "blk")),
    )
    out_specs = P(("basin", "blk"), None, None)
    return jax.shard_map(local, mesh=mesh, in_specs=in_specs, out_specs=out_specs, check_vma=False)
```

```python
import functools

import jax
import jax.numpy as jnp
from jax import lax
from jax.experimental import pallas as pl
from jax.experimental.pallas import tpu as pltpu
from jax.sharding import PartitionSpec as P

NSTEP = 2
F32 = jnp.float32
BF16 = jnp.bfloat16


def padded(levels):
    return -(-(levels + 1) // 8) * 8


def direction(slot, parity):
    return 2 if slot == 1 else lax.bitwise_xor(parity, jnp.int32(1 - slot // 2))


def pack_edges(parity, levels, send, weights, tbl, column, outs):
    rows = padded(levels)
    nedge, _, width = outs[0].shape
    is_level = lax.broadcasted_iota(jnp.int32, (rows, width), 0) < levels
    for slot, out in enumerate(outs):
        d = direction(slot, parity)
        table = jnp.broadcast_to(tbl[slot : slot + 1, :], (rows, width))
        for e in range(nedge):
            k = slot * nedge + e
            w = weights[0:rows, k : k + 1]
            out[e] = jnp.where(is_level, column(send[d, e]) * w, table).astype(BF16)


def product(operator, x):
    pad = jnp.zeros((64 - x.shape[0], x.shape[1]), F32)
    x = jnp.concatenate([x.astype(F32), pad], axis=0).astype(BF16)
    return jnp.dot(operator[:, 0:64], x, preferred_element_type=F32)


def vertical(vt_ref, exs, out):
    cols, rows, _ = vt_ref.shape

    def column(j, _):
        out[j] = product(vt_ref[j], exs[pl.ds(pl.multiple_of(j * rows, 8), rows), :])
        return _

    lax.fori_loop(0, cols, column, 0, unroll=16)


def add_edges(edges, vt_ref, total, tbl_v, tbl_s, sem):
    levels_at = edges[0].shape[1] - 8
    for slot, ref in enumerate(edges):
        tbl_v[slot] = ref[0, levels_at:, :].astype(F32).astype(jnp.int32)
    copy = pltpu.make_async_copy(tbl_v, tbl_s, sem)
    copy.start()
    copy.wait()
    group = 4
    for slot, ref in enumerate(edges):
        for first in range(0, ref.shape[0], group):
            at = [tbl_s[slot, 7, e] for e in range(first, first + group)]
            parts = [product(vt_ref[j], ref[first + i]) for i, j in enumerate(at)]
            for j, part in zip(at, parts):
                total[j] = total[j] + part


def gather_kernel(
    blk, c_h, send_h, recv_h, edge_h, nbr_h, nw_h, sw_h, wet_h, v_h,
    s0, s1, s2, c_v, nbr_v, nw_v, sw_v, wet_v, v_v, wts_o, tbl_o,
    cf, wts, recv_v, edge_v, send_s, sems,
):
    levels, cols, width = c_h.shape
    nedge = edge_h.shape[1]
    pitch = cols + 8
    count = 5
    edges = [levels * i // count for i in range(count + 1)]
    pairs = [(send_h, send_s), (recv_h, recv_v), (edge_h, edge_v)]
    pairs += [(c_h.at[pl.ds(lo, hi - lo)], c_v.at[pl.ds(lo, hi - lo)]) for lo, hi in zip(edges, edges[1:])]
    pairs += [(nbr_h, nbr_v), (nw_h, nw_v), (sw_h, sw_v), (wet_h, wet_v), (v_h, v_v)]
    copies = [pltpu.make_async_copy(a, b, sems.at[i]) for i, (a, b) in enumerate(pairs)]
    for copy in copies:
        copy.start()
    parity = lax.bitwise_and(lax.axis_index(blk), jnp.int32(1))
    wts[...] = jnp.zeros_like(wts)
    tbl_o[...] = jnp.zeros_like(tbl_o)
    for copy in copies[:3]:
        copy.wait()
    for slot in range(3):
        d = direction(slot, parity)
        wts[slot * nedge : (slot + 1) * nedge, 0:levels] = edge_v[d]
        tbl_o[slot : slot + 1, 0:nedge] = recv_v[pl.ds(d, 1), :].astype(F32)
    weights = wts[...].T
    wts_o[...] = weights
    for i, (lo, hi) in enumerate(zip(edges, edges[1:])):
        copies[3 + i].wait()
        for l in range(lo, hi):
            cf[l * pitch : l * pitch + cols, :] = c_v[l].astype(F32)
    column = lambda s: cf[pl.ds(s, padded(levels), stride=pitch), :]
    pack_edges(parity, levels, send_s, weights, tbl_o, column, (s0, s1, s2))
    for copy in copies[3 + count :]:
        copy.wait()


def operator_kernel(c_ref, nbr_ref, nw_ref, sw_ref, wet_ref, v_ref, a_ref, state_ref, vt_ref, exs, merged, vf, vts):
    levels, cols, width = c_ref.shape
    rows = padded(levels)
    nbr = nbr_ref.shape[0]
    lane = lax.broadcasted_iota(jnp.int32, (8, cols), 1)
    sub = lax.broadcasted_iota(jnp.int32, (8, cols), 0)
    target = jnp.where(sub == nbr, lane, -1)
    for n in range(nbr):
        target = jnp.where(sub == n, nbr_ref[n : n + 1, :], target)
    same = [(target == nbr_ref[n : n + 1, :]).astype(F32) for n in range(nbr)]
    same.append((target == lane).astype(F32))
    for l in range(levels):
        total = same[nbr] * sw_ref[l : l + 1, :]
        for n in range(nbr):
            total = total + same[n] * nw_ref[l, n : n + 1, :]
        merged[l] = total
    half = 16
    for jt in range(cols // half):
        j = lax.broadcasted_iota(jnp.int32, (half, cols), 0) + jt * half
        hits = [j == nbr_ref[n : n + 1, :] for n in range(nbr)]
        hits.append(j == lax.broadcasted_iota(jnp.int32, (half, cols), 1))

        def fill(l, _):
            value = jnp.zeros((half, cols), F32)
            for n in range(nbr, -1, -1):
                value = jnp.where(hits[n], merged[l, n : n + 1, :], value)
            a_ref[l, jt * half : (jt + 1) * half, :] = value.astype(BF16)
            return _

        lax.fori_loop(0, levels, fill, 0, unroll=5)
    for l in range(levels):
        exs[pl.ds(l, cols, stride=rows), :] = jnp.dot(a_ref[l], c_ref[l], preferred_element_type=F32)
    for l in range(levels, rows):
        exs[pl.ds(l, cols, stride=rows), :] = jnp.zeros((cols, width), F32)
    level = lax.broadcasted_iota(jnp.int32, (levels, cols), 0)
    wet = wet_ref[...]
    vf[...] = jnp.zeros_like(vf)
    for m in range(levels):
        keep = jnp.maximum(level, m) < wet
        vf[m * rows : m * rows + levels, :] = jnp.where(keep, v_ref[m].astype(F32), 0.0)
    for l in range(rows):
        block = vf[pl.ds(l, rows, stride=rows), :]
        block = jnp.concatenate([block, jnp.zeros((128 - rows, cols), F32)], axis=0)
        vts[pl.ds(l, cols, stride=rows), :] = block.T
    vt_ref[...] = vts[...].reshape(cols, rows, 128).astype(BF16)
    vertical(vt_ref, exs, state_ref)


def first_kernel(blk, levels, r0, r1, r2, local_ref, vt_ref, wts_ref, tbl_ref, send_h, state_ref, s0, s1, s2, tbl_v, tbl_s, send_s, sems):
    copy = pltpu.make_async_copy(send_h, send_s, sems.at[1])
    copy.start()
    parity = lax.bitwise_and(lax.axis_index(blk), jnp.int32(1))
    add_edges((r0, r1, r2), vt_ref, state_ref, tbl_v, tbl_s, sems.at[0])
    copy.wait()
    pack_edges(parity, levels, send_s, wts_ref, tbl_ref, lambda s: state_ref[s], (s0, s1, s2))


def middle_kernel(c_ref, a_ref, vt_ref, out_ref, cs, exs):
    levels = a_ref.shape[0]
    cols, rows, width = c_ref.shape
    cs[...] = c_ref[...].reshape(cols * rows, width)
    for l in range(levels):
        state = cs[pl.ds(l, cols, stride=rows), :].astype(BF16)
        exs[pl.ds(l, cols, stride=rows), :] = jnp.dot(a_ref[l], state, preferred_element_type=F32)
    for l in range(levels, rows):
        exs[pl.ds(l, cols, stride=rows), :] = jnp.zeros((cols, width), F32)
    vertical(vt_ref, exs, out_ref)


def last_kernel(r0, r1, r2, local_ref, vt_ref, out_h, total, cs, out_v, tbl_v, tbl_s, sems):
    levels = out_h.shape[0]
    cols, rows, width = total.shape
    add_edges((r0, r1, r2), vt_ref, total, tbl_v, tbl_s, sems.at[0])
    cs[...] = total[...].reshape(cols * rows, width)
    count = 5
    edges = [levels * i // count for i in range(count + 1)]
    copies = []
    for i, (lo, hi) in enumerate(zip(edges, edges[1:])):
        for l in range(lo, hi):
            out_v[l] = cs[pl.ds(l, cols, stride=rows), :].astype(BF16)
        copies.append(pltpu.make_async_copy(out_v.at[pl.ds(lo, hi - lo)], out_h.at[pl.ds(lo, hi - lo)], sems.at[1 + i]))
        copies[-1].start()
    for copy in copies:
        copy.wait()


VM = pl.BlockSpec(memory_space=pltpu.VMEM)
HB = pl.BlockSpec(memory_space=pltpu.HBM)
DMA = pltpu.SemaphoreType.DMA


def call(kernel, ins, specs, outs, out_specs, scratch, limit, flops=0, aliases=None):
    size = sum(x.size * x.dtype.itemsize for x in (*ins, *outs))
    return pl.pallas_call(
        kernel,
        out_shape=outs,
        in_specs=specs,
        out_specs=out_specs,
        scratch_shapes=scratch,
        input_output_aliases=aliases or {},
        compiler_params=pltpu.CompilerParams(vmem_limit_bytes=limit * 2**20),
        cost_estimate=pl.CostEstimate(flops=flops, bytes_accessed=size, transcendentals=0),
    )(*ins)


def swapped(values, blk, basin):
    n, b = lax.axis_size(blk), lax.axis_size(basin)
    pairs = lambda first: [pair for i in range(first, n - 1, 2) for pair in ((i, i + 1), (i + 1, i))]
    if n % 2:
        odd = lax.ppermute(values[0], blk, pairs(1))
    else:
        held = lax.ppermute(values[0], blk, pairs(0))
    along = lax.ppermute(values[1], basin, [(i, (i + 1) % b) for i in range(b)])
    if not n % 2:
        odd = lax.ppermute(held, blk, [pair for i in range(0, n - 2, 2) for pair in ((i, i + 2), (i + 3, i + 1))])
    return odd, along, lax.ppermute(values[2], blk, pairs(0))


def local(tracers, nbr_cols, nbr_wts, self_wts, send_cols, recv_cols, edge_wts, wet_levels, vert_inv):
    cols, levels, width = tracers.shape
    rows = padded(levels)
    nedge = send_cols.shape[1]
    shape = jax.ShapeDtypeStruct
    by_level = jnp.transpose(tracers, (1, 0, 2))
    nbr_by_level = jnp.transpose(nbr_wts, (1, 0, 2))
    edge_by_entry = jnp.transpose(edge_wts, (0, 2, 1))
    wet = wet_levels.reshape(1, cols)
    in_hbm = lambda x: pltpu.with_memory_space_constraint(x, pltpu.HBM)
    send_h = in_hbm(send_cols)
    loads = [by_level, nbr_cols, nbr_by_level, self_wts, wet, vert_inv]
    same = lambda x: shape(x.shape, x.dtype)
    packed = [shape((nedge, rows, width), BF16)] * 3
    flat = pltpu.VMEM((cols * rows, width), F32)
    columns = shape((cols, rows, width), F32)
    tables = [pltpu.VMEM((3, 8, 128), jnp.int32), pltpu.SMEM((3, 8, 128), jnp.int32)]

    first = call(
        functools.partial(gather_kernel, "blk"),
        (in_hbm(by_level), send_h, *map(in_hbm, (recv_cols, edge_by_entry, *loads[1:]))),
        [HB] * 9,
        packed + [same(x) for x in loads] + [shape((128, 128), F32), shape((8, 128), F32)],
        [VM] * 11,
        [
            pltpu.VMEM((rows * (cols + 8), width), F32), pltpu.VMEM((128, 128), F32),
            pltpu.VMEM(recv_cols.shape, jnp.int32), pltpu.VMEM(edge_by_entry.shape, F32),
            pltpu.SMEM(send_cols.shape, jnp.int32), DMA((13,)),
        ],
        16,
    )
    sends, loads, (wts, tbl) = first[:3], first[3:9], first[9:]
    received = swapped(sends, "blk", "basin")
    operator, partial, vt = call(
        operator_kernel, loads, [VM] * 6,
        [shape((levels, cols, cols), BF16), columns, shape((cols, rows, 128), BF16)], [VM] * 3,
        [flat, pltpu.VMEM((levels, 8, cols), F32), pltpu.VMEM((rows * rows, cols), F32), pltpu.VMEM((cols * rows, 128), F32)],
        32, flops=2 * levels * cols * cols * width,
    )
    state, *sends = call(
        functools.partial(first_kernel, "blk", levels),
        (*received, partial, vt, wts, tbl, send_h), [VM] * 7 + [HB],
        [columns] + packed, [VM] * 4,
        tables + [pltpu.SMEM(send_cols.shape, jnp.int32), DMA((2,))], 16,
        flops=2 * cols * rows * rows * width, aliases={3: 0},
    )
    received = swapped(sends, "blk", "basin")
    (partial,) = call(
        middle_kernel, (state, operator, vt), [VM] * 3, [columns], [VM], [flat, flat], 32,
        flops=2 * levels * cols * cols * width,
    )
    out, _ = call(
        last_kernel, (*received, partial, vt), [VM] * 5,
        [shape((levels, cols, width), BF16), columns], [HB, VM],
        [flat, pltpu.VMEM((levels, cols, width), BF16)] + tables + [DMA((6,))], 16,
        flops=2 * cols * rows * rows * width, aliases={3: 1},
    )
    return jnp.transpose(out, (1, 0, 2))


def solution(mesh):
    in_specs = (
        P(("basin", "blk"), None, None),
        P(None, ("basin", "blk")),
        P(None, None, ("basin", "blk")),
        P(None, ("basin", "blk")),
        P(None, ("basin", "blk")),
        P(None, ("basin", "blk")),
        P(None, None, ("basin", "blk")),
        P(("basin", "blk")),
        P(None, None, ("basin", "blk")),
    )
    out_specs = P(("basin", "blk"), None, None)
    return jax.shard_map(local, mesh=mesh, in_specs=in_specs, out_specs=out_specs, check_vma=False)
```

```python
import functools

import jax
import jax.numpy as jnp
from jax import lax
from jax.experimental import pallas as pl
from jax.experimental.pallas import tpu as pltpu
from jax.sharding import PartitionSpec as P

NSTEP = 2
F32 = jnp.float32
BF16 = jnp.bfloat16


def padded(levels):
    return -(-(levels + 1) // 8) * 8


def direction(slot, parity):
    return 2 if slot == 1 else lax.bitwise_xor(parity, jnp.int32(1 - slot // 2))


def has_partner(slot, at, count):
    first = lax.bitwise_and(at + slot // 2, jnp.int32(1)) == 1
    return jnp.where(first, at + 1 < count, at > 0)


def pack_edges(parity, levels, send, weights, tbl, column, outs):
    rows = padded(levels)
    nedge, _, width = outs[0].shape
    is_level = lax.broadcasted_iota(jnp.int32, (rows, width), 0) < levels
    for slot, out in enumerate(outs):
        d = direction(slot, parity)
        table = jnp.broadcast_to(tbl[slot : slot + 1, :], (rows, width))
        for e in range(nedge):
            k = slot * nedge + e
            w = weights[0:rows, k : k + 1]
            out[e] = jnp.where(is_level, column(send[d, e]) * w, table).astype(BF16)


def product(operator, x):
    pad = jnp.zeros((64 - x.shape[0], x.shape[1]), F32)
    x = jnp.concatenate([x.astype(F32), pad], axis=0).astype(BF16)
    return jnp.dot(operator[:, 0:64], x, preferred_element_type=F32)


def vertical(vt_ref, exs, out):
    cols, rows, _ = vt_ref.shape

    def column(j, _):
        out[j] = product(vt_ref[j], exs[pl.ds(pl.multiple_of(j * rows, 8), rows), :])
        return _

    lax.fori_loop(0, cols, column, 0, unroll=16)


def add_edges(edges, vt_ref, total, tbl_v, tbl_s, sem):
    levels_at = edges[0].shape[1] - 8
    for slot, ref in enumerate(edges):
        tbl_v[slot] = ref[0, levels_at:, :].astype(F32).astype(jnp.int32)
    copy = pltpu.make_async_copy(tbl_v, tbl_s, sem)
    copy.start()
    copy.wait()
    group = 4
    for slot, ref in enumerate(edges):
        for first in range(0, ref.shape[0], group):
            at = [tbl_s[slot, 7, e] for e in range(first, first + group)]
            parts = [product(vt_ref[j], ref[first + i]) for i, j in enumerate(at)]
            for j, part in zip(at, parts):
                total[j] = total[j] + part


def gather_kernel(
    blk, c_h, send_h, recv_h, edge_h, nbr_h, nw_h, sw_h, wet_h, v_h,
    s0, s1, s2, c_v, nbr_v, nw_v, sw_v, wet_v, v_v, wts_o, tbl_o,
    cf, wts, recv_v, edge_v, send_s, sems,
):
    levels, cols, width = c_h.shape
    nedge = edge_h.shape[1]
    pitch = cols + 8
    count = 5
    edges = [levels * i // count for i in range(count + 1)]
    pairs = [(send_h, send_s), (recv_h, recv_v), (edge_h, edge_v)]
    pairs += [(c_h.at[pl.ds(lo, hi - lo)], c_v.at[pl.ds(lo, hi - lo)]) for lo, hi in zip(edges, edges[1:])]
    pairs += [(nbr_h, nbr_v), (nw_h, nw_v), (sw_h, sw_v), (wet_h, wet_v), (v_h, v_v)]
    copies = [pltpu.make_async_copy(a, b, sems.at[i]) for i, (a, b) in enumerate(pairs)]
    for copy in copies:
        copy.start()
    parity = lax.bitwise_and(lax.axis_index(blk), jnp.int32(1))
    wts[...] = jnp.zeros_like(wts)
    tbl_o[...] = jnp.zeros_like(tbl_o)
    for copy in copies[:3]:
        copy.wait()
    for slot in range(3):
        d = direction(slot, parity)
        weight = edge_v[d]
        if slot != 1:
            weight = jnp.where(has_partner(slot, lax.axis_index(blk), lax.axis_size(blk)), weight, 0.0)
        wts[slot * nedge : (slot + 1) * nedge, 0:levels] = weight
        tbl_o[slot : slot + 1, 0:nedge] = recv_v[pl.ds(d, 1), :].astype(F32)
    weights = wts[...].T
    wts_o[...] = weights
    for i, (lo, hi) in enumerate(zip(edges, edges[1:])):
        copies[3 + i].wait()
        for l in range(lo, hi):
            cf[l * pitch : l * pitch + cols, :] = c_v[l].astype(F32)
    column = lambda s: cf[pl.ds(s, padded(levels), stride=pitch), :]
    pack_edges(parity, levels, send_s, weights, tbl_o, column, (s0, s1, s2))
    for copy in copies[3 + count :]:
        copy.wait()


def operator_kernel(c_ref, nbr_ref, nw_ref, sw_ref, wet_ref, v_ref, a_ref, state_ref, vt_ref, exs, merged, vf, vts):
    levels, cols, width = c_ref.shape
    rows = padded(levels)
    nbr = nbr_ref.shape[0]
    lane = lax.broadcasted_iota(jnp.int32, (8, cols), 1)
    sub = lax.broadcasted_iota(jnp.int32, (8, cols), 0)
    target = jnp.where(sub == nbr, lane, -1)
    for n in range(nbr):
        target = jnp.where(sub == n, nbr_ref[n : n + 1, :], target)
    same = [(target == nbr_ref[n : n + 1, :]).astype(F32) for n in range(nbr)]
    same.append((target == lane).astype(F32))
    for l in range(levels):
        total = same[nbr] * sw_ref[l : l + 1, :]
        for n in range(nbr):
            total = total + same[n] * nw_ref[l, n : n + 1, :]
        merged[l] = total
    half = 16
    for jt in range(cols // half):
        j = lax.broadcasted_iota(jnp.int32, (half, cols), 0) + jt * half
        hits = [j == nbr_ref[n : n + 1, :] for n in range(nbr)]
        hits.append(j == lax.broadcasted_iota(jnp.int32, (half, cols), 1))

        def fill(l, _):
            value = jnp.zeros((half, cols), F32)
            for n in range(nbr, -1, -1):
                value = jnp.where(hits[n], merged[l, n : n + 1, :], value)
            a_ref[l, jt * half : (jt + 1) * half, :] = value.astype(BF16)
            return _

        lax.fori_loop(0, levels, fill, 0, unroll=5)
    for l in range(levels):
        exs[pl.ds(l, cols, stride=rows), :] = jnp.dot(a_ref[l], c_ref[l], preferred_element_type=F32)
    for l in range(levels, rows):
        exs[pl.ds(l, cols, stride=rows), :] = jnp.zeros((cols, width), F32)
    level = lax.broadcasted_iota(jnp.int32, (levels, cols), 0)
    wet = wet_ref[...]
    vf[...] = jnp.zeros_like(vf)
    for m in range(levels):
        keep = jnp.maximum(level, m) < wet
        vf[m * rows : m * rows + levels, :] = jnp.where(keep, v_ref[m].astype(F32), 0.0)
    for l in range(rows):
        block = vf[pl.ds(l, rows, stride=rows), :]
        block = jnp.concatenate([block, jnp.zeros((128 - rows, cols), F32)], axis=0)
        vts[pl.ds(l, cols, stride=rows), :] = block.T
    vt_ref[...] = vts[...].reshape(cols, rows, 128).astype(BF16)
    vertical(vt_ref, exs, state_ref)


def first_kernel(blk, levels, r0, r1, r2, local_ref, vt_ref, wts_ref, tbl_ref, send_h, state_ref, s0, s1, s2, tbl_v, tbl_s, send_s, sems):
    copy = pltpu.make_async_copy(send_h, send_s, sems.at[1])
    copy.start()
    parity = lax.bitwise_and(lax.axis_index(blk), jnp.int32(1))
    add_edges((r0, r1, r2), vt_ref, state_ref, tbl_v, tbl_s, sems.at[0])
    copy.wait()
    pack_edges(parity, levels, send_s, wts_ref, tbl_ref, lambda s: state_ref[s], (s0, s1, s2))


def middle_kernel(c_ref, a_ref, vt_ref, out_ref, cs, exs):
    levels = a_ref.shape[0]
    cols, rows, width = c_ref.shape
    cs[...] = c_ref[...].reshape(cols * rows, width)
    for l in range(levels):
        state = cs[pl.ds(l, cols, stride=rows), :].astype(BF16)
        exs[pl.ds(l, cols, stride=rows), :] = jnp.dot(a_ref[l], state, preferred_element_type=F32)
    for l in range(levels, rows):
        exs[pl.ds(l, cols, stride=rows), :] = jnp.zeros((cols, width), F32)
    vertical(vt_ref, exs, out_ref)


def last_kernel(r0, r1, r2, local_ref, vt_ref, out_h, total, cs, out_v, tbl_v, tbl_s, sems):
    levels = out_h.shape[0]
    cols, rows, width = total.shape
    add_edges((r0, r1, r2), vt_ref, total, tbl_v, tbl_s, sems.at[0])
    cs[...] = total[...].reshape(cols * rows, width)
    count = 5
    edges = [levels * i // count for i in range(count + 1)]
    copies = []
    for i, (lo, hi) in enumerate(zip(edges, edges[1:])):
        for l in range(lo, hi):
            out_v[l] = cs[pl.ds(l, cols, stride=rows), :].astype(BF16)
        copies.append(pltpu.make_async_copy(out_v.at[pl.ds(lo, hi - lo)], out_h.at[pl.ds(lo, hi - lo)], sems.at[1 + i]))
        copies[-1].start()
    for copy in copies:
        copy.wait()


VM = pl.BlockSpec(memory_space=pltpu.VMEM)
HB = pl.BlockSpec(memory_space=pltpu.HBM)
DMA = pltpu.SemaphoreType.DMA


def call(kernel, ins, specs, outs, out_specs, scratch, limit, flops=0, aliases=None):
    size = sum(x.size * x.dtype.itemsize for x in (*ins, *outs))
    return pl.pallas_call(
        kernel,
        out_shape=outs,
        in_specs=specs,
        out_specs=out_specs,
        scratch_shapes=scratch,
        input_output_aliases=aliases or {},
        compiler_params=pltpu.CompilerParams(vmem_limit_bytes=limit * 2**20),
        cost_estimate=pl.CostEstimate(flops=flops, bytes_accessed=size, transcendentals=0),
    )(*ins)


def swapped(values, blk, basin):
    n, b = lax.axis_size(blk), lax.axis_size(basin)

    def pairs(first):
        order = [(i + first) % n for i in range(n)]
        partner = {order[i]: order[i + 1] for i in range(0, n - 1, 2)}
        partner |= {j: i for i, j in partner.items()}
        return [(i, partner.get(i, i)) for i in range(n)]

    return (
        lax.ppermute(values[0], blk, pairs(1)),
        lax.ppermute(values[1], basin, [(i, (i + 1) % b) for i in range(b)]),
        lax.ppermute(values[2], blk, pairs(0)),
    )


def local(tracers, nbr_cols, nbr_wts, self_wts, send_cols, recv_cols, edge_wts, wet_levels, vert_inv):
    cols, levels, width = tracers.shape
    rows = padded(levels)
    nedge = send_cols.shape[1]
    shape = jax.ShapeDtypeStruct
    by_level = jnp.transpose(tracers, (1, 0, 2))
    nbr_by_level = jnp.transpose(nbr_wts, (1, 0, 2))
    edge_by_entry = jnp.transpose(edge_wts, (0, 2, 1))
    wet = wet_levels.reshape(1, cols)
    in_hbm = lambda x: pltpu.with_memory_space_constraint(x, pltpu.HBM)
    send_h = in_hbm(send_cols)
    loads = [by_level, nbr_cols, nbr_by_level, self_wts, wet, vert_inv]
    same = lambda x: shape(x.shape, x.dtype)
    packed = [shape((nedge, rows, width), BF16)] * 3
    flat = pltpu.VMEM((cols * rows, width), F32)
    columns = shape((cols, rows, width), F32)
    tables = [pltpu.VMEM((3, 8, 128), jnp.int32), pltpu.SMEM((3, 8, 128), jnp.int32)]

    first = call(
        functools.partial(gather_kernel, "blk"),
        (in_hbm(by_level), send_h, *map(in_hbm, (recv_cols, edge_by_entry, *loads[1:]))),
        [HB] * 9,
        packed + [same(x) for x in loads] + [shape((128, 128), F32), shape((8, 128), F32)],
        [VM] * 11,
        [
            pltpu.VMEM((rows * (cols + 8), width), F32), pltpu.VMEM((128, 128), F32),
            pltpu.VMEM(recv_cols.shape, jnp.int32), pltpu.VMEM(edge_by_entry.shape, F32),
            pltpu.SMEM(send_cols.shape, jnp.int32), DMA((13,)),
        ],
        16,
    )
    sends, loads, (wts, tbl) = first[:3], first[3:9], first[9:]
    received = swapped(sends, "blk", "basin")
    operator, partial, vt = call(
        operator_kernel, loads, [VM] * 6,
        [shape((levels, cols, cols), BF16), columns, shape((cols, rows, 128), BF16)], [VM] * 3,
        [flat, pltpu.VMEM((levels, 8, cols), F32), pltpu.VMEM((rows * rows, cols), F32), pltpu.VMEM((cols * rows, 128), F32)],
        32, flops=2 * levels * cols * cols * width,
    )
    state, *sends = call(
        functools.partial(first_kernel, "blk", levels),
        (*received, partial, vt, wts, tbl, send_h), [VM] * 7 + [HB],
        [columns] + packed, [VM] * 4,
        tables + [pltpu.SMEM(send_cols.shape, jnp.int32), DMA((2,))], 16,
        flops=2 * cols * rows * rows * width, aliases={3: 0},
    )
    received = swapped(sends, "blk", "basin")
    (partial,) = call(
        middle_kernel, (state, operator, vt), [VM] * 3, [columns], [VM], [flat, flat], 32,
        flops=2 * levels * cols * cols * width,
    )
    out, _ = call(
        last_kernel, (*received, partial, vt), [VM] * 5,
        [shape((levels, cols, width), BF16), columns], [HB, VM],
        [flat, pltpu.VMEM((levels, cols, width), BF16)] + tables + [DMA((6,))], 16,
        flops=2 * cols * rows * rows * width, aliases={3: 1},
    )
    return jnp.transpose(out, (1, 0, 2))


def solution(mesh):
    in_specs = (
        P(("basin", "blk"), None, None),
        P(None, ("basin", "blk")),
        P(None, None, ("basin", "blk")),
        P(None, ("basin", "blk")),
        P(None, ("basin", "blk")),
        P(None, ("basin", "blk")),
        P(None, None, ("basin", "blk")),
        P(("basin", "blk")),
        P(None, None, ("basin", "blk")),
    )
    out_specs = P(("basin", "blk"), None, None)
    return jax.shard_map(local, mesh=mesh, in_specs=in_specs, out_specs=out_specs, check_vma=False)
```

```python
import functools

import jax
import jax.numpy as jnp
from jax import lax
from jax.experimental import pallas as pl
from jax.experimental.pallas import tpu as pltpu
from jax.sharding import PartitionSpec as P

NSTEP = 2
F32 = jnp.float32
BF16 = jnp.bfloat16


def padded(levels):
    return -(-levels // 8) * 8


def whole_rows(levels):
    return levels // 16 * 16


def message_rows(levels, nedge):
    return levels * nedge + 16


def direction(slot, parity):
    return 2 if slot == 1 else lax.bitwise_xor(parity, jnp.int32(1 - slot // 2))


def has_partner(slot, at, count):
    first = lax.bitwise_and(at + slot // 2, jnp.int32(1)) == 1
    return jnp.where(first, at + 1 < count, at > 0)


def pack_chunk(parity, lo, levels, send, weights, tbl, rows_of, outs):
    whole = whole_rows(levels)
    nedge = send.shape[1]
    rest = levels - whole
    share = 8 // rest if rest else 0
    for slot, out in enumerate(outs):
        d = direction(slot, parity)
        if lo < whole:
            for e in range(nedge):
                k = slot * nedge + e
                value = rows_of(send[d, e], lo, 16) * weights[lo : lo + 16, k : k + 1]
                out[e * whole + lo : e * whole + lo + 16, :] = value.astype(BF16)
            continue
        sub = lax.broadcasted_iota(jnp.int32, (8, out.shape[1]), 0)
        parts = []
        for first in range(0, nedge, share or nedge):
            part = None
            for q in range(share):
                k = slot * nedge + first + q
                value = rows_of(send[d, first + q], lo, 8) * weights[lo : lo + 8, k : k + 1]
                if q:
                    value = pltpu.roll(value, q * rest, 0)
                part = value if part is None else jnp.where(sub >= q * rest, value, part)
            if share:
                parts.append(part)
        table = jnp.broadcast_to(tbl[slot : slot + 1, :], (16, out.shape[1]))
        out[nedge * whole :, :] = jnp.concatenate(parts + [table], axis=0).astype(BF16)


def vertical(vt_ref, exs, out):
    cols, rows, _ = vt_ref.shape
    pad = jnp.zeros((64 - rows, out.shape[1]), F32)

    def column(j, _):
        at = pl.ds(pl.multiple_of(j * rows, 8), rows)
        x = jnp.concatenate([exs[at, :], pad], axis=0).astype(BF16)
        out[at, :] = jnp.dot(vt_ref[j][:, 0:64], x, preferred_element_type=F32)
        return _

    lax.fori_loop(0, cols, column, 0, unroll=16)


def add_edges(edges, levels, nedge, vt_ref, total, tbl_v, tbl_s, sem):
    whole = whole_rows(levels)
    rest = levels - whole
    share = 8 // rest if rest else 0
    rows = vt_ref.shape[1]
    for i, ref in enumerate(edges):
        tbl_v[i] = ref[levels * nedge :, :].astype(F32)[0:8].astype(jnp.int32)
    copy = pltpu.make_async_copy(tbl_v, tbl_s, sem)
    copy.start()
    copy.wait()
    group = max(share, 4)
    pad = jnp.zeros((8, total.shape[1]), F32)
    for i, ref in enumerate(edges):
        tails = ref[whole * nedge : levels * nedge, :].astype(F32) if rest else None
        for first in range(0, nedge, group):
            targets = [tbl_s[i, 0, e] for e in range(first, first + group)]
            products = []
            for e, j in zip(range(first, first + group), targets):
                x = ref[e * whole : (e + 1) * whole, :]
                if rest:
                    tail = tails[e // share * 8 : e // share * 8 + 8]
                    if e % share:
                        tail = pltpu.roll(tail, 8 - e % share * rest, 0)
                    x = jnp.concatenate([x, jnp.concatenate([tail, pad], axis=0).astype(BF16)], axis=0)
                products.append(jnp.dot(vt_ref[j][:, 0 : x.shape[0]], x, preferred_element_type=F32))
            for j, part in zip(targets, products):
                at = pl.ds(pl.multiple_of(j * rows, 8), rows)
                total[at, :] = total[at, :] + part


def gather_kernel(
    blk, c_h, send_h, recv_h, edge_h, nbr_h, nw_h, sw_h, wet_h, v_h,
    s0, s1, s2, c_v, nbr_v, nw_v, sw_v, wet_v, v_v, wts_o, tbl_o,
    cf, wts, recv_v, edge_v, send_s, sems,
):
    levels, cols, width = c_h.shape
    nedge = edge_h.shape[1]
    pitch = cols + 8
    bounds = [(lo, min(lo + 16, levels)) for lo in range(0, levels, 16)]
    pairs = [(send_h, send_s), (recv_h, recv_v), (edge_h, edge_v)]
    pairs += [(c_h.at[pl.ds(lo, hi - lo)], c_v.at[pl.ds(lo, hi - lo)]) for lo, hi in bounds]
    pairs += [(nbr_h, nbr_v), (nw_h, nw_v), (sw_h, sw_v), (wet_h, wet_v), (v_h, v_v)]
    copies = [pltpu.make_async_copy(a, b, sems.at[i]) for i, (a, b) in enumerate(pairs)]
    for copy in copies:
        copy.start()
    parity = lax.bitwise_and(lax.axis_index(blk), jnp.int32(1))
    wts[...] = jnp.zeros_like(wts)
    tbl_o[...] = jnp.zeros_like(tbl_o)
    for copy in copies[:3]:
        copy.wait()
    for slot in range(3):
        d = direction(slot, parity)
        weight = edge_v[d]
        if slot != 1:
            weight = jnp.where(has_partner(slot, lax.axis_index(blk), lax.axis_size(blk)), weight, 0.0)
        wts[slot * nedge : (slot + 1) * nedge, 0:levels] = weight
        tbl_o[slot : slot + 1, 0:nedge] = recv_v[pl.ds(d, 1), :].astype(F32)
    weights = wts[...].T
    wts_o[...] = weights
    rows_of = lambda s, lo, n: cf[pl.ds(lo * pitch + s, n, stride=pitch), :]
    for i, (lo, hi) in enumerate(bounds):
        copies[3 + i].wait()
        for l in range(lo, hi):
            cf[l * pitch : l * pitch + cols, :] = c_v[l].astype(F32)
        pack_chunk(parity, lo, levels, send_s, weights, tbl_o, rows_of, (s0, s1, s2))
    if levels % 16 == 0:
        pack_chunk(parity, levels, levels, send_s, weights, tbl_o, rows_of, (s0, s1, s2))
    for copy in copies[3 + len(bounds) :]:
        copy.wait()


def operator_kernel(c_ref, nbr_ref, nw_ref, sw_ref, wet_ref, v_ref, a_ref, state_ref, vt_ref, exs, merged, vf, vts):
    levels, cols, width = c_ref.shape
    rows = padded(levels)
    nbr = nbr_ref.shape[0]
    lane = lax.broadcasted_iota(jnp.int32, (8, cols), 1)
    sub = lax.broadcasted_iota(jnp.int32, (8, cols), 0)
    target = jnp.where(sub == nbr, lane, -1)
    for n in range(nbr):
        target = jnp.where(sub == n, nbr_ref[n : n + 1, :], target)
    same = [(target == nbr_ref[n : n + 1, :]).astype(F32) for n in range(nbr)]
    same.append((target == lane).astype(F32))
    for l in range(levels):
        total = same[nbr] * sw_ref[l : l + 1, :]
        for n in range(nbr):
            total = total + same[n] * nw_ref[l, n : n + 1, :]
        merged[l] = total
    half = 16
    for jt in range(cols // half):
        j = lax.broadcasted_iota(jnp.int32, (half, cols), 0) + jt * half
        hits = [j == nbr_ref[n : n + 1, :] for n in range(nbr)]
        hits.append(j == lax.broadcasted_iota(jnp.int32, (half, cols), 1))

        def fill(l, _):
            value = jnp.zeros((half, cols), F32)
            for n in range(nbr, -1, -1):
                value = jnp.where(hits[n], merged[l, n : n + 1, :], value)
            a_ref[l, jt * half : (jt + 1) * half, :] = value.astype(BF16)
            return _

        lax.fori_loop(0, levels, fill, 0, unroll=5)
    for l in range(levels):
        exs[pl.ds(l, cols, stride=rows), :] = jnp.dot(a_ref[l], c_ref[l], preferred_element_type=F32)
    for l in range(levels, rows):
        exs[pl.ds(l, cols, stride=rows), :] = jnp.zeros((cols, width), F32)
    level = lax.broadcasted_iota(jnp.int32, (levels, cols), 0)
    wet = wet_ref[...]
    vf[...] = jnp.zeros_like(vf)
    for m in range(levels):
        keep = jnp.maximum(level, m) < wet
        vf[m * rows : m * rows + levels, :] = jnp.where(keep, v_ref[m].astype(F32), 0.0)
    for l in range(rows):
        block = vf[pl.ds(l, rows, stride=rows), :]
        block = jnp.concatenate([block, jnp.zeros((128 - rows, cols), F32)], axis=0)
        vts[pl.ds(l, cols, stride=rows), :] = block.T
    vt_ref[...] = vts[...].reshape(cols, rows, 128).astype(BF16)
    vertical(vt_ref, exs, state_ref)


def arrived_kernel(levels, nedge, *refs):
    *edges, _, vt_ref, total, tbl_v, tbl_s, sem = refs
    add_edges(edges, levels, nedge, vt_ref, total, tbl_v, tbl_s, sem)


def send_kernel(blk, levels, r1, local_ref, vt_ref, wts_ref, tbl_ref, send_h, state, s0, s1, s2, tbl_v, tbl_s, send_s, sems):
    copy = pltpu.make_async_copy(send_h, send_s, sems.at[1])
    copy.start()
    parity = lax.bitwise_and(lax.axis_index(blk), jnp.int32(1))
    rows = vt_ref.shape[1]
    add_edges((r1,), levels, send_h.shape[1], vt_ref, state, tbl_v, tbl_s, sems.at[0])
    copy.wait()
    rows_of = lambda s, lo, n: state[pl.ds(pl.multiple_of(s * rows + lo, 8), n), :]
    for lo in range(0, levels + 1, 16):
        pack_chunk(parity, lo, levels, send_s, wts_ref, tbl_ref, rows_of, (s0, s1, s2))


def middle_kernel(cs, a_ref, vt_ref, out_ref, exs):
    levels, cols, _ = a_ref.shape
    rows = vt_ref.shape[1]
    for l in range(levels):
        state = cs[pl.ds(l, cols, stride=rows), :].astype(BF16)
        exs[pl.ds(l, cols, stride=rows), :] = jnp.dot(a_ref[l], state, preferred_element_type=F32)
    for l in range(levels, rows):
        exs[pl.ds(l, cols, stride=rows), :] = jnp.zeros((cols, exs.shape[1]), F32)
    vertical(vt_ref, exs, out_ref)


def last_kernel(nedge, r1, local_ref, vt_ref, out_h, total, out_v, tbl_v, tbl_s, sems):
    levels, cols, width = out_h.shape
    rows = vt_ref.shape[1]
    add_edges((r1,), levels, nedge, vt_ref, total, tbl_v, tbl_s, sems.at[0])
    count = 5
    edges = [levels * i // count for i in range(count + 1)]
    copies = []
    for i, (lo, hi) in enumerate(zip(edges, edges[1:])):
        for l in range(lo, hi):
            out_v[l] = total[pl.ds(l, cols, stride=rows), :].astype(BF16)
        copies.append(pltpu.make_async_copy(out_v.at[pl.ds(lo, hi - lo)], out_h.at[pl.ds(lo, hi - lo)], sems.at[1 + i]))
        copies[-1].start()
    for copy in copies:
        copy.wait()


VM = pl.BlockSpec(memory_space=pltpu.VMEM)
HB = pl.BlockSpec(memory_space=pltpu.HBM)
DMA = pltpu.SemaphoreType.DMA


def call(kernel, ins, specs, outs, out_specs, scratch, limit, flops=0, aliases=None):
    size = sum(x.size * x.dtype.itemsize for x in (*ins, *outs))
    return pl.pallas_call(
        kernel,
        out_shape=outs,
        in_specs=specs,
        out_specs=out_specs,
        scratch_shapes=scratch,
        input_output_aliases=aliases or {},
        compiler_params=pltpu.CompilerParams(vmem_limit_bytes=limit * 2**20),
        cost_estimate=pl.CostEstimate(flops=flops, bytes_accessed=size, transcendentals=0),
    )(*ins)


def swapped(values, blk, basin):
    n, b = lax.axis_size(blk), lax.axis_size(basin)

    def pairs(first):
        order = [(i + first) % n for i in range(n)]
        partner = {order[i]: order[i + 1] for i in range(0, n - 1, 2)}
        partner |= {j: i for i, j in partner.items()}
        return [(i, partner.get(i, i)) for i in range(n)]

    return (
        lax.ppermute(values[0], blk, pairs(1)),
        lax.ppermute(values[1], basin, [(i, (i + 1) % b) for i in range(b)]),
        lax.ppermute(values[2], blk, pairs(0)),
    )


def local(tracers, nbr_cols, nbr_wts, self_wts, send_cols, recv_cols, edge_wts, wet_levels, vert_inv):
    cols, levels, width = tracers.shape
    rows = padded(levels)
    nedge = send_cols.shape[1]
    shape = jax.ShapeDtypeStruct
    by_level = jnp.transpose(tracers, (1, 0, 2))
    nbr_by_level = jnp.transpose(nbr_wts, (1, 0, 2))
    edge_by_entry = jnp.transpose(edge_wts, (0, 2, 1))
    wet = wet_levels.reshape(1, cols)
    in_hbm = lambda x: pltpu.with_memory_space_constraint(x, pltpu.HBM)
    send_h = in_hbm(send_cols)
    loads = [by_level, nbr_cols, nbr_by_level, self_wts, wet, vert_inv]
    same = lambda x: shape(x.shape, x.dtype)
    packed = [shape((message_rows(levels, nedge), width), BF16)] * 3
    columns = shape((cols * rows, width), F32)
    flat = pltpu.VMEM(columns.shape, F32)

    first = call(
        functools.partial(gather_kernel, "blk"),
        (in_hbm(by_level), send_h, *map(in_hbm, (recv_cols, edge_by_entry, *loads[1:]))),
        [HB] * 9,
        packed + [same(x) for x in loads] + [shape((128, 128), F32), shape((8, 128), F32)],
        [VM] * 11,
        [
            pltpu.VMEM((rows * (cols + 8), width), F32), pltpu.VMEM((128, 128), F32),
            pltpu.VMEM(recv_cols.shape, jnp.int32), pltpu.VMEM(edge_by_entry.shape, F32),
            pltpu.SMEM(send_cols.shape, jnp.int32), DMA((8 + -(-levels // 16),)),
        ],
        16,
    )
    sends, loads, (wts, tbl) = first[:3], first[3:9], first[9:]
    operator_flops = 2 * levels * cols * cols * width
    vertical_flops = 2 * cols * rows * rows * width

    def tables(count):
        return [pltpu.VMEM((count, 8, 128), jnp.int32), pltpu.SMEM((count, 8, 128), jnp.int32)]

    def arrived(partial, messages):
        return call(
            functools.partial(arrived_kernel, levels, nedge), (*messages, partial, vt), [VM] * (len(messages) + 2),
            [columns], [VM], tables(len(messages)) + [DMA], 16,
            flops=len(messages) * nedge * 2 * rows * rows * width, aliases={len(messages): 0},
        )[0]

    odd, along, even = swapped(sends, "blk", "basin")
    operator, partial, vt = call(
        operator_kernel, loads, [VM] * 6,
        [shape((levels, cols, cols), BF16), columns, shape((cols, rows, 128), BF16)], [VM] * 3,
        [flat, pltpu.VMEM((levels, 8, cols), F32), pltpu.VMEM((rows * rows, cols), F32), pltpu.VMEM((cols * rows, 128), F32)],
        32, flops=operator_flops + vertical_flops,
    )
    state, *sends = call(
        functools.partial(send_kernel, "blk", levels),
        (along, arrived(partial, (odd, even)), vt, wts, tbl, send_h), [VM] * 5 + [HB],
        [columns] + packed, [VM] * 4,
        tables(1) + [pltpu.SMEM(send_cols.shape, jnp.int32), DMA((2,))], 16, aliases={1: 0},
    )
    odd, along, even = swapped(sends, "blk", "basin")
    (partial,) = call(
        middle_kernel, (state, operator, vt), [VM] * 3, [columns], [VM], [flat], 32, flops=operator_flops + vertical_flops,
    )
    out, _ = call(
        functools.partial(last_kernel, nedge), (along, arrived(partial, (odd, even)), vt), [VM] * 3,
        [shape((levels, cols, width), BF16), columns], [HB, VM],
        [pltpu.VMEM((levels, cols, width), BF16)] + tables(1) + [DMA((6,))], 16, aliases={1: 1},
    )
    return jnp.transpose(out, (1, 0, 2))


def solution(mesh):
    in_specs = (
        P(("basin", "blk"), None, None),
        P(None, ("basin", "blk")),
        P(None, None, ("basin", "blk")),
        P(None, ("basin", "blk")),
        P(None, ("basin", "blk")),
        P(None, ("basin", "blk")),
        P(None, None, ("basin", "blk")),
        P(("basin", "blk")),
        P(None, None, ("basin", "blk")),
    )
    out_specs = P(("basin", "blk"), None, None)
    return jax.shard_map(local, mesh=mesh, in_specs=in_specs, out_specs=out_specs, check_vma=False)
```

```python
import functools

import jax
import jax.numpy as jnp
from jax import lax
from jax.experimental import pallas as pl
from jax.experimental.pallas import tpu as pltpu
from jax.sharding import PartitionSpec as P

NSTEP = 2
F32 = jnp.float32
BF16 = jnp.bfloat16


def padded(levels):
    return -(-levels // 8) * 8


def whole_rows(levels):
    return levels // 16 * 16


def message_rows(levels, nedge):
    return levels * nedge + 16


def direction(slot, parity):
    return 2 if slot == 1 else lax.bitwise_xor(parity, jnp.int32(1 - slot // 2))


def has_partner(slot, at, count):
    first = lax.bitwise_and(at + slot // 2, jnp.int32(1)) == 1
    return jnp.where(first, at + 1 < count, at > 0)


def pack_chunk(parity, lo, levels, send, weights, tbl, rows_of, outs):
    whole = whole_rows(levels)
    nedge = send.shape[1]
    rest = levels - whole
    share = 8 // rest if rest else 0
    for slot, out in enumerate(outs):
        d = direction(slot, parity)
        if lo < whole:
            for e in range(nedge):
                k = slot * nedge + e
                value = rows_of(send[d, e], lo, 16) * weights[lo : lo + 16, k : k + 1]
                out[e * whole + lo : e * whole + lo + 16, :] = value.astype(BF16)
            continue
        sub = lax.broadcasted_iota(jnp.int32, (8, out.shape[1]), 0)
        parts = []
        for first in range(0, nedge, share or nedge):
            part = None
            for q in range(share):
                k = slot * nedge + first + q
                value = rows_of(send[d, first + q], lo, 8) * weights[lo : lo + 8, k : k + 1]
                if q:
                    value = pltpu.roll(value, q * rest, 0)
                part = value if part is None else jnp.where(sub >= q * rest, value, part)
            if share:
                parts.append(part)
        table = jnp.broadcast_to(tbl[slot : slot + 1, :], (16, out.shape[1]))
        out[nedge * whole :, :] = jnp.concatenate(parts + [table], axis=0).astype(BF16)


def vertical(vt_ref, exs, out):
    cols, rows, _ = vt_ref.shape
    pad = jnp.zeros((64 - rows, out.shape[1]), F32)

    def column(j, _):
        at = pl.ds(pl.multiple_of(j * rows, 8), rows)
        x = jnp.concatenate([exs[at, :], pad], axis=0).astype(BF16)
        out[at, :] = jnp.dot(vt_ref[j][:, 0:64], x, preferred_element_type=F32)
        return _

    lax.fori_loop(0, cols, column, 0, unroll=16)


def add_edges(edges, levels, nedge, vt_ref, total, tbl_v, tbl_s, sem):
    whole = whole_rows(levels)
    rest = levels - whole
    share = 8 // rest if rest else 0
    rows = vt_ref.shape[1]
    for i, ref in enumerate(edges):
        tbl_v[i] = ref[levels * nedge :, :].astype(F32)[0:8].astype(jnp.int32)
    copy = pltpu.make_async_copy(tbl_v, tbl_s, sem)
    copy.start()
    copy.wait()
    group = max(share, 4)
    pad = jnp.zeros((8, total.shape[1]), F32)
    for i, ref in enumerate(edges):
        tails = ref[whole * nedge : levels * nedge, :].astype(F32) if rest else None
        for first in range(0, nedge, group):
            targets = [tbl_s[i, 0, e] for e in range(first, first + group)]
            products = []
            for e, j in zip(range(first, first + group), targets):
                x = ref[e * whole : (e + 1) * whole, :]
                if rest:
                    tail = tails[e // share * 8 : e // share * 8 + 8]
                    if e % share:
                        tail = pltpu.roll(tail, 8 - e % share * rest, 0)
                    x = jnp.concatenate([x, jnp.concatenate([tail, pad], axis=0).astype(BF16)], axis=0)
                products.append(jnp.dot(vt_ref[j][:, 0 : x.shape[0]], x, preferred_element_type=F32))
            for j, part in zip(targets, products):
                at = pl.ds(pl.multiple_of(j * rows, 8), rows)
                total[at, :] = total[at, :] + part


def gather_kernel(
    blk, c_h, send_h, recv_h, edge_h, nbr_h, nw_h, sw_h, wet_h,
    s0, s1, s2, c_v, nbr_v, nw_v, sw_v, wet_v, wts_o, tbl_o,
    cf, wts, recv_v, edge_v, send_s, sems,
):
    levels, cols, width = c_h.shape
    nedge = edge_h.shape[1]
    pitch = cols + 8
    bounds = [(lo, min(lo + 16, levels)) for lo in range(0, levels, 16)]
    pairs = [(send_h, send_s), (recv_h, recv_v), (edge_h, edge_v)]
    pairs += [(c_h.at[pl.ds(lo, hi - lo)], c_v.at[pl.ds(lo, hi - lo)]) for lo, hi in bounds]
    pairs += [(nbr_h, nbr_v), (nw_h, nw_v), (sw_h, sw_v), (wet_h, wet_v)]
    copies = [pltpu.make_async_copy(a, b, sems.at[i]) for i, (a, b) in enumerate(pairs)]
    for copy in copies:
        copy.start()
    parity = lax.bitwise_and(lax.axis_index(blk), jnp.int32(1))
    wts[...] = jnp.zeros_like(wts)
    tbl_o[...] = jnp.zeros_like(tbl_o)
    for copy in copies[:3]:
        copy.wait()
    for slot in range(3):
        d = direction(slot, parity)
        weight = edge_v[d]
        if slot != 1:
            weight = jnp.where(has_partner(slot, lax.axis_index(blk), lax.axis_size(blk)), weight, 0.0)
        wts[slot * nedge : (slot + 1) * nedge, 0:levels] = weight
        tbl_o[slot : slot + 1, 0:nedge] = recv_v[pl.ds(d, 1), :].astype(F32)
    weights = wts[...].T
    wts_o[...] = weights
    rows_of = lambda s, lo, n: cf[pl.ds(lo * pitch + s, n, stride=pitch), :]
    for i, (lo, hi) in enumerate(bounds):
        copies[3 + i].wait()
        for l in range(lo, hi):
            cf[l * pitch : l * pitch + cols, :] = c_v[l].astype(F32)
        pack_chunk(parity, lo, levels, send_s, weights, tbl_o, rows_of, (s0, s1, s2))
    if levels % 16 == 0:
        pack_chunk(parity, levels, levels, send_s, weights, tbl_o, rows_of, (s0, s1, s2))
    for copy in copies[3 + len(bounds) :]:
        copy.wait()


def operator_kernel(c_ref, nbr_ref, nw_ref, sw_ref, wet_ref, v_h, a_ref, state_ref, vt_ref, exs, merged, vf, vts, v_ref, sem):
    levels, cols, width = c_ref.shape
    load = pltpu.make_async_copy(v_h, v_ref, sem)
    load.start()
    rows = padded(levels)
    nbr = nbr_ref.shape[0]
    lane = lax.broadcasted_iota(jnp.int32, (8, cols), 1)
    sub = lax.broadcasted_iota(jnp.int32, (8, cols), 0)
    target = jnp.where(sub == nbr, lane, -1)
    for n in range(nbr):
        target = jnp.where(sub == n, nbr_ref[n : n + 1, :], target)
    same = [(target == nbr_ref[n : n + 1, :]).astype(F32) for n in range(nbr)]
    same.append((target == lane).astype(F32))
    for l in range(levels):
        total = same[nbr] * sw_ref[l : l + 1, :]
        for n in range(nbr):
            total = total + same[n] * nw_ref[l, n : n + 1, :]
        merged[l] = total
    half = 16
    for jt in range(cols // half):
        j = lax.broadcasted_iota(jnp.int32, (half, cols), 0) + jt * half
        hits = [j == nbr_ref[n : n + 1, :] for n in range(nbr)]
        hits.append(j == lax.broadcasted_iota(jnp.int32, (half, cols), 1))

        def fill(l, _):
            value = jnp.zeros((half, cols), F32)
            for n in range(nbr, -1, -1):
                value = jnp.where(hits[n], merged[l, n : n + 1, :], value)
            a_ref[l, jt * half : (jt + 1) * half, :] = value.astype(BF16)
            return _

        lax.fori_loop(0, levels, fill, 0, unroll=5)
    for l in range(levels):
        exs[pl.ds(l, cols, stride=rows), :] = jnp.dot(a_ref[l], c_ref[l], preferred_element_type=F32)
    for l in range(levels, rows):
        exs[pl.ds(l, cols, stride=rows), :] = jnp.zeros((cols, width), F32)
    level = lax.broadcasted_iota(jnp.int32, (levels, cols), 0)
    wet = wet_ref[...]
    load.wait()
    vf[...] = jnp.zeros_like(vf)
    for m in range(levels):
        keep = jnp.maximum(level, m) < wet
        vf[m * rows : m * rows + levels, :] = jnp.where(keep, v_ref[m].astype(F32), 0.0)
    for l in range(rows):
        block = vf[pl.ds(l, rows, stride=rows), :]
        block = jnp.concatenate([block, jnp.zeros((128 - rows, cols), F32)], axis=0)
        vts[pl.ds(l, cols, stride=rows), :] = block.T
    vt_ref[...] = vts[...].reshape(cols, rows, 128).astype(BF16)
    vertical(vt_ref, exs, state_ref)


def arrived_kernel(levels, nedge, *refs):
    *edges, _, vt_ref, total, tbl_v, tbl_s, sem = refs
    add_edges(edges, levels, nedge, vt_ref, total, tbl_v, tbl_s, sem)


def send_kernel(blk, levels, r1, local_ref, vt_ref, wts_ref, tbl_ref, send_h, state, s0, s1, s2, tbl_v, tbl_s, send_s, sems):
    copy = pltpu.make_async_copy(send_h, send_s, sems.at[1])
    copy.start()
    parity = lax.bitwise_and(lax.axis_index(blk), jnp.int32(1))
    rows = vt_ref.shape[1]
    add_edges((r1,), levels, send_h.shape[1], vt_ref, state, tbl_v, tbl_s, sems.at[0])
    copy.wait()
    rows_of = lambda s, lo, n: state[pl.ds(pl.multiple_of(s * rows + lo, 8), n), :]
    for lo in range(0, levels + 1, 16):
        pack_chunk(parity, lo, levels, send_s, wts_ref, tbl_ref, rows_of, (s0, s1, s2))


def middle_kernel(cs, a_ref, vt_ref, out_ref, exs):
    levels, cols, _ = a_ref.shape
    rows = vt_ref.shape[1]
    for l in range(levels):
        state = cs[pl.ds(l, cols, stride=rows), :].astype(BF16)
        exs[pl.ds(l, cols, stride=rows), :] = jnp.dot(a_ref[l], state, preferred_element_type=F32)
    for l in range(levels, rows):
        exs[pl.ds(l, cols, stride=rows), :] = jnp.zeros((cols, exs.shape[1]), F32)
    vertical(vt_ref, exs, out_ref)


def last_kernel(nedge, r1, local_ref, vt_ref, out_h, total, out_v, tbl_v, tbl_s, sems):
    levels, cols, width = out_h.shape
    rows = vt_ref.shape[1]
    add_edges((r1,), levels, nedge, vt_ref, total, tbl_v, tbl_s, sems.at[0])
    count = 5
    edges = [levels * i // count for i in range(count + 1)]
    copies = []
    for i, (lo, hi) in enumerate(zip(edges, edges[1:])):
        for l in range(lo, hi):
            out_v[l] = total[pl.ds(l, cols, stride=rows), :].astype(BF16)
        copies.append(pltpu.make_async_copy(out_v.at[pl.ds(lo, hi - lo)], out_h.at[pl.ds(lo, hi - lo)], sems.at[1 + i]))
        copies[-1].start()
    for copy in copies:
        copy.wait()


VM = pl.BlockSpec(memory_space=pltpu.VMEM)
HB = pl.BlockSpec(memory_space=pltpu.HBM)
DMA = pltpu.SemaphoreType.DMA


def call(kernel, ins, specs, outs, out_specs, scratch, limit, flops=0, aliases=None):
    size = sum(x.size * x.dtype.itemsize for x in (*ins, *outs))
    return pl.pallas_call(
        kernel,
        out_shape=outs,
        in_specs=specs,
        out_specs=out_specs,
        scratch_shapes=scratch,
        input_output_aliases=aliases or {},
        compiler_params=pltpu.CompilerParams(vmem_limit_bytes=limit * 2**20),
        cost_estimate=pl.CostEstimate(flops=flops, bytes_accessed=size, transcendentals=0),
    )(*ins)


def swapped(values, blk, basin):
    n, b = lax.axis_size(blk), lax.axis_size(basin)

    def pairs(first):
        partner = {i: i + 1 for i in range(first, n - 1, 2)}
        partner |= {j: i for i, j in partner.items()}
        across = lambda g: g ^ 1 if g ^ 1 < b else g
        return [(g * n + i, g * n + partner[i] if i in partner else across(g) * n + i) for g in range(b) for i in range(n)]

    return (
        lax.ppermute(values[0], (basin, blk), pairs(1)),
        lax.ppermute(values[1], basin, [(i, (i + 1) % b) for i in range(b)]),
        lax.ppermute(values[2], (basin, blk), pairs(0)),
    )


def local(tracers, nbr_cols, nbr_wts, self_wts, send_cols, recv_cols, edge_wts, wet_levels, vert_inv):
    cols, levels, width = tracers.shape
    rows = padded(levels)
    nedge = send_cols.shape[1]
    shape = jax.ShapeDtypeStruct
    by_level = jnp.transpose(tracers, (1, 0, 2))
    nbr_by_level = jnp.transpose(nbr_wts, (1, 0, 2))
    edge_by_entry = jnp.transpose(edge_wts, (0, 2, 1))
    wet = wet_levels.reshape(1, cols)
    in_hbm = lambda x: pltpu.with_memory_space_constraint(x, pltpu.HBM)
    send_h = in_hbm(send_cols)
    loads = [by_level, nbr_cols, nbr_by_level, self_wts, wet]
    same = lambda x: shape(x.shape, x.dtype)
    packed = [shape((message_rows(levels, nedge), width), BF16)] * 3
    columns = shape((cols * rows, width), F32)
    flat = pltpu.VMEM(columns.shape, F32)

    first = call(
        functools.partial(gather_kernel, "blk"),
        (in_hbm(by_level), send_h, *map(in_hbm, (recv_cols, edge_by_entry, *loads[1:]))),
        [HB] * 8,
        packed + [same(x) for x in loads] + [shape((128, 128), F32), shape((8, 128), F32)],
        [VM] * 10,
        [
            pltpu.VMEM((rows * (cols + 8), width), F32), pltpu.VMEM((128, 128), F32),
            pltpu.VMEM(recv_cols.shape, jnp.int32), pltpu.VMEM(edge_by_entry.shape, F32),
            pltpu.SMEM(send_cols.shape, jnp.int32), DMA((7 + -(-levels // 16),)),
        ],
        16,
    )
    sends, loads, (wts, tbl) = first[:3], first[3:8], first[8:]
    operator_flops = 2 * levels * cols * cols * width
    vertical_flops = 2 * cols * rows * rows * width

    def tables(count):
        return [pltpu.VMEM((count, 8, 128), jnp.int32), pltpu.SMEM((count, 8, 128), jnp.int32)]

    def arrived(partial, messages):
        return call(
            functools.partial(arrived_kernel, levels, nedge), (*messages, partial, vt), [VM] * (len(messages) + 2),
            [columns], [VM], tables(len(messages)) + [DMA], 16,
            flops=len(messages) * nedge * 2 * rows * rows * width, aliases={len(messages): 0},
        )[0]

    odd, along, even = swapped(sends, "blk", "basin")
    operator, partial, vt = call(
        operator_kernel, (*loads, in_hbm(vert_inv)), [VM] * 5 + [HB],
        [shape((levels, cols, cols), BF16), columns, shape((cols, rows, 128), BF16)], [VM] * 3,
        [flat, pltpu.VMEM((levels, 8, cols), F32), pltpu.VMEM((rows * rows, cols), F32), pltpu.VMEM((cols * rows, 128), F32),
         pltpu.VMEM(vert_inv.shape, BF16), DMA],
        32, flops=operator_flops + vertical_flops,
    )
    state, *sends = call(
        functools.partial(send_kernel, "blk", levels),
        (along, arrived(partial, (odd, even)), vt, wts, tbl, send_h), [VM] * 5 + [HB],
        [columns] + packed, [VM] * 4,
        tables(1) + [pltpu.SMEM(send_cols.shape, jnp.int32), DMA((2,))], 16, aliases={1: 0},
    )
    odd, along, even = swapped(sends, "blk", "basin")
    (partial,) = call(
        middle_kernel, (state, operator, vt), [VM] * 3, [columns], [VM], [flat], 32, flops=operator_flops + vertical_flops,
    )
    out, _ = call(
        functools.partial(last_kernel, nedge), (along, arrived(partial, (odd, even)), vt), [VM] * 3,
        [shape((levels, cols, width), BF16), columns], [HB, VM],
        [pltpu.VMEM((levels, cols, width), BF16)] + tables(1) + [DMA((6,))], 16, aliases={1: 1},
    )
    return jnp.transpose(out, (1, 0, 2))


def solution(mesh):
    in_specs = (
        P(("basin", "blk"), None, None),
        P(None, ("basin", "blk")),
        P(None, None, ("basin", "blk")),
        P(None, ("basin", "blk")),
        P(None, ("basin", "blk")),
        P(None, ("basin", "blk")),
        P(None, None, ("basin", "blk")),
        P(("basin", "blk")),
        P(None, None, ("basin", "blk")),
    )
    out_specs = P(("basin", "blk"), None, None)
    return jax.shard_map(local, mesh=mesh, in_specs=in_specs, out_specs=out_specs, check_vma=False)
```

```python
import functools

import jax
import jax.numpy as jnp
from jax import lax
from jax.experimental import pallas as pl
from jax.experimental.pallas import tpu as pltpu
from jax.sharding import PartitionSpec as P

NSTEP = 2
F32 = jnp.float32
BF16 = jnp.bfloat16


def padded(levels):
    return -(-levels // 8) * 8


def whole_rows(levels):
    return levels // 16 * 16


def message_rows(levels, nedge):
    return levels * nedge + 16


def direction(slot, parity):
    return 2 if slot == 1 else lax.bitwise_xor(parity, jnp.int32(1 - slot // 2))


def has_partner(slot, at, count):
    first = lax.bitwise_and(at + slot // 2, jnp.int32(1)) == 1
    return jnp.where(first, at + 1 < count, at > 0)


def pack_chunk(parity, lo, levels, send, weights, tbl, rows_of, slots, outs):
    whole = whole_rows(levels)
    nedge = send.shape[1]
    rest = levels - whole
    share = 8 // rest if rest else 0
    for slot, out in zip(slots, outs):
        d = direction(slot, parity)
        if lo < whole:
            for e in range(nedge):
                k = slot * nedge + e
                value = rows_of(send[d, e], lo, 16) * weights[lo : lo + 16, k : k + 1]
                out[e * whole + lo : e * whole + lo + 16, :] = value.astype(BF16)
            continue
        sub = lax.broadcasted_iota(jnp.int32, (8, out.shape[1]), 0)
        parts = []
        for first in range(0, nedge, share or nedge):
            part = None
            for q in range(share):
                k = slot * nedge + first + q
                value = rows_of(send[d, first + q], lo, 8) * weights[lo : lo + 8, k : k + 1]
                if q:
                    value = pltpu.roll(value, q * rest, 0)
                part = value if part is None else jnp.where(sub >= q * rest, value, part)
            if share:
                parts.append(part)
        table = jnp.broadcast_to(tbl[slot : slot + 1, :], (16, out.shape[1]))
        out[nedge * whole :, :] = jnp.concatenate(parts + [table], axis=0).astype(BF16)


def vertical(vt_ref, exs, out):
    cols, rows, _ = vt_ref.shape
    pad = jnp.zeros((64 - rows, out.shape[1]), F32)

    def column(j, _):
        at = pl.ds(pl.multiple_of(j * rows, 8), rows)
        x = jnp.concatenate([exs[at, :], pad], axis=0).astype(BF16)
        out[at, :] = jnp.dot(vt_ref[j][:, 0:64], x, preferred_element_type=F32)
        return _

    lax.fori_loop(0, cols, column, 0, unroll=16)


def add_edges(edges, levels, nedge, vt_ref, total, tbl_v, tbl_s, sem):
    whole = whole_rows(levels)
    rest = levels - whole
    share = 8 // rest if rest else 0
    rows = vt_ref.shape[1]
    for i, ref in enumerate(edges):
        tbl_v[i] = ref[levels * nedge :, :].astype(F32)[0:8].astype(jnp.int32)
    copy = pltpu.make_async_copy(tbl_v, tbl_s, sem)
    copy.start()
    copy.wait()
    group = max(share, 4)
    pad = jnp.zeros((8, total.shape[1]), F32)
    for i, ref in enumerate(edges):
        tails = ref[whole * nedge : levels * nedge, :].astype(F32) if rest else None
        for first in range(0, nedge, group):
            targets = [tbl_s[i, 0, e] for e in range(first, first + group)]
            products = []
            for e, j in zip(range(first, first + group), targets):
                x = ref[e * whole : (e + 1) * whole, :]
                if rest:
                    tail = tails[e // share * 8 : e // share * 8 + 8]
                    if e % share:
                        tail = pltpu.roll(tail, 8 - e % share * rest, 0)
                    x = jnp.concatenate([x, jnp.concatenate([tail, pad], axis=0).astype(BF16)], axis=0)
                products.append(jnp.dot(vt_ref[j][:, 0 : x.shape[0]], x, preferred_element_type=F32))
            for j, part in zip(targets, products):
                at = pl.ds(pl.multiple_of(j * rows, 8), rows)
                total[at, :] = total[at, :] + part


def gather_kernel(
    blk, c_h, send_h, recv_h, edge_h, nbr_h, nw_h, sw_h, wet_h,
    s0, s1, c_v, nbr_v, nw_v, sw_v, wet_v, wts_o, tbl_o, cf,
    wts, recv_v, edge_v, send_s, sems,
):
    levels, cols, width = c_h.shape
    nedge = edge_h.shape[1]
    pitch = cols + 8
    bounds = [(lo, min(lo + 16, levels)) for lo in range(0, levels, 16)]
    pairs = [(send_h, send_s), (recv_h, recv_v), (edge_h, edge_v)]
    pairs += [(c_h.at[pl.ds(lo, hi - lo)], c_v.at[pl.ds(lo, hi - lo)]) for lo, hi in bounds]
    pairs += [(nbr_h, nbr_v), (nw_h, nw_v), (sw_h, sw_v), (wet_h, wet_v)]
    copies = [pltpu.make_async_copy(a, b, sems.at[i]) for i, (a, b) in enumerate(pairs)]
    for copy in copies:
        copy.start()
    parity = lax.bitwise_and(lax.axis_index(blk), jnp.int32(1))
    wts[...] = jnp.zeros_like(wts)
    tbl_o[...] = jnp.zeros_like(tbl_o)
    for copy in copies[:3]:
        copy.wait()
    for slot in range(3):
        d = direction(slot, parity)
        weight = edge_v[d]
        if slot != 1:
            weight = jnp.where(has_partner(slot, lax.axis_index(blk), lax.axis_size(blk)), weight, 0.0)
        wts[slot * nedge : (slot + 1) * nedge, 0:levels] = weight
        tbl_o[slot : slot + 1, 0:nedge] = recv_v[pl.ds(d, 1), :].astype(F32)
    weights = wts[...].T
    wts_o[...] = weights
    rows_of = lambda s, lo, n: cf[pl.ds(lo * pitch + s, n, stride=pitch), :]
    for i, (lo, hi) in enumerate(bounds):
        copies[3 + i].wait()
        for l in range(lo, hi):
            cf[l * pitch : l * pitch + cols, :] = c_v[l].astype(F32)
        pack_chunk(parity, lo, levels, send_s, weights, tbl_o, rows_of, (0, 1), (s0, s1))
    if levels % 16 == 0:
        pack_chunk(parity, levels, levels, send_s, weights, tbl_o, rows_of, (0, 1), (s0, s1))
    for copy in copies[3 + len(bounds) :]:
        copy.wait()


def column_operator(nbr_ref, nw_ref, sw_ref, a_ref, merged):
    levels = nw_ref.shape[0]
    cols = nbr_ref.shape[1]
    nbr = nbr_ref.shape[0]
    lane = lax.broadcasted_iota(jnp.int32, (8, cols), 1)
    sub = lax.broadcasted_iota(jnp.int32, (8, cols), 0)
    target = jnp.where(sub == nbr, lane, -1)
    for n in range(nbr):
        target = jnp.where(sub == n, nbr_ref[n : n + 1, :], target)
    same = [(target == nbr_ref[n : n + 1, :]).astype(F32) for n in range(nbr)]
    same.append((target == lane).astype(F32))
    for l in range(levels):
        total = same[nbr] * sw_ref[l : l + 1, :]
        for n in range(nbr):
            total = total + same[n] * nw_ref[l, n : n + 1, :]
        merged[l] = total
    half = 16
    for jt in range(cols // half):
        j = lax.broadcasted_iota(jnp.int32, (half, cols), 0) + jt * half
        hits = [j == nbr_ref[n : n + 1, :] for n in range(nbr)]
        hits.append(j == lax.broadcasted_iota(jnp.int32, (half, cols), 1))

        def fill(p, _):
            for i in range(2):
                value = jnp.zeros((half, cols), F32)
                for n in range(nbr, -1, -1):
                    value = jnp.where(hits[n], merged[p * 2 + i, n : n + 1, :], value)
                a_ref[p, jt * half : (jt + 1) * half, i * cols : (i + 1) * cols] = value.astype(BF16)
            return _

        lax.fori_loop(0, levels // 2, fill, 0, unroll=5)


def level_products(a_ref, state_of, exs, rows):
    pairs, cols, _ = a_ref.shape
    width = exs.shape[1]
    zero = jnp.zeros((cols, width), BF16)
    for p in range(pairs):
        left = jnp.concatenate([state_of(2 * p), zero], axis=1)
        right = jnp.concatenate([zero, state_of(2 * p + 1)], axis=1)
        both = jnp.dot(a_ref[p], jnp.concatenate([left, right], axis=0), preferred_element_type=F32)
        exs[pl.ds(2 * p, cols, stride=rows), :] = both[:, 0:width]
        exs[pl.ds(2 * p + 1, cols, stride=rows), :] = both[:, width:]
    for l in range(2 * pairs, rows):
        exs[pl.ds(l, cols, stride=rows), :] = jnp.zeros((cols, width), F32)


def operator_kernel(
    blk, c_ref, nbr_ref, nw_ref, sw_ref, wet_ref, cf, wts_ref, tbl_ref, send_h, v_h,
    a_ref, state_ref, vt_ref, s2, exs, merged, vf, vts, v_ref, send_s, sems,
):
    levels, cols, width = c_ref.shape
    rows = padded(levels)
    load = pltpu.make_async_copy(v_h, v_ref, sems.at[0])
    load.start()
    copy = pltpu.make_async_copy(send_h, send_s, sems.at[1])
    copy.start()
    column_operator(nbr_ref, nw_ref, sw_ref, a_ref, merged)
    copy.wait()
    parity = lax.bitwise_and(lax.axis_index(blk), jnp.int32(1))
    pitch = cols + 8
    rows_of = lambda s, lo, n: cf[pl.ds(lo * pitch + s, n, stride=pitch), :]
    for lo in range(0, levels + 1, 16):
        pack_chunk(parity, lo, levels, send_s, wts_ref, tbl_ref, rows_of, (2,), (s2,))
    level_products(a_ref, lambda l: c_ref[l], exs, rows)
    level = lax.broadcasted_iota(jnp.int32, (levels, cols), 0)
    wet = wet_ref[...]
    load.wait()
    vf[...] = jnp.zeros_like(vf)
    for m in range(levels):
        keep = jnp.maximum(level, m) < wet
        vf[m * rows : m * rows + levels, :] = jnp.where(keep, v_ref[m].astype(F32), 0.0)
    for l in range(rows):
        block = vf[pl.ds(l, rows, stride=rows), :]
        block = jnp.concatenate([block, jnp.zeros((128 - rows, cols), F32)], axis=0)
        vts[pl.ds(l, cols, stride=rows), :] = block.T
    vt_ref[...] = vts[...].reshape(cols, rows, 128).astype(BF16)
    vertical(vt_ref, exs, state_ref)


def arrived_kernel(levels, nedge, *refs):
    *edges, _, vt_ref, total, tbl_v, tbl_s, sem = refs
    add_edges(edges, levels, nedge, vt_ref, total, tbl_v, tbl_s, sem)


def send_kernel(blk, levels, r0, r2, local_ref, vt_ref, wts_ref, tbl_ref, send_h, state, s0, s1, tbl_v, tbl_s, send_s, sems):
    copy = pltpu.make_async_copy(send_h, send_s, sems.at[1])
    copy.start()
    add_edges((r0, r2), levels, send_h.shape[1], vt_ref, state, tbl_v, tbl_s, sems.at[0])
    copy.wait()
    pack_state(blk, levels, send_s, wts_ref, tbl_ref, state, vt_ref.shape[1], (0, 1), (s0, s1))


def pack_state(blk, levels, send, weights, tbl, state, rows, slots, outs):
    parity = lax.bitwise_and(lax.axis_index(blk), jnp.int32(1))
    rows_of = lambda s, lo, n: state[pl.ds(pl.multiple_of(s * rows + lo, 8), n), :]
    for lo in range(0, levels + 1, 16):
        pack_chunk(parity, lo, levels, send, weights, tbl, rows_of, slots, outs)


def middle_kernel(blk, levels, cs, a_ref, vt_ref, wts_ref, tbl_ref, send_h, out_ref, s2, exs, send_s, sem):
    copy = pltpu.make_async_copy(send_h, send_s, sem)
    copy.start()
    cols, rows, _ = vt_ref.shape
    level_products(a_ref, lambda l: cs[pl.ds(l, cols, stride=rows), :].astype(BF16), exs, rows)
    copy.wait()
    pack_state(blk, levels, send_s, wts_ref, tbl_ref, cs, rows, (2,), (s2,))
    vertical(vt_ref, exs, out_ref)


def last_kernel(nedge, r0, r2, local_ref, vt_ref, out_h, total, out_v, tbl_v, tbl_s, sems):
    levels, cols, width = out_h.shape
    rows = vt_ref.shape[1]
    add_edges((r0, r2), levels, nedge, vt_ref, total, tbl_v, tbl_s, sems.at[0])
    count = 5
    edges = [levels * i // count for i in range(count + 1)]
    copies = []
    for i, (lo, hi) in enumerate(zip(edges, edges[1:])):
        for l in range(lo, hi):
            out_v[l] = total[pl.ds(l, cols, stride=rows), :].astype(BF16)
        copies.append(pltpu.make_async_copy(out_v.at[pl.ds(lo, hi - lo)], out_h.at[pl.ds(lo, hi - lo)], sems.at[1 + i]))
        copies[-1].start()
    for copy in copies:
        copy.wait()


VM = pl.BlockSpec(memory_space=pltpu.VMEM)
HB = pl.BlockSpec(memory_space=pltpu.HBM)
DMA = pltpu.SemaphoreType.DMA


def call(kernel, ins, specs, outs, out_specs, scratch, limit, flops=0, aliases=None):
    size = sum(x.size * x.dtype.itemsize for x in (*ins, *outs))
    return pl.pallas_call(
        kernel,
        out_shape=outs,
        in_specs=specs,
        out_specs=out_specs,
        scratch_shapes=scratch,
        input_output_aliases=aliases or {},
        compiler_params=pltpu.CompilerParams(vmem_limit_bytes=limit * 2**20),
        cost_estimate=pl.CostEstimate(flops=flops, bytes_accessed=size, transcendentals=0),
    )(*ins)


def odd_or_even(value, first, blk, basin):
    n, b = lax.axis_size(blk), lax.axis_size(basin)
    partner = {i: i + 1 for i in range(first, n - 1, 2)}
    partner |= {j: i for i, j in partner.items()}
    across = lambda g: g ^ 1 if g ^ 1 < b else g
    route = [(g * n + i, g * n + partner[i] if i in partner else across(g) * n + i) for g in range(b) for i in range(n)]
    return lax.ppermute(value, (basin, blk), route)


def along_basin(value, basin):
    b = lax.axis_size(basin)
    return lax.ppermute(value, basin, [(i, (i + 1) % b) for i in range(b)])


def local(tracers, nbr_cols, nbr_wts, self_wts, send_cols, recv_cols, edge_wts, wet_levels, vert_inv):
    cols, levels, width = tracers.shape
    rows = padded(levels)
    nedge = send_cols.shape[1]
    shape = jax.ShapeDtypeStruct
    by_level = jnp.transpose(tracers, (1, 0, 2))
    nbr_by_level = jnp.transpose(nbr_wts, (1, 0, 2))
    edge_by_entry = jnp.transpose(edge_wts, (0, 2, 1))
    wet = wet_levels.reshape(1, cols)
    in_hbm = lambda x: pltpu.with_memory_space_constraint(x, pltpu.HBM)
    send_h = in_hbm(send_cols)
    loads = [by_level, nbr_cols, nbr_by_level, self_wts, wet]
    same = lambda x: shape(x.shape, x.dtype)
    message = shape((message_rows(levels, nedge), width), BF16)
    columns = shape((cols * rows, width), F32)
    flat = pltpu.VMEM(columns.shape, F32)
    send_table = pltpu.SMEM(send_cols.shape, jnp.int32)

    first = call(
        functools.partial(gather_kernel, "blk"),
        (in_hbm(by_level), send_h, *map(in_hbm, (recv_cols, edge_by_entry, *loads[1:]))),
        [HB] * 8,
        [message] * 2 + [same(x) for x in loads]
        + [shape((128, 128), F32), shape((8, 128), F32), shape((rows * (cols + 8), width), F32)],
        [VM] * 10,
        [
            pltpu.VMEM((128, 128), F32), pltpu.VMEM(recv_cols.shape, jnp.int32), pltpu.VMEM(edge_by_entry.shape, F32),
            send_table, DMA((7 + -(-levels // 16),)),
        ],
        16,
    )
    (to_odd, to_next), (state, nbr, nbr_w, self_w, wet), (wts, tbl, by_row) = first[:2], first[2:7], first[7:]
    operator_flops = 2 * levels * cols * cols * width
    vertical_flops = 2 * cols * rows * rows * width

    def tables(count):
        return [pltpu.VMEM((count, 8, 128), jnp.int32), pltpu.SMEM((count, 8, 128), jnp.int32)]

    def arrived(partial, *messages):
        return call(
            functools.partial(arrived_kernel, levels, nedge), (*messages, partial, vt), [VM] * (len(messages) + 2),
            [columns], [VM], tables(len(messages)) + [DMA], 16,
            flops=len(messages) * nedge * 2 * rows * rows * width, aliases={len(messages): 0},
        )[0]

    along = along_basin(to_next, "basin")
    odd = odd_or_even(to_odd, 1, "blk", "basin")
    operator, partial, vt, to_even = call(
        functools.partial(operator_kernel, "blk"),
        (state, nbr, nbr_w, self_w, wet, by_row, wts, tbl, send_h, in_hbm(vert_inv)), [VM] * 8 + [HB] * 2,
        [shape((levels // 2, cols, 2 * cols), BF16), columns, shape((cols, rows, 128), BF16), message], [VM] * 4,
        [flat, pltpu.VMEM((levels, 8, cols), F32), pltpu.VMEM((rows * rows, cols), F32), pltpu.VMEM((cols * rows, 128), F32),
         pltpu.VMEM(vert_inv.shape, BF16), send_table, DMA((2,))],
        32, flops=operator_flops + vertical_flops,
    )
    even = odd_or_even(to_even, 0, "blk", "basin")
    state, to_odd, to_next = call(
        functools.partial(send_kernel, "blk", levels),
        (odd, even, arrived(partial, along), vt, wts, tbl, send_h), [VM] * 6 + [HB],
        [columns] + [message] * 2, [VM] * 3,
        tables(2) + [send_table, DMA((2,))], 16, aliases={2: 0},
    )
    along = along_basin(to_next, "basin")
    odd = odd_or_even(to_odd, 1, "blk", "basin")
    partial, to_even = call(
        functools.partial(middle_kernel, "blk", levels), (state, operator, vt, wts, tbl, send_h), [VM] * 5 + [HB],
        [columns, message], [VM] * 2, [flat, send_table, DMA], 32, flops=operator_flops + vertical_flops,
    )
    even = odd_or_even(to_even, 0, "blk", "basin")
    out, _ = call(
        functools.partial(last_kernel, nedge), (odd, even, arrived(partial, along), vt), [VM] * 4,
        [shape((levels, cols, width), BF16), columns], [HB, VM],
        [pltpu.VMEM((levels, cols, width), BF16)] + tables(2) + [DMA((6,))], 16, aliases={2: 1},
    )
    return jnp.transpose(out, (1, 0, 2))


def solution(mesh):
    in_specs = (
        P(("basin", "blk"), None, None),
        P(None, ("basin", "blk")),
        P(None, None, ("basin", "blk")),
        P(None, ("basin", "blk")),
        P(None, ("basin", "blk")),
        P(None, ("basin", "blk")),
        P(None, None, ("basin", "blk")),
        P(("basin", "blk")),
        P(None, None, ("basin", "blk")),
    )
    out_specs = P(("basin", "blk"), None, None)
    return jax.shard_map(local, mesh=mesh, in_specs=in_specs, out_specs=out_specs, check_vma=False)
```

```python
import functools

import jax
import jax.numpy as jnp
from jax import lax
from jax.experimental import pallas as pl
from jax.experimental.pallas import tpu as pltpu
from jax.sharding import PartitionSpec as P

NSTEP = 2
F32 = jnp.float32
BF16 = jnp.bfloat16


def padded(levels):
    return -(-levels // 8) * 8


def whole_rows(levels):
    return levels // 16 * 16


def message_rows(levels, nedge):
    return levels * nedge + 16


def direction(slot, parity):
    return lax.bitwise_xor(parity, jnp.int32(2 - slot)) if slot else 2


def has_partner(slot, at, count):
    first = lax.bitwise_and(at + slot // 2, jnp.int32(1)) == 1
    return jnp.where(first, at + 1 < count, at > 0)


def pack_chunk(parity, lo, levels, send, weights, tbl, rows_of, slots, outs):
    whole = whole_rows(levels)
    nedge = send.shape[1]
    rest = levels - whole
    share = 8 // rest if rest else 0
    for slot, out in zip(slots, outs):
        d = direction(slot, parity)
        if lo < whole:
            for e in range(nedge):
                k = slot * nedge + e
                value = rows_of(send[d, e], lo, 16) * weights[lo : lo + 16, k : k + 1]
                out[e * whole + lo : e * whole + lo + 16, :] = value.astype(BF16)
            continue
        sub = lax.broadcasted_iota(jnp.int32, (8, out.shape[1]), 0)
        parts = []
        for first in range(0, nedge, share or nedge):
            part = None
            for q in range(share):
                k = slot * nedge + first + q
                value = rows_of(send[d, first + q], lo, 8) * weights[lo : lo + 8, k : k + 1]
                if q:
                    value = pltpu.roll(value, q * rest, 0)
                part = value if part is None else jnp.where(sub >= q * rest, value, part)
            if share:
                parts.append(part)
        table = jnp.broadcast_to(tbl[slot : slot + 1, :], (16, out.shape[1]))
        out[nedge * whole :, :] = jnp.concatenate(parts + [table], axis=0).astype(BF16)


def vertical(vt_ref, exs, out):
    cols, rows, _ = vt_ref.shape
    pad = jnp.zeros((64 - rows, out.shape[1]), F32)

    def column(j, _):
        at = pl.ds(pl.multiple_of(j * rows, 8), rows)
        x = jnp.concatenate([exs[at, :], pad], axis=0).astype(BF16)
        out[at, :] = jnp.dot(vt_ref[j][:, 0:64], x, preferred_element_type=F32)
        return _

    lax.fori_loop(0, cols, column, 0, unroll=16)


def add_edges(edges, levels, nedge, vt_ref, total, tbl_v, tbl_s, sem):
    whole = whole_rows(levels)
    rest = levels - whole
    share = 8 // rest if rest else 0
    rows = vt_ref.shape[1]
    for i, ref in enumerate(edges):
        tbl_v[i] = ref[levels * nedge :, :].astype(F32)[0:8].astype(jnp.int32)
    copy = pltpu.make_async_copy(tbl_v, tbl_s, sem)
    copy.start()
    copy.wait()
    group = max(share, 4)
    pad = jnp.zeros((8, total.shape[1]), F32)
    for i, ref in enumerate(edges):
        tails = ref[whole * nedge : levels * nedge, :].astype(F32) if rest else None
        for first in range(0, nedge, group):
            targets = [tbl_s[i, 0, e] for e in range(first, first + group)]
            products = []
            for e, j in zip(range(first, first + group), targets):
                x = ref[e * whole : (e + 1) * whole, :]
                if rest:
                    tail = tails[e // share * 8 : e // share * 8 + 8]
                    if e % share:
                        tail = pltpu.roll(tail, 8 - e % share * rest, 0)
                    x = jnp.concatenate([x, jnp.concatenate([tail, pad], axis=0).astype(BF16)], axis=0)
                products.append(jnp.dot(vt_ref[j][:, 0 : x.shape[0]], x, preferred_element_type=F32))
            for j, part in zip(targets, products):
                at = pl.ds(pl.multiple_of(j * rows, 8), rows)
                total[at, :] = total[at, :] + part


def gather_kernel(
    blk, c_h, send_h, recv_h, edge_h, nbr_h, nw_h, sw_h, wet_h,
    s0, s1, c_v, nbr_v, nw_v, sw_v, wet_v, wts_o, tbl_o, cf,
    wts, recv_v, edge_v, send_s, sems,
):
    levels, cols, width = c_h.shape
    nedge = edge_h.shape[1]
    pitch = cols + 8
    bounds = [(lo, min(lo + 16, levels)) for lo in range(0, levels, 16)]
    pairs = [(send_h, send_s), (recv_h, recv_v), (edge_h, edge_v)]
    pairs += [(c_h.at[pl.ds(lo, hi - lo)], c_v.at[pl.ds(lo, hi - lo)]) for lo, hi in bounds]
    pairs += [(nbr_h, nbr_v), (nw_h, nw_v), (sw_h, sw_v), (wet_h, wet_v)]
    copies = [pltpu.make_async_copy(a, b, sems.at[i]) for i, (a, b) in enumerate(pairs)]
    for copy in copies:
        copy.start()
    parity = lax.bitwise_and(lax.axis_index(blk), jnp.int32(1))
    wts[...] = jnp.zeros_like(wts)
    tbl_o[...] = jnp.zeros_like(tbl_o)
    for copy in copies[:3]:
        copy.wait()
    for slot in range(3):
        d = direction(slot, parity)
        weight = edge_v[d]
        if slot:
            weight = jnp.where(has_partner(slot, lax.axis_index(blk), lax.axis_size(blk)), weight, 0.0)
        wts[slot * nedge : (slot + 1) * nedge, 0:levels] = weight
        tbl_o[slot : slot + 1, 0:nedge] = recv_v[pl.ds(d, 1), :].astype(F32)
    weights = wts[...].T
    wts_o[...] = weights
    rows_of = lambda s, lo, n: cf[pl.ds(lo * pitch + s, n, stride=pitch), :]
    for i, (lo, hi) in enumerate(bounds):
        copies[3 + i].wait()
        for l in range(lo, hi):
            cf[l * pitch : l * pitch + cols, :] = c_v[l].astype(F32)
        pack_chunk(parity, lo, levels, send_s, weights, tbl_o, rows_of, (0, 1), (s0, s1))
    if levels % 16 == 0:
        pack_chunk(parity, levels, levels, send_s, weights, tbl_o, rows_of, (0, 1), (s0, s1))
    for copy in copies[3 + len(bounds) :]:
        copy.wait()


def column_operator(nbr_ref, nw_ref, sw_ref, a_ref, merged):
    levels = nw_ref.shape[0]
    cols = nbr_ref.shape[1]
    nbr = nbr_ref.shape[0]
    lane = lax.broadcasted_iota(jnp.int32, (8, cols), 1)
    sub = lax.broadcasted_iota(jnp.int32, (8, cols), 0)
    target = jnp.where(sub == nbr, lane, -1)
    for n in range(nbr):
        target = jnp.where(sub == n, nbr_ref[n : n + 1, :], target)
    same = [(target == nbr_ref[n : n + 1, :]).astype(F32) for n in range(nbr)]
    same.append((target == lane).astype(F32))
    for l in range(levels):
        total = same[nbr] * sw_ref[l : l + 1, :]
        for n in range(nbr):
            total = total + same[n] * nw_ref[l, n : n + 1, :]
        merged[l] = total
    half = 16
    for jt in range(cols // half):
        j = lax.broadcasted_iota(jnp.int32, (half, cols), 0) + jt * half
        hits = [j == nbr_ref[n : n + 1, :] for n in range(nbr)]
        hits.append(j == lax.broadcasted_iota(jnp.int32, (half, cols), 1))

        def fill(p, _):
            for i in range(2):
                value = jnp.zeros((half, cols), F32)
                for n in range(nbr, -1, -1):
                    value = jnp.where(hits[n], merged[p * 2 + i, n : n + 1, :], value)
                a_ref[p, jt * half : (jt + 1) * half, i * cols : (i + 1) * cols] = value.astype(BF16)
            return _

        lax.fori_loop(0, levels // 2, fill, 0, unroll=5)


def level_products(a_ref, state_of, exs, rows):
    pairs, cols, _ = a_ref.shape
    width = exs.shape[1]
    zero = jnp.zeros((cols, width), BF16)
    for p in range(pairs):
        left = jnp.concatenate([state_of(2 * p), zero], axis=1)
        right = jnp.concatenate([zero, state_of(2 * p + 1)], axis=1)
        both = jnp.dot(a_ref[p], jnp.concatenate([left, right], axis=0), preferred_element_type=F32)
        exs[pl.ds(2 * p, cols, stride=rows), :] = both[:, 0:width]
        exs[pl.ds(2 * p + 1, cols, stride=rows), :] = both[:, width:]
    for l in range(2 * pairs, rows):
        exs[pl.ds(l, cols, stride=rows), :] = jnp.zeros((cols, width), F32)


def operator_kernel(
    blk, c_ref, nbr_ref, nw_ref, sw_ref, wet_ref, cf, wts_ref, tbl_ref, send_h, v_h,
    a_ref, state_ref, vt_ref, s2, exs, merged, vf, vts, v_ref, send_s, sems,
):
    levels, cols, width = c_ref.shape
    rows = padded(levels)
    load = pltpu.make_async_copy(v_h, v_ref, sems.at[0])
    load.start()
    copy = pltpu.make_async_copy(send_h, send_s, sems.at[1])
    copy.start()
    column_operator(nbr_ref, nw_ref, sw_ref, a_ref, merged)
    copy.wait()
    parity = lax.bitwise_and(lax.axis_index(blk), jnp.int32(1))
    pitch = cols + 8
    rows_of = lambda s, lo, n: cf[pl.ds(lo * pitch + s, n, stride=pitch), :]
    for lo in range(0, levels + 1, 16):
        pack_chunk(parity, lo, levels, send_s, wts_ref, tbl_ref, rows_of, (2,), (s2,))
    level_products(a_ref, lambda l: c_ref[l], exs, rows)
    level = lax.broadcasted_iota(jnp.int32, (levels, cols), 0)
    wet = wet_ref[...]
    load.wait()
    vf[...] = jnp.zeros_like(vf)
    for m in range(levels):
        keep = jnp.maximum(level, m) < wet
        vf[m * rows : m * rows + levels, :] = jnp.where(keep, v_ref[m].astype(F32), 0.0)
    for l in range(rows):
        block = vf[pl.ds(l, rows, stride=rows), :]
        block = jnp.concatenate([block, jnp.zeros((128 - rows, cols), F32)], axis=0)
        vts[pl.ds(l, cols, stride=rows), :] = block.T
    vt_ref[...] = vts[...].reshape(cols, rows, 128).astype(BF16)
    vertical(vt_ref, exs, state_ref)


def send_kernel(blk, levels, r0, r1, r2, local_ref, vt_ref, wts_ref, tbl_ref, send_h, state, s0, s1, tbl_v, tbl_s, send_s, sems):
    copy = pltpu.make_async_copy(send_h, send_s, sems.at[1])
    copy.start()
    add_edges((r0, r1, r2), levels, send_h.shape[1], vt_ref, state, tbl_v, tbl_s, sems.at[0])
    copy.wait()
    pack_state(blk, levels, send_s, wts_ref, tbl_ref, state, vt_ref.shape[1], (0, 1), (s0, s1))


def pack_state(blk, levels, send, weights, tbl, state, rows, slots, outs):
    parity = lax.bitwise_and(lax.axis_index(blk), jnp.int32(1))
    rows_of = lambda s, lo, n: state[pl.ds(pl.multiple_of(s * rows + lo, 8), n), :]
    for lo in range(0, levels + 1, 16):
        pack_chunk(parity, lo, levels, send, weights, tbl, rows_of, slots, outs)


def middle_kernel(blk, levels, cs, a_ref, vt_ref, wts_ref, tbl_ref, send_h, out_ref, s2, exs, send_s, sem):
    copy = pltpu.make_async_copy(send_h, send_s, sem)
    copy.start()
    cols, rows, _ = vt_ref.shape
    level_products(a_ref, lambda l: cs[pl.ds(l, cols, stride=rows), :].astype(BF16), exs, rows)
    copy.wait()
    pack_state(blk, levels, send_s, wts_ref, tbl_ref, cs, rows, (2,), (s2,))
    vertical(vt_ref, exs, out_ref)


def last_kernel(nedge, r0, r1, r2, local_ref, vt_ref, out_h, total, out_v, tbl_v, tbl_s, sems):
    levels, cols, width = out_h.shape
    rows = vt_ref.shape[1]
    add_edges((r0, r1, r2), levels, nedge, vt_ref, total, tbl_v, tbl_s, sems.at[0])
    count = 5
    edges = [levels * i // count for i in range(count + 1)]
    copies = []
    for i, (lo, hi) in enumerate(zip(edges, edges[1:])):
        for l in range(lo, hi):
            out_v[l] = total[pl.ds(l, cols, stride=rows), :].astype(BF16)
        copies.append(pltpu.make_async_copy(out_v.at[pl.ds(lo, hi - lo)], out_h.at[pl.ds(lo, hi - lo)], sems.at[1 + i]))
        copies[-1].start()
    for copy in copies:
        copy.wait()


VM = pl.BlockSpec(memory_space=pltpu.VMEM)
HB = pl.BlockSpec(memory_space=pltpu.HBM)
DMA = pltpu.SemaphoreType.DMA


def call(kernel, ins, specs, outs, out_specs, scratch, limit, flops=0, aliases=None):
    size = sum(x.size * x.dtype.itemsize for x in (*ins, *outs))
    return pl.pallas_call(
        kernel,
        out_shape=outs,
        in_specs=specs,
        out_specs=out_specs,
        scratch_shapes=scratch,
        input_output_aliases=aliases or {},
        compiler_params=pltpu.CompilerParams(vmem_limit_bytes=limit * 2**20),
        cost_estimate=pl.CostEstimate(flops=flops, bytes_accessed=size, transcendentals=0),
    )(*ins)


def odd_or_even(value, first, blk, basin):
    n, b = lax.axis_size(blk), lax.axis_size(basin)
    partner = {i: i + 1 for i in range(first, n - 1, 2)}
    partner |= {j: i for i, j in partner.items()}
    across = lambda g: g ^ 1 if g ^ 1 < b else g
    route = [(g * n + i, g * n + partner[i] if i in partner else across(g) * n + i) for g in range(b) for i in range(n)]
    return lax.ppermute(value, (basin, blk), route)


def along_basin(value, basin):
    b = lax.axis_size(basin)
    return lax.ppermute(value, basin, [(i, (i + 1) % b) for i in range(b)])


def local(tracers, nbr_cols, nbr_wts, self_wts, send_cols, recv_cols, edge_wts, wet_levels, vert_inv):
    cols, levels, width = tracers.shape
    rows = padded(levels)
    nedge = send_cols.shape[1]
    shape = jax.ShapeDtypeStruct
    by_level = jnp.transpose(tracers, (1, 0, 2))
    nbr_by_level = jnp.transpose(nbr_wts, (1, 0, 2))
    edge_by_entry = jnp.transpose(edge_wts, (0, 2, 1))
    wet = wet_levels.reshape(1, cols)
    in_hbm = lambda x: pltpu.with_memory_space_constraint(x, pltpu.HBM)
    send_h = in_hbm(send_cols)
    loads = [by_level, nbr_cols, nbr_by_level, self_wts, wet]
    same = lambda x: shape(x.shape, x.dtype)
    message = shape((message_rows(levels, nedge), width), BF16)
    columns = shape((cols * rows, width), F32)
    flat = pltpu.VMEM(columns.shape, F32)
    send_table = pltpu.SMEM(send_cols.shape, jnp.int32)

    first = call(
        functools.partial(gather_kernel, "blk"),
        (in_hbm(by_level), send_h, *map(in_hbm, (recv_cols, edge_by_entry, *loads[1:]))),
        [HB] * 8,
        [message] * 2 + [same(x) for x in loads]
        + [shape((128, 128), F32), shape((8, 128), F32), shape((rows * (cols + 8), width), F32)],
        [VM] * 10,
        [
            pltpu.VMEM((128, 128), F32), pltpu.VMEM(recv_cols.shape, jnp.int32), pltpu.VMEM(edge_by_entry.shape, F32),
            send_table, DMA((7 + -(-levels // 16),)),
        ],
        16,
    )
    (to_next, to_odd), (state, nbr, nbr_w, self_w, wet), (wts, tbl, by_row) = first[:2], first[2:7], first[7:]
    operator_flops = 2 * levels * cols * cols * width
    vertical_flops = 2 * cols * rows * rows * width

    edge_flops = 3 * nedge * 2 * rows * rows * width
    tables = [pltpu.VMEM((3, 8, 128), jnp.int32), pltpu.SMEM((3, 8, 128), jnp.int32)]

    along = along_basin(to_next, "basin")
    odd = odd_or_even(to_odd, 1, "blk", "basin")
    operator, partial, vt, to_even = call(
        functools.partial(operator_kernel, "blk"),
        (state, nbr, nbr_w, self_w, wet, by_row, wts, tbl, send_h, in_hbm(vert_inv)), [VM] * 8 + [HB] * 2,
        [shape((levels // 2, cols, 2 * cols), BF16), columns, shape((cols, rows, 128), BF16), message], [VM] * 4,
        [flat, pltpu.VMEM((levels, 8, cols), F32), pltpu.VMEM((rows * rows, cols), F32), pltpu.VMEM((cols * rows, 128), F32),
         pltpu.VMEM(vert_inv.shape, BF16), send_table, DMA((2,))],
        32, flops=operator_flops + vertical_flops,
    )
    even = odd_or_even(to_even, 0, "blk", "basin")
    state, to_next, to_odd = call(
        functools.partial(send_kernel, "blk", levels),
        (along, odd, even, partial, vt, wts, tbl, send_h), [VM] * 7 + [HB],
        [columns] + [message] * 2, [VM] * 3,
        tables + [send_table, DMA((2,))], 16, flops=edge_flops, aliases={3: 0},
    )
    along = along_basin(to_next, "basin")
    odd = odd_or_even(to_odd, 1, "blk", "basin")
    partial, to_even = call(
        functools.partial(middle_kernel, "blk", levels), (state, operator, vt, wts, tbl, send_h), [VM] * 5 + [HB],
        [columns, message], [VM] * 2, [flat, send_table, DMA], 32, flops=operator_flops + vertical_flops,
    )
    even = odd_or_even(to_even, 0, "blk", "basin")
    out, _ = call(
        functools.partial(last_kernel, nedge), (along, odd, even, partial, vt), [VM] * 5,
        [shape((levels, cols, width), BF16), columns], [HB, VM],
        [pltpu.VMEM((levels, cols, width), BF16)] + tables + [DMA((6,))], 16, flops=edge_flops, aliases={3: 1},
    )
    return jnp.transpose(out, (1, 0, 2))


def solution(mesh):
    in_specs = (
        P(("basin", "blk"), None, None),
        P(None, ("basin", "blk")),
        P(None, None, ("basin", "blk")),
        P(None, ("basin", "blk")),
        P(None, ("basin", "blk")),
        P(None, ("basin", "blk")),
        P(None, None, ("basin", "blk")),
        P(("basin", "blk")),
        P(None, None, ("basin", "blk")),
    )
    out_specs = P(("basin", "blk"), None, None)
    return jax.shard_map(local, mesh=mesh, in_specs=in_specs, out_specs=out_specs, check_vma=False)
```

```python
import functools

import jax
import jax.numpy as jnp
from jax import lax
from jax.experimental import pallas as pl
from jax.experimental.pallas import tpu as pltpu
from jax.sharding import PartitionSpec as P

NSTEP = 2
F32 = jnp.float32
BF16 = jnp.bfloat16


def padded(levels):
    return -(-levels // 8) * 8


def whole_rows(levels):
    return levels // 16 * 16


def message_rows(levels, nedge):
    return levels * nedge + 16


def direction(slot, parity):
    return lax.bitwise_xor(parity, jnp.int32(2 - slot)) if slot else 2


def has_partner(slot, at, count):
    first = lax.bitwise_and(at + slot // 2, jnp.int32(1)) == 1
    return jnp.where(first, at + 1 < count, at > 0)


def pack_chunk(parity, lo, levels, send, weights, tbl, rows_of, slots, outs):
    whole = whole_rows(levels)
    nedge = send.shape[1]
    rest = levels - whole
    share = 8 // rest if rest else 0
    for slot, out in zip(slots, outs):
        d = direction(slot, parity)
        if lo < whole:
            for e in range(nedge):
                k = slot * nedge + e
                value = rows_of(send[d, e], lo, 16) * weights[lo : lo + 16, k : k + 1]
                out[e * whole + lo : e * whole + lo + 16, :] = value.astype(BF16)
            continue
        sub = lax.broadcasted_iota(jnp.int32, (8, out.shape[1]), 0)
        parts = []
        for first in range(0, nedge, share or nedge):
            part = None
            for q in range(share):
                k = slot * nedge + first + q
                value = rows_of(send[d, first + q], lo, 8) * weights[lo : lo + 8, k : k + 1]
                if q:
                    value = pltpu.roll(value, q * rest, 0)
                part = value if part is None else jnp.where(sub >= q * rest, value, part)
            if share:
                parts.append(part)
        table = jnp.broadcast_to(tbl[slot : slot + 1, :], (16, out.shape[1]))
        out[nedge * whole :, :] = jnp.concatenate(parts + [table], axis=0).astype(BF16)


def vertical(vt_ref, exs, out):
    cols, rows, _ = vt_ref.shape
    pad = jnp.zeros((64 - rows, out.shape[1]), F32)

    def column(j, _):
        at = pl.ds(pl.multiple_of(j * rows, 8), rows)
        x = jnp.concatenate([exs[at, :], pad], axis=0).astype(BF16)
        out[at, :] = jnp.dot(vt_ref[j][:, 0:64], x, preferred_element_type=F32)
        return _

    lax.fori_loop(0, cols, column, 0, unroll=16)


def add_edges(edges, levels, nedge, vt_ref, total, tbl_v, tbl_s, sem):
    whole = whole_rows(levels)
    rest = levels - whole
    share = 8 // rest if rest else 0
    rows = vt_ref.shape[1]
    for i, ref in enumerate(edges):
        tbl_v[i] = ref[levels * nedge :, :].astype(F32)[0:8].astype(jnp.int32)
    copy = pltpu.make_async_copy(tbl_v, tbl_s, sem)
    copy.start()
    copy.wait()
    group = max(share, 4)
    pad = jnp.zeros((8, total.shape[1]), F32)
    for i, ref in enumerate(edges):
        tails = ref[whole * nedge : levels * nedge, :].astype(F32) if rest else None
        for first in range(0, nedge, group):
            targets = [tbl_s[i, 0, e] for e in range(first, first + group)]
            products = []
            for e, j in zip(range(first, first + group), targets):
                x = ref[e * whole : (e + 1) * whole, :]
                if rest:
                    tail = tails[e // share * 8 : e // share * 8 + 8]
                    if e % share:
                        tail = pltpu.roll(tail, 8 - e % share * rest, 0)
                    x = jnp.concatenate([x, jnp.concatenate([tail, pad], axis=0).astype(BF16)], axis=0)
                products.append(jnp.dot(vt_ref[j][:, 0 : x.shape[0]], x, preferred_element_type=F32))
            for j, part in zip(targets, products):
                at = pl.ds(pl.multiple_of(j * rows, 8), rows)
                total[at, :] = total[at, :] + part


def gather_kernel(
    blk, c_h, send_h, recv_h, edge_h, nbr_h, nw_h, sw_h, wet_h,
    s0, s1, s2, c_v, nbr_v, nw_v, sw_v, wet_v, wts_o, tbl_o,
    cf, wts, recv_v, edge_v, send_s, sems,
):
    levels, cols, width = c_h.shape
    nedge = edge_h.shape[1]
    pitch = cols + 8
    bounds = [(lo, min(lo + 16, levels)) for lo in range(0, levels, 16)]
    pairs = [(send_h, send_s), (recv_h, recv_v), (edge_h, edge_v)]
    pairs += [(c_h.at[pl.ds(lo, hi - lo)], c_v.at[pl.ds(lo, hi - lo)]) for lo, hi in bounds]
    pairs += [(nbr_h, nbr_v), (nw_h, nw_v), (sw_h, sw_v), (wet_h, wet_v)]
    copies = [pltpu.make_async_copy(a, b, sems.at[i]) for i, (a, b) in enumerate(pairs)]
    for copy in copies:
        copy.start()
    parity = lax.bitwise_and(lax.axis_index(blk), jnp.int32(1))
    wts[...] = jnp.zeros_like(wts)
    tbl_o[...] = jnp.zeros_like(tbl_o)
    for copy in copies[:3]:
        copy.wait()
    for slot in range(3):
        d = direction(slot, parity)
        weight = edge_v[d]
        if slot:
            weight = jnp.where(has_partner(slot, lax.axis_index(blk), lax.axis_size(blk)), weight, 0.0)
        wts[slot * nedge : (slot + 1) * nedge, 0:levels] = weight
        tbl_o[slot : slot + 1, 0:nedge] = recv_v[pl.ds(d, 1), :].astype(F32)
    weights = wts[...].T
    wts_o[...] = weights
    rows_of = lambda s, lo, n: cf[pl.ds(lo * pitch + s, n, stride=pitch), :]
    for i, (lo, hi) in enumerate(bounds):
        copies[3 + i].wait()
        for l in range(lo, hi):
            cf[l * pitch : l * pitch + cols, :] = c_v[l].astype(F32)
        pack_chunk(parity, lo, levels, send_s, weights, tbl_o, rows_of, (0, 1, 2), (s0, s1, s2))
    if levels % 16 == 0:
        pack_chunk(parity, levels, levels, send_s, weights, tbl_o, rows_of, (0, 1, 2), (s0, s1, s2))
    for copy in copies[3 + len(bounds) :]:
        copy.wait()


def column_operator(nbr_ref, nw_ref, sw_ref, a_ref, merged):
    levels = nw_ref.shape[0]
    cols = nbr_ref.shape[1]
    nbr = nbr_ref.shape[0]
    lane = lax.broadcasted_iota(jnp.int32, (8, cols), 1)
    sub = lax.broadcasted_iota(jnp.int32, (8, cols), 0)
    target = jnp.where(sub == nbr, lane, -1)
    for n in range(nbr):
        target = jnp.where(sub == n, nbr_ref[n : n + 1, :], target)
    same = [(target == nbr_ref[n : n + 1, :]).astype(F32) for n in range(nbr)]
    same.append((target == lane).astype(F32))
    for l in range(levels):
        total = same[nbr] * sw_ref[l : l + 1, :]
        for n in range(nbr):
            total = total + same[n] * nw_ref[l, n : n + 1, :]
        merged[l] = total
    half = 16
    for jt in range(cols // half):
        j = lax.broadcasted_iota(jnp.int32, (half, cols), 0) + jt * half
        hits = [j == nbr_ref[n : n + 1, :] for n in range(nbr)]
        hits.append(j == lax.broadcasted_iota(jnp.int32, (half, cols), 1))

        def fill(p, _):
            for i in range(2):
                value = jnp.zeros((half, cols), F32)
                for n in range(nbr, -1, -1):
                    value = jnp.where(hits[n], merged[p * 2 + i, n : n + 1, :], value)
                a_ref[p, jt * half : (jt + 1) * half, i * cols : (i + 1) * cols] = value.astype(BF16)
            return _

        lax.fori_loop(0, levels // 2, fill, 0, unroll=5)


def level_products(a_ref, state_of, exs, rows):
    pairs, cols, _ = a_ref.shape
    width = exs.shape[1]
    zero = jnp.zeros((cols, width), BF16)
    for p in range(pairs):
        left = jnp.concatenate([state_of(2 * p), zero], axis=1)
        right = jnp.concatenate([zero, state_of(2 * p + 1)], axis=1)
        both = jnp.dot(a_ref[p], jnp.concatenate([left, right], axis=0), preferred_element_type=F32)
        exs[pl.ds(2 * p, cols, stride=rows), :] = both[:, 0:width]
        exs[pl.ds(2 * p + 1, cols, stride=rows), :] = both[:, width:]
    for l in range(2 * pairs, rows):
        exs[pl.ds(l, cols, stride=rows), :] = jnp.zeros((cols, width), F32)


def operator_kernel(
    c_ref, nbr_ref, nw_ref, sw_ref, wet_ref, v_h, a_ref, state_ref, vt_ref, exs, merged, vf, vts, v_ref, sem
):
    levels, cols, width = c_ref.shape
    rows = padded(levels)
    load = pltpu.make_async_copy(v_h, v_ref, sem)
    load.start()
    column_operator(nbr_ref, nw_ref, sw_ref, a_ref, merged)
    level_products(a_ref, lambda l: c_ref[l], exs, rows)
    level = lax.broadcasted_iota(jnp.int32, (levels, cols), 0)
    wet = wet_ref[...]
    load.wait()
    vf[...] = jnp.zeros_like(vf)
    for m in range(levels):
        keep = jnp.maximum(level, m) < wet
        vf[m * rows : m * rows + levels, :] = jnp.where(keep, v_ref[m].astype(F32), 0.0)
    for l in range(rows):
        block = vf[pl.ds(l, rows, stride=rows), :]
        block = jnp.concatenate([block, jnp.zeros((128 - rows, cols), F32)], axis=0)
        vts[pl.ds(l, cols, stride=rows), :] = block.T
    vt_ref[...] = vts[...].reshape(cols, rows, 128).astype(BF16)
    vertical(vt_ref, exs, state_ref)


def send_kernel(blk, levels, r0, r1, r2, local_ref, vt_ref, wts_ref, tbl_ref, send_h, state, s0, s1, tbl_v, tbl_s, send_s, sems):
    copy = pltpu.make_async_copy(send_h, send_s, sems.at[1])
    copy.start()
    add_edges((r0, r1, r2), levels, send_h.shape[1], vt_ref, state, tbl_v, tbl_s, sems.at[0])
    copy.wait()
    pack_state(blk, levels, send_s, wts_ref, tbl_ref, state, vt_ref.shape[1], (0, 1), (s0, s1))


def pack_state(blk, levels, send, weights, tbl, state, rows, slots, outs):
    parity = lax.bitwise_and(lax.axis_index(blk), jnp.int32(1))
    rows_of = lambda s, lo, n: state[pl.ds(pl.multiple_of(s * rows + lo, 8), n), :]
    for lo in range(0, levels + 1, 16):
        pack_chunk(parity, lo, levels, send, weights, tbl, rows_of, slots, outs)


def middle_kernel(blk, levels, cs, a_ref, vt_ref, wts_ref, tbl_ref, send_h, out_ref, s2, exs, send_s, sem):
    copy = pltpu.make_async_copy(send_h, send_s, sem)
    copy.start()
    cols, rows, _ = vt_ref.shape
    level_products(a_ref, lambda l: cs[pl.ds(l, cols, stride=rows), :].astype(BF16), exs, rows)
    copy.wait()
    pack_state(blk, levels, send_s, wts_ref, tbl_ref, cs, rows, (2,), (s2,))
    vertical(vt_ref, exs, out_ref)


def last_kernel(nedge, r0, r1, r2, local_ref, vt_ref, out_h, total, out_v, tbl_v, tbl_s, sems):
    levels, cols, width = out_h.shape
    rows = vt_ref.shape[1]
    add_edges((r0, r1, r2), levels, nedge, vt_ref, total, tbl_v, tbl_s, sems.at[0])
    bounds = [0, *range(4, levels, 8), levels]
    copies = []
    for i, (lo, hi) in enumerate(zip(bounds, bounds[1:])):
        for l in range(lo, hi):
            out_v[l] = total[pl.ds(l, cols, stride=rows), :].astype(BF16)
        copies.append(pltpu.make_async_copy(out_v.at[pl.ds(lo, hi - lo)], out_h.at[pl.ds(lo, hi - lo)], sems.at[1 + i]))
        copies[-1].start()
    for copy in copies:
        copy.wait()


VM = pl.BlockSpec(memory_space=pltpu.VMEM)
HB = pl.BlockSpec(memory_space=pltpu.HBM)
DMA = pltpu.SemaphoreType.DMA


def call(kernel, ins, specs, outs, out_specs, scratch, limit, flops=0, aliases=None):
    size = sum(x.size * x.dtype.itemsize for x in (*ins, *outs))
    return pl.pallas_call(
        kernel,
        out_shape=outs,
        in_specs=specs,
        out_specs=out_specs,
        scratch_shapes=scratch,
        input_output_aliases=aliases or {},
        compiler_params=pltpu.CompilerParams(vmem_limit_bytes=limit * 2**20),
        cost_estimate=pl.CostEstimate(flops=flops, bytes_accessed=size, transcendentals=0),
    )(*ins)


def odd_or_even(value, first, blk):
    n = lax.axis_size(blk)
    order = [(i + first) % n for i in range(n)]
    partner = {order[i]: order[i + 1] for i in range(0, n - 1, 2)}
    partner |= {j: i for i, j in partner.items()}
    return lax.ppermute(value, blk, [(i, partner.get(i, i)) for i in range(n)])


def along_basin(value, basin):
    b = lax.axis_size(basin)
    return lax.ppermute(value, basin, [(i, (i + 1) % b) for i in range(b)])


def local(tracers, nbr_cols, nbr_wts, self_wts, send_cols, recv_cols, edge_wts, wet_levels, vert_inv):
    cols, levels, width = tracers.shape
    rows = padded(levels)
    nedge = send_cols.shape[1]
    shape = jax.ShapeDtypeStruct
    by_level = jnp.transpose(tracers, (1, 0, 2))
    nbr_by_level = jnp.transpose(nbr_wts, (1, 0, 2))
    edge_by_entry = jnp.transpose(edge_wts, (0, 2, 1))
    wet = wet_levels.reshape(1, cols)
    in_hbm = lambda x: pltpu.with_memory_space_constraint(x, pltpu.HBM)
    send_h = in_hbm(send_cols)
    loads = [by_level, nbr_cols, nbr_by_level, self_wts, wet]
    same = lambda x: shape(x.shape, x.dtype)
    message = shape((message_rows(levels, nedge), width), BF16)
    columns = shape((cols * rows, width), F32)
    flat = pltpu.VMEM(columns.shape, F32)
    send_table = pltpu.SMEM(send_cols.shape, jnp.int32)

    first = call(
        functools.partial(gather_kernel, "blk"),
        (in_hbm(by_level), send_h, *map(in_hbm, (recv_cols, edge_by_entry, *loads[1:]))),
        [HB] * 8,
        [message] * 3 + [same(x) for x in loads] + [shape((128, 128), F32), shape((8, 128), F32)],
        [VM] * 10,
        [
            pltpu.VMEM((rows * (cols + 8), width), F32),
            pltpu.VMEM((128, 128), F32), pltpu.VMEM(recv_cols.shape, jnp.int32), pltpu.VMEM(edge_by_entry.shape, F32),
            send_table, DMA((7 + -(-levels // 16),)),
        ],
        16,
    )
    (to_next, to_odd, to_even), loads, (wts, tbl) = first[:3], first[3:8], first[8:]
    operator_flops = 2 * levels * cols * cols * width
    vertical_flops = 2 * cols * rows * rows * width

    edge_flops = 3 * nedge * 2 * rows * rows * width
    tables = [pltpu.VMEM((3, 8, 128), jnp.int32), pltpu.SMEM((3, 8, 128), jnp.int32)]

    along = along_basin(to_next, "basin")
    odd = odd_or_even(to_odd, 1, "blk")
    even = odd_or_even(to_even, 0, "blk")
    operator, partial, vt = call(
        operator_kernel, (*loads, in_hbm(vert_inv)), [VM] * 5 + [HB],
        [shape((levels // 2, cols, 2 * cols), BF16), columns, shape((cols, rows, 128), BF16)], [VM] * 3,
        [flat, pltpu.VMEM((levels, 8, cols), F32), pltpu.VMEM((rows * rows, cols), F32), pltpu.VMEM((cols * rows, 128), F32),
         pltpu.VMEM(vert_inv.shape, BF16), DMA],
        32, flops=operator_flops + vertical_flops,
    )
    state, to_next, to_odd = call(
        functools.partial(send_kernel, "blk", levels),
        (along, odd, even, partial, vt, wts, tbl, send_h), [VM] * 7 + [HB],
        [columns] + [message] * 2, [VM] * 3,
        tables + [send_table, DMA((2,))], 16, flops=edge_flops, aliases={3: 0},
    )
    along = along_basin(to_next, "basin")
    odd = odd_or_even(to_odd, 1, "blk")
    partial, to_even = call(
        functools.partial(middle_kernel, "blk", levels), (state, operator, vt, wts, tbl, send_h), [VM] * 5 + [HB],
        [columns, message], [VM] * 2, [flat, send_table, DMA], 32, flops=operator_flops + vertical_flops,
    )
    even = odd_or_even(to_even, 0, "blk")
    out, _ = call(
        functools.partial(last_kernel, nedge), (along, odd, even, partial, vt), [VM] * 5,
        [shape((levels, cols, width), BF16), columns], [HB, VM],
        [pltpu.VMEM((levels, cols, width), BF16)] + tables + [DMA((2 + -(-levels // 8),))], 16, flops=edge_flops, aliases={3: 1},
    )
    return jnp.transpose(out, (1, 0, 2))


def solution(mesh):
    in_specs = (
        P(("basin", "blk"), None, None),
        P(None, ("basin", "blk")),
        P(None, None, ("basin", "blk")),
        P(None, ("basin", "blk")),
        P(None, ("basin", "blk")),
        P(None, ("basin", "blk")),
        P(None, None, ("basin", "blk")),
        P(("basin", "blk")),
        P(None, None, ("basin", "blk")),
    )
    out_specs = P(("basin", "blk"), None, None)
    return jax.shard_map(local, mesh=mesh, in_specs=in_specs, out_specs=out_specs, check_vma=False)
```

```python
import functools

import jax
import jax.numpy as jnp
from jax import lax
from jax.experimental import pallas as pl
from jax.experimental.pallas import tpu as pltpu
from jax.sharding import PartitionSpec as P

NSTEP = 2
F32 = jnp.float32
BF16 = jnp.bfloat16


def padded(levels):
    return -(-levels // 8) * 8


def whole_rows(levels):
    return levels // 16 * 16


def message_rows(levels, nedge):
    return levels * nedge + 16


def direction(slot, parity):
    return lax.bitwise_xor(parity, jnp.int32(2 - slot)) if slot else 2


def has_partner(slot, at, count):
    first = lax.bitwise_and(at + slot // 2, jnp.int32(1)) == 1
    return jnp.where(first, at + 1 < count, at > 0)


def pack_chunk(parity, lo, levels, send, weights, rows_of, slots, outs):
    whole = whole_rows(levels)
    nedge = send.shape[1]
    rest = levels - whole
    share = 8 // rest if rest else 0
    for slot, out in zip(slots, outs):
        d = direction(slot, parity)
        if lo < whole:
            for e in range(nedge):
                k = slot * nedge + e
                value = rows_of(send[d, e], lo, 16) * weights[lo : lo + 16, k : k + 1]
                out[e * whole + lo : e * whole + lo + 16, :] = value.astype(BF16)
            continue
        sub = lax.broadcasted_iota(jnp.int32, (8, out.shape[1]), 0)
        parts = []
        for first in range(0, nedge, share or nedge):
            part = None
            for q in range(share):
                k = slot * nedge + first + q
                value = rows_of(send[d, first + q], lo, 8) * weights[lo : lo + 8, k : k + 1]
                if q:
                    value = pltpu.roll(value, q * rest, 0)
                part = value if part is None else jnp.where(sub >= q * rest, value, part)
            if share:
                parts.append(part)
        table = jnp.broadcast_to(weights[0:16, 3 * nedge + slot : 3 * nedge + slot + 1], (16, out.shape[1]))
        out[nedge * whole :, :] = jnp.concatenate(parts + [table], axis=0).astype(BF16)


def vertical(vt_ref, exs, out):
    cols, rows, _ = vt_ref.shape
    pad = jnp.zeros((64 - rows, out.shape[1]), F32)

    def column(j, _):
        at = pl.ds(pl.multiple_of(j * rows, 8), rows)
        x = jnp.concatenate([exs[at, :], pad], axis=0).astype(BF16)
        out[at, :] = jnp.dot(vt_ref[j][:, 0:64], x, preferred_element_type=F32)
        return _

    lax.fori_loop(0, cols, column, 0, unroll=16)


def add_edges(edges, levels, nedge, vt_ref, total):
    whole = whole_rows(levels)
    rest = levels - whole
    share = 8 // rest if rest else 0
    rows = vt_ref.shape[1]
    group = max(share, 4)
    pad = jnp.zeros((8, total.shape[1]), F32)
    for ref in edges:
        table = ref[levels * nedge :, :].astype(F32).astype(jnp.int32)
        tails = ref[whole * nedge : levels * nedge, :].astype(F32) if rest else None
        for first in range(0, nedge, group):
            targets = [table[e, 0] for e in range(first, first + group)]
            products = []
            for e, j in zip(range(first, first + group), targets):
                x = ref[e * whole : (e + 1) * whole, :]
                if rest:
                    tail = tails[e // share * 8 : e // share * 8 + 8]
                    if e % share:
                        tail = pltpu.roll(tail, 8 - e % share * rest, 0)
                    x = jnp.concatenate([x, jnp.concatenate([tail, pad], axis=0).astype(BF16)], axis=0)
                products.append(jnp.dot(vt_ref[j][:, 0 : x.shape[0]], x, preferred_element_type=F32))
            for j, part in zip(targets, products):
                at = pl.ds(pl.multiple_of(j * rows, 8), rows)
                total[at, :] = total[at, :] + part


def gather_kernel(
    blk, c_h, send_h, recv_h, edge_h, nbr_h, nw_h, sw_h, wet_h,
    s0, s1, s2, c_v, nbr_v, nw_v, sw_v, wet_v, wts_o,
    cf, wts, recv_v, edge_v, send_s, sems,
):
    levels, cols, width = c_h.shape
    nedge = edge_h.shape[1]
    pitch = cols + 8
    bounds = [(lo, min(lo + 16, levels)) for lo in range(0, levels, 16)]
    pairs = [(send_h, send_s), (recv_h, recv_v), (edge_h, edge_v)]
    pairs += [(c_h.at[pl.ds(lo, hi - lo)], c_v.at[pl.ds(lo, hi - lo)]) for lo, hi in bounds]
    pairs += [(nbr_h, nbr_v), (nw_h, nw_v), (sw_h, sw_v), (wet_h, wet_v)]
    copies = [pltpu.make_async_copy(a, b, sems.at[i]) for i, (a, b) in enumerate(pairs)]
    for copy in copies:
        copy.start()
    parity = lax.bitwise_and(lax.axis_index(blk), jnp.int32(1))
    wts[...] = jnp.zeros_like(wts)
    for copy in copies[:3]:
        copy.wait()
    for slot in range(3):
        d = direction(slot, parity)
        weight = edge_v[d]
        if slot:
            weight = jnp.where(has_partner(slot, lax.axis_index(blk), lax.axis_size(blk)), weight, 0.0)
        wts[slot * nedge : (slot + 1) * nedge, 0:levels] = weight
        wts[3 * nedge + slot : 3 * nedge + slot + 1, 0:nedge] = recv_v[pl.ds(d, 1), :].astype(F32)
    weights = wts[...].T
    wts_o[...] = weights
    rows_of = lambda s, lo, n: cf[pl.ds(lo * pitch + s, n, stride=pitch), :]
    for i, (lo, hi) in enumerate(bounds):
        copies[3 + i].wait()
        for l in range(lo, hi):
            cf[l * pitch : l * pitch + cols, :] = c_v[l].astype(F32)
        pack_chunk(parity, lo, levels, send_s, weights, rows_of, (0, 1, 2), (s0, s1, s2))
    if levels % 16 == 0:
        pack_chunk(parity, levels, levels, send_s, weights, rows_of, (0, 1, 2), (s0, s1, s2))
    for copy in copies[3 + len(bounds) :]:
        copy.wait()


def column_operator(nbr_ref, nw_ref, sw_ref, a_ref, merged):
    levels = nw_ref.shape[0]
    cols = nbr_ref.shape[1]
    nbr = nbr_ref.shape[0]
    lane = lax.broadcasted_iota(jnp.int32, (8, cols), 1)
    sub = lax.broadcasted_iota(jnp.int32, (8, cols), 0)
    target = jnp.where(sub == nbr, lane, -1)
    for n in range(nbr):
        target = jnp.where(sub == n, nbr_ref[n : n + 1, :], target)
    same = [(target == nbr_ref[n : n + 1, :]).astype(F32) for n in range(nbr)]
    same.append((target == lane).astype(F32))
    for l in range(levels):
        total = same[nbr] * sw_ref[l : l + 1, :]
        for n in range(nbr):
            total = total + same[n] * nw_ref[l, n : n + 1, :]
        merged[l] = total
    half = 16
    for jt in range(cols // half):
        j = lax.broadcasted_iota(jnp.int32, (half, cols), 0) + jt * half
        hits = [j == nbr_ref[n : n + 1, :] for n in range(nbr)]
        hits.append(j == lax.broadcasted_iota(jnp.int32, (half, cols), 1))

        def fill(p, _):
            for i in range(2):
                value = jnp.zeros((half, cols), F32)
                for n in range(nbr, -1, -1):
                    value = jnp.where(hits[n], merged[p * 2 + i, n : n + 1, :], value)
                a_ref[p, jt * half : (jt + 1) * half, i * cols : (i + 1) * cols] = value.astype(BF16)
            return _

        lax.fori_loop(0, levels // 2, fill, 0, unroll=5)


def level_products(a_ref, state_of, exs, rows):
    pairs, cols, _ = a_ref.shape
    width = exs.shape[1]
    zero = jnp.zeros((cols, width), BF16)
    for p in range(pairs):
        left = jnp.concatenate([state_of(2 * p), zero], axis=1)
        right = jnp.concatenate([zero, state_of(2 * p + 1)], axis=1)
        both = jnp.dot(a_ref[p], jnp.concatenate([left, right], axis=0), preferred_element_type=F32)
        exs[pl.ds(2 * p, cols, stride=rows), :] = both[:, 0:width]
        exs[pl.ds(2 * p + 1, cols, stride=rows), :] = both[:, width:]
    for l in range(2 * pairs, rows):
        exs[pl.ds(l, cols, stride=rows), :] = jnp.zeros((cols, width), F32)


def operator_kernel(
    c_ref, nbr_ref, nw_ref, sw_ref, wet_ref, v_h, a_ref, state_ref, vt_ref, exs, merged, vf, vts, v_ref, sem
):
    levels, cols, width = c_ref.shape
    rows = padded(levels)
    load = pltpu.make_async_copy(v_h, v_ref, sem)
    load.start()
    column_operator(nbr_ref, nw_ref, sw_ref, a_ref, merged)
    level_products(a_ref, lambda l: c_ref[l], exs, rows)
    level = lax.broadcasted_iota(jnp.int32, (levels, cols), 0)
    wet = wet_ref[...]
    load.wait()
    vf[...] = jnp.zeros_like(vf)
    for m in range(levels):
        keep = jnp.maximum(level, m) < wet
        vf[m * rows : m * rows + levels, :] = jnp.where(keep, v_ref[m].astype(F32), 0.0)
    for l in range(rows):
        block = vf[pl.ds(l, rows, stride=rows), :]
        block = jnp.concatenate([block, jnp.zeros((128 - rows, cols), F32)], axis=0)
        vts[pl.ds(l, cols, stride=rows), :] = block.T
    vt_ref[...] = vts[...].reshape(cols, rows, 128).astype(BF16)
    vertical(vt_ref, exs, state_ref)


def send_kernel(blk, levels, r0, r1, r2, local_ref, vt_ref, wts_ref, send_h, state, s0, s1, send_s, sem):
    copy = pltpu.make_async_copy(send_h, send_s, sem)
    copy.start()
    add_edges((r0, r1, r2), levels, send_h.shape[1], vt_ref, state)
    copy.wait()
    pack_state(blk, levels, send_s, wts_ref, state, vt_ref.shape[1], (0, 1), (s0, s1))


def pack_state(blk, levels, send, weights, state, rows, slots, outs):
    parity = lax.bitwise_and(lax.axis_index(blk), jnp.int32(1))
    rows_of = lambda s, lo, n: state[pl.ds(pl.multiple_of(s * rows + lo, 8), n), :]
    for lo in range(0, levels + 1, 16):
        pack_chunk(parity, lo, levels, send, weights, rows_of, slots, outs)


def middle_kernel(blk, levels, cs, a_ref, vt_ref, wts_ref, send_h, out_ref, s2, exs, send_s, sem):
    copy = pltpu.make_async_copy(send_h, send_s, sem)
    copy.start()
    cols, rows, _ = vt_ref.shape
    level_products(a_ref, lambda l: cs[pl.ds(l, cols, stride=rows), :].astype(BF16), exs, rows)
    copy.wait()
    pack_state(blk, levels, send_s, wts_ref, cs, rows, (2,), (s2,))
    vertical(vt_ref, exs, out_ref)


def last_kernel(nedge, r0, r1, r2, local_ref, vt_ref, out_h, total, out_v, sems):
    levels, cols, width = out_h.shape
    rows = vt_ref.shape[1]
    add_edges((r0, r1, r2), levels, nedge, vt_ref, total)
    bounds = [0, *range(4, levels, 8), levels]
    copies = []
    for i, (lo, hi) in enumerate(zip(bounds, bounds[1:])):
        for l in range(lo, hi):
            out_v[l] = total[pl.ds(l, cols, stride=rows), :].astype(BF16)
        copies.append(pltpu.make_async_copy(out_v.at[pl.ds(lo, hi - lo)], out_h.at[pl.ds(lo, hi - lo)], sems.at[i]))
        copies[-1].start()
    for copy in copies:
        copy.wait()


VM = pl.BlockSpec(memory_space=pltpu.VMEM)
HB = pl.BlockSpec(memory_space=pltpu.HBM)
DMA = pltpu.SemaphoreType.DMA


def call(kernel, ins, specs, outs, out_specs, scratch, limit, flops=0, aliases=None):
    size = sum(x.size * x.dtype.itemsize for x in (*ins, *outs))
    return pl.pallas_call(
        kernel,
        out_shape=outs,
        in_specs=specs,
        out_specs=out_specs,
        scratch_shapes=scratch,
        input_output_aliases=aliases or {},
        compiler_params=pltpu.CompilerParams(vmem_limit_bytes=limit * 2**20),
        cost_estimate=pl.CostEstimate(flops=flops, bytes_accessed=size, transcendentals=0),
    )(*ins)


def odd_or_even(value, first, blk, basin):
    n, b = lax.axis_size(blk), lax.axis_size(basin)
    partner = {i: i + 1 for i in range(first, n - 1, 2)}
    partner |= {j: i for i, j in partner.items()}
    across = lambda g: g ^ 1 if g ^ 1 < b else g
    route = [(g * n + i, g * n + partner[i] if i in partner else across(g) * n + i) for g in range(b) for i in range(n)]
    return lax.ppermute(value, (basin, blk), route)


def along_basin(value, basin):
    b = lax.axis_size(basin)
    return lax.ppermute(value, basin, [(i, (i + 1) % b) for i in range(b)])


def local(tracers, nbr_cols, nbr_wts, self_wts, send_cols, recv_cols, edge_wts, wet_levels, vert_inv):
    cols, levels, width = tracers.shape
    rows = padded(levels)
    nedge = send_cols.shape[1]
    shape = jax.ShapeDtypeStruct
    by_level = jnp.transpose(tracers, (1, 0, 2))
    nbr_by_level = jnp.transpose(nbr_wts, (1, 0, 2))
    edge_by_entry = jnp.transpose(edge_wts, (0, 2, 1))
    wet = wet_levels.reshape(1, cols)
    in_hbm = lambda x: pltpu.with_memory_space_constraint(x, pltpu.HBM)
    send_h = in_hbm(send_cols)
    loads = [by_level, nbr_cols, nbr_by_level, self_wts, wet]
    same = lambda x: shape(x.shape, x.dtype)
    message = shape((message_rows(levels, nedge), width), BF16)
    columns = shape((cols * rows, width), F32)
    flat = pltpu.VMEM(columns.shape, F32)
    send_table = pltpu.SMEM(send_cols.shape, jnp.int32)

    first = call(
        functools.partial(gather_kernel, "blk"),
        (in_hbm(by_level), send_h, *map(in_hbm, (recv_cols, edge_by_entry, *loads[1:]))),
        [HB] * 8,
        [message] * 3 + [same(x) for x in loads] + [shape((128, 128), F32)],
        [VM] * 9,
        [
            pltpu.VMEM((rows * (cols + 8), width), F32),
            pltpu.VMEM((128, 128), F32), pltpu.VMEM(recv_cols.shape, jnp.int32), pltpu.VMEM(edge_by_entry.shape, F32),
            send_table, DMA((7 + -(-levels // 16),)),
        ],
        16,
    )
    (to_next, to_odd, to_even), loads, wts = first[:3], first[3:8], first[8]
    operator_flops = 2 * levels * cols * cols * width
    vertical_flops = 2 * cols * rows * rows * width

    edge_flops = 3 * nedge * 2 * rows * rows * width
    along = along_basin(to_next, "basin")
    odd = odd_or_even(to_odd, 1, "blk", "basin")
    even = odd_or_even(to_even, 0, "blk", "basin")
    operator, partial, vt = call(
        operator_kernel, (*loads, in_hbm(vert_inv)), [VM] * 5 + [HB],
        [shape((levels // 2, cols, 2 * cols), BF16), columns, shape((cols, rows, 128), BF16)], [VM] * 3,
        [flat, pltpu.VMEM((levels, 8, cols), F32), pltpu.VMEM((rows * rows, cols), F32), pltpu.VMEM((cols * rows, 128), F32),
         pltpu.VMEM(vert_inv.shape, BF16), DMA],
        32, flops=operator_flops + vertical_flops,
    )
    state, to_next, to_odd = call(
        functools.partial(send_kernel, "blk", levels),
        (along, odd, even, partial, vt, wts, send_h), [VM] * 6 + [HB],
        [columns] + [message] * 2, [VM] * 3,
        [send_table, DMA], 16, flops=edge_flops, aliases={3: 0},
    )
    along = along_basin(to_next, "basin")
    odd = odd_or_even(to_odd, 1, "blk", "basin")
    partial, to_even = call(
        functools.partial(middle_kernel, "blk", levels), (state, operator, vt, wts, send_h), [VM] * 4 + [HB],
        [columns, message], [VM] * 2, [flat, send_table, DMA], 32, flops=operator_flops + vertical_flops,
    )
    even = odd_or_even(to_even, 0, "blk", "basin")
    out, _ = call(
        functools.partial(last_kernel, nedge), (along, odd, even, partial, vt), [VM] * 5,
        [shape((levels, cols, width), BF16), columns], [HB, VM],
        [pltpu.VMEM((levels, cols, width), BF16), DMA((1 + -(-levels // 8),))], 16, flops=edge_flops, aliases={3: 1},
    )
    return jnp.transpose(out, (1, 0, 2))


def solution(mesh):
    in_specs = (
        P(("basin", "blk"), None, None),
        P(None, ("basin", "blk")),
        P(None, None, ("basin", "blk")),
        P(None, ("basin", "blk")),
        P(None, ("basin", "blk")),
        P(None, ("basin", "blk")),
        P(None, None, ("basin", "blk")),
        P(("basin", "blk")),
        P(None, None, ("basin", "blk")),
    )
    out_specs = P(("basin", "blk"), None, None)
    return jax.shard_map(local, mesh=mesh, in_specs=in_specs, out_specs=out_specs, check_vma=False)
```

```python
import functools

import jax
import jax.numpy as jnp
from jax import lax
from jax.experimental import pallas as pl
from jax.experimental.pallas import tpu as pltpu
from jax.sharding import PartitionSpec as P

NSTEP = 2
F32 = jnp.float32
BF16 = jnp.bfloat16


def padded(levels):
    return -(-levels // 8) * 8


def whole_rows(levels):
    return levels // 16 * 16


def message_rows(levels, nedge):
    return levels * nedge + 16


def direction(slot, parity):
    return lax.bitwise_xor(parity, jnp.int32(2 - slot)) if slot else 2


def has_partner(slot, at, count):
    first = lax.bitwise_and(at + slot // 2, jnp.int32(1)) == 1
    return jnp.where(first, at + 1 < count, at > 0)


def pack_chunk(lo, levels, nedge, weights, rows_of, slots, outs):
    whole = whole_rows(levels)
    rest = levels - whole
    share = 8 // rest if rest else 0
    for slot, out in zip(slots, outs):
        if lo < whole:
            for e in range(nedge):
                k = slot * nedge + e
                value = rows_of(slot, e, lo, 16) * weights[lo : lo + 16, k : k + 1]
                out[e * whole + lo : e * whole + lo + 16, :] = value.astype(BF16)
            continue
        sub = lax.broadcasted_iota(jnp.int32, (8, out.shape[1]), 0)
        parts = []
        for first in range(0, nedge, share or nedge):
            part = None
            for q in range(share):
                k = slot * nedge + first + q
                value = rows_of(slot, first + q, lo, 8) * weights[lo : lo + 8, k : k + 1]
                if q:
                    value = pltpu.roll(value, q * rest, 0)
                part = value if part is None else jnp.where(sub >= q * rest, value, part)
            if share:
                parts.append(part)
        table = jnp.broadcast_to(weights[0:16, 3 * nedge + slot : 3 * nedge + slot + 1], (16, out.shape[1]))
        out[nedge * whole :, :] = jnp.concatenate(parts + [table], axis=0).astype(BF16)


def vertical(vt_ref, exs, out):
    cols, rows, _ = vt_ref.shape
    pad = jnp.zeros((64 - rows, out.shape[1]), F32)

    def column(j, _):
        at = pl.ds(pl.multiple_of(j * rows, 8), rows)
        x = jnp.concatenate([exs[at, :], pad], axis=0).astype(BF16)
        out[at, :] = jnp.dot(vt_ref[j][:, 0:64], x, preferred_element_type=F32)
        return _

    lax.fori_loop(0, cols, column, 0, unroll=16)


def add_edges(edges, levels, nedge, vt_ref, total):
    whole = whole_rows(levels)
    rest = levels - whole
    share = 8 // rest if rest else 0
    rows = vt_ref.shape[1]
    group = max(share, 4)
    pad = jnp.zeros((8, total.shape[1]), F32)
    for ref in edges:
        table = ref[levels * nedge :, :].astype(F32).astype(jnp.int32)
        tails = ref[whole * nedge : levels * nedge, :].astype(F32) if rest else None
        for first in range(0, nedge, group):
            targets = [table[e, 0] for e in range(first, first + group)]
            products = []
            for e, j in zip(range(first, first + group), targets):
                x = ref[e * whole : (e + 1) * whole, :]
                if rest:
                    tail = tails[e // share * 8 : e // share * 8 + 8]
                    if e % share:
                        tail = pltpu.roll(tail, 8 - e % share * rest, 0)
                    x = jnp.concatenate([x, jnp.concatenate([tail, pad], axis=0).astype(BF16)], axis=0)
                products.append(jnp.dot(vt_ref[j][:, 0 : x.shape[0]], x, preferred_element_type=F32))
            for j, part in zip(targets, products):
                at = pl.ds(pl.multiple_of(j * rows, 8), rows)
                total[at, :] = total[at, :] + part


def gather_kernel(
    blk, c_h, send_h, recv_h, edge_h, nbr_h, nw_h, sw_h, wet_h,
    s0, s1, s2, c_v, nbr_v, nw_v, sw_v, wet_v, wts_o,
    picked, wts, send_v, recv_v, edge_v, sems,
):
    levels, cols, width = c_h.shape
    nedge = edge_h.shape[1]
    rows = padded(levels)
    bounds = [(lo, min(lo + 16, levels)) for lo in range(0, levels, 16)]
    pairs = [(send_h, send_v), (recv_h, recv_v), (edge_h, edge_v)]
    pairs += [(c_h.at[pl.ds(lo, hi - lo)], c_v.at[pl.ds(lo, hi - lo)]) for lo, hi in bounds]
    pairs += [(nbr_h, nbr_v), (nw_h, nw_v), (sw_h, sw_v), (wet_h, wet_v)]
    copies = [pltpu.make_async_copy(a, b, sems.at[i]) for i, (a, b) in enumerate(pairs)]
    for copy in copies:
        copy.start()
    parity = lax.bitwise_and(lax.axis_index(blk), jnp.int32(1))
    wts[...] = jnp.zeros_like(wts)
    for copy in copies[:3]:
        copy.wait()
    for slot in range(3):
        d = direction(slot, parity)
        weight = edge_v[d]
        if slot:
            weight = jnp.where(has_partner(slot, lax.axis_index(blk), lax.axis_size(blk)), weight, 0.0)
        wts[slot * nedge : (slot + 1) * nedge, 0:levels] = weight
        wts[3 * nedge + slot : 3 * nedge + slot + 1, 0:nedge] = recv_v[pl.ds(d, 1), :].astype(F32)
        wts[3 * nedge + 3 + slot : 3 * nedge + 4 + slot, 0:nedge] = send_v[pl.ds(d, 1), :].astype(F32)
    weights = wts[...].T
    wts_o[...] = weights
    lane = lax.broadcasted_iota(jnp.int32, (nedge, cols), 1).astype(F32)
    pick = [lane == weights[0:nedge, 3 * nedge + 3 + slot : 3 * nedge + 4 + slot] for slot in range(3)]
    pick = jnp.concatenate([p.astype(F32) for p in pick], axis=0).astype(BF16)
    rows_of = lambda slot, e, lo, n: picked[(slot * nedge + e) * rows + lo : (slot * nedge + e) * rows + lo + n, :]
    for i, (lo, hi) in enumerate(bounds):
        copies[3 + i].wait()
        for l in range(lo, hi):
            picked[pl.ds(l, 3 * nedge, stride=rows), :] = jnp.dot(pick, c_v[l], preferred_element_type=F32)
        pack_chunk(lo, levels, nedge, weights, rows_of, (0, 1, 2), (s0, s1, s2))
    if levels % 16 == 0:
        pack_chunk(levels, levels, nedge, weights, rows_of, (0, 1, 2), (s0, s1, s2))
    for copy in copies[3 + len(bounds) :]:
        copy.wait()


def column_operator(nbr_ref, nw_ref, sw_ref, a_ref, merged):
    levels = nw_ref.shape[0]
    cols = nbr_ref.shape[1]
    nbr = nbr_ref.shape[0]
    lane = lax.broadcasted_iota(jnp.int32, (8, cols), 1)
    sub = lax.broadcasted_iota(jnp.int32, (8, cols), 0)
    target = jnp.where(sub == nbr, lane, -1)
    for n in range(nbr):
        target = jnp.where(sub == n, nbr_ref[n : n + 1, :], target)
    same = [(target == nbr_ref[n : n + 1, :]).astype(F32) for n in range(nbr)]
    same.append((target == lane).astype(F32))
    for l in range(levels):
        total = same[nbr] * sw_ref[l : l + 1, :]
        for n in range(nbr):
            total = total + same[n] * nw_ref[l, n : n + 1, :]
        merged[l] = total
    half = 16
    for jt in range(cols // half):
        j = lax.broadcasted_iota(jnp.int32, (half, cols), 0) + jt * half
        hits = [j == nbr_ref[n : n + 1, :] for n in range(nbr)]
        hits.append(j == lax.broadcasted_iota(jnp.int32, (half, cols), 1))

        def fill(p, _):
            for i in range(2):
                value = jnp.zeros((half, cols), F32)
                for n in range(nbr, -1, -1):
                    value = jnp.where(hits[n], merged[p * 2 + i, n : n + 1, :], value)
                a_ref[p, jt * half : (jt + 1) * half, i * cols : (i + 1) * cols] = value.astype(BF16)
            return _

        lax.fori_loop(0, levels // 2, fill, 0, unroll=5)


def level_products(a_ref, state_of, exs, rows):
    pairs, cols, _ = a_ref.shape
    width = exs.shape[1]
    zero = jnp.zeros((cols, width), BF16)
    for p in range(pairs):
        left = jnp.concatenate([state_of(2 * p), zero], axis=1)
        right = jnp.concatenate([zero, state_of(2 * p + 1)], axis=1)
        both = jnp.dot(a_ref[p], jnp.concatenate([left, right], axis=0), preferred_element_type=F32)
        exs[pl.ds(2 * p, cols, stride=rows), :] = both[:, 0:width]
        exs[pl.ds(2 * p + 1, cols, stride=rows), :] = both[:, width:]
    for l in range(2 * pairs, rows):
        exs[pl.ds(l, cols, stride=rows), :] = jnp.zeros((cols, width), F32)


def operator_kernel(
    c_ref, nbr_ref, nw_ref, sw_ref, wet_ref, v_h, a_ref, state_ref, vt_ref, exs, merged, vf, vts, v_ref, sem
):
    levels, cols, width = c_ref.shape
    rows = padded(levels)
    load = pltpu.make_async_copy(v_h, v_ref, sem)
    load.start()
    column_operator(nbr_ref, nw_ref, sw_ref, a_ref, merged)
    level_products(a_ref, lambda l: c_ref[l], exs, rows)
    level = lax.broadcasted_iota(jnp.int32, (levels, cols), 0)
    wet = wet_ref[...]
    load.wait()
    vf[...] = jnp.zeros_like(vf)
    for m in range(levels):
        keep = jnp.maximum(level, m) < wet
        vf[m * rows : m * rows + levels, :] = jnp.where(keep, v_ref[m].astype(F32), 0.0)
    for l in range(rows):
        block = vf[pl.ds(l, rows, stride=rows), :]
        block = jnp.concatenate([block, jnp.zeros((128 - rows, cols), F32)], axis=0)
        vts[pl.ds(l, cols, stride=rows), :] = block.T
    vt_ref[...] = vts[...].reshape(cols, rows, 128).astype(BF16)
    vertical(vt_ref, exs, state_ref)


def send_kernel(blk, levels, r0, r1, r2, local_ref, vt_ref, wts_ref, send_h, state, s0, s1, send_s, sem):
    copy = pltpu.make_async_copy(send_h, send_s, sem)
    copy.start()
    add_edges((r0, r1, r2), levels, send_h.shape[1], vt_ref, state)
    copy.wait()
    pack_state(blk, levels, send_s, wts_ref, state, vt_ref.shape[1], (0, 1), (s0, s1))


def pack_state(blk, levels, send, weights, state, rows, slots, outs):
    parity = lax.bitwise_and(lax.axis_index(blk), jnp.int32(1))

    def rows_of(slot, e, lo, n):
        return state[pl.ds(pl.multiple_of(send[direction(slot, parity), e] * rows + lo, 8), n), :]

    for lo in range(0, levels + 1, 16):
        pack_chunk(lo, levels, send.shape[1], weights, rows_of, slots, outs)


def middle_kernel(blk, levels, cs, a_ref, vt_ref, wts_ref, send_h, out_ref, s2, exs, send_s, sem):
    copy = pltpu.make_async_copy(send_h, send_s, sem)
    copy.start()
    cols, rows, _ = vt_ref.shape
    level_products(a_ref, lambda l: cs[pl.ds(l, cols, stride=rows), :].astype(BF16), exs, rows)
    copy.wait()
    pack_state(blk, levels, send_s, wts_ref, cs, rows, (2,), (s2,))
    vertical(vt_ref, exs, out_ref)


def last_kernel(nedge, r0, r1, r2, local_ref, vt_ref, out_h, total, out_v, sems):
    levels, cols, width = out_h.shape
    rows = vt_ref.shape[1]
    add_edges((r0, r1, r2), levels, nedge, vt_ref, total)
    bounds = [0, *range(4, levels, 8), levels]
    copies = []
    for i, (lo, hi) in enumerate(zip(bounds, bounds[1:])):
        for l in range(lo, hi):
            out_v[l] = total[pl.ds(l, cols, stride=rows), :].astype(BF16)
        copies.append(pltpu.make_async_copy(out_v.at[pl.ds(lo, hi - lo)], out_h.at[pl.ds(lo, hi - lo)], sems.at[i]))
        copies[-1].start()
    for copy in copies:
        copy.wait()


VM = pl.BlockSpec(memory_space=pltpu.VMEM)
HB = pl.BlockSpec(memory_space=pltpu.HBM)
DMA = pltpu.SemaphoreType.DMA


def call(kernel, ins, specs, outs, out_specs, scratch, limit, flops=0, aliases=None):
    size = sum(x.size * x.dtype.itemsize for x in (*ins, *outs))
    return pl.pallas_call(
        kernel,
        out_shape=outs,
        in_specs=specs,
        out_specs=out_specs,
        scratch_shapes=scratch,
        input_output_aliases=aliases or {},
        compiler_params=pltpu.CompilerParams(vmem_limit_bytes=limit * 2**20),
        cost_estimate=pl.CostEstimate(flops=flops, bytes_accessed=size, transcendentals=0),
    )(*ins)


def odd_or_even(value, first, blk, basin):
    n, b = lax.axis_size(blk), lax.axis_size(basin)
    partner = {i: i + 1 for i in range(first, n - 1, 2)}
    partner |= {j: i for i, j in partner.items()}
    across = lambda g: g ^ 1 if g ^ 1 < b else g
    route = [(g * n + i, g * n + partner[i] if i in partner else across(g) * n + i) for g in range(b) for i in range(n)]
    return lax.ppermute(value, (basin, blk), route)


def along_basin(value, basin):
    b = lax.axis_size(basin)
    return lax.ppermute(value, basin, [(i, (i + 1) % b) for i in range(b)])


def local(tracers, nbr_cols, nbr_wts, self_wts, send_cols, recv_cols, edge_wts, wet_levels, vert_inv):
    cols, levels, width = tracers.shape
    rows = padded(levels)
    nedge = send_cols.shape[1]
    shape = jax.ShapeDtypeStruct
    by_level = jnp.transpose(tracers, (1, 0, 2))
    nbr_by_level = jnp.transpose(nbr_wts, (1, 0, 2))
    edge_by_entry = jnp.transpose(edge_wts, (0, 2, 1))
    wet = wet_levels.reshape(1, cols)
    in_hbm = lambda x: pltpu.with_memory_space_constraint(x, pltpu.HBM)
    send_h = in_hbm(send_cols)
    loads = [by_level, nbr_cols, nbr_by_level, self_wts, wet]
    same = lambda x: shape(x.shape, x.dtype)
    message = shape((message_rows(levels, nedge), width), BF16)
    columns = shape((cols * rows, width), F32)
    flat = pltpu.VMEM(columns.shape, F32)
    send_table = pltpu.SMEM(send_cols.shape, jnp.int32)

    first = call(
        functools.partial(gather_kernel, "blk"),
        (in_hbm(by_level), send_h, *map(in_hbm, (recv_cols, edge_by_entry, *loads[1:]))),
        [HB] * 8,
        [message] * 3 + [same(x) for x in loads] + [shape((128, 128), F32)],
        [VM] * 9,
        [
            pltpu.VMEM((3 * nedge * rows, width), F32), pltpu.VMEM((128, 128), F32), pltpu.VMEM(send_cols.shape, jnp.int32),
            pltpu.VMEM(recv_cols.shape, jnp.int32), pltpu.VMEM(edge_by_entry.shape, F32), DMA((7 + -(-levels // 16),)),
        ],
        16,
    )
    (to_next, to_odd, to_even), loads, wts = first[:3], first[3:8], first[8]
    operator_flops = 2 * levels * cols * cols * width
    vertical_flops = 2 * cols * rows * rows * width

    edge_flops = 3 * nedge * 2 * rows * rows * width
    along = along_basin(to_next, "basin")
    odd = odd_or_even(to_odd, 1, "blk", "basin")
    even = odd_or_even(to_even, 0, "blk", "basin")
    operator, partial, vt = call(
        operator_kernel, (*loads, in_hbm(vert_inv)), [VM] * 5 + [HB],
        [shape((levels // 2, cols, 2 * cols), BF16), columns, shape((cols, rows, 128), BF16)], [VM] * 3,
        [flat, pltpu.VMEM((levels, 8, cols), F32), pltpu.VMEM((rows * rows, cols), F32), pltpu.VMEM((cols * rows, 128), F32),
         pltpu.VMEM(vert_inv.shape, BF16), DMA],
        32, flops=operator_flops + vertical_flops,
    )
    state, to_next, to_odd = call(
        functools.partial(send_kernel, "blk", levels),
        (along, odd, even, partial, vt, wts, send_h), [VM] * 6 + [HB],
        [columns] + [message] * 2, [VM] * 3,
        [send_table, DMA], 16, flops=edge_flops, aliases={3: 0},
    )
    along = along_basin(to_next, "basin")
    odd = odd_or_even(to_odd, 1, "blk", "basin")
    partial, to_even = call(
        functools.partial(middle_kernel, "blk", levels), (state, operator, vt, wts, send_h), [VM] * 4 + [HB],
        [columns, message], [VM] * 2, [flat, send_table, DMA], 32, flops=operator_flops + vertical_flops,
    )
    even = odd_or_even(to_even, 0, "blk", "basin")
    out, _ = call(
        functools.partial(last_kernel, nedge), (along, odd, even, partial, vt), [VM] * 5,
        [shape((levels, cols, width), BF16), columns], [HB, VM],
        [pltpu.VMEM((levels, cols, width), BF16), DMA((1 + -(-levels // 8),))], 16, flops=edge_flops, aliases={3: 1},
    )
    return jnp.transpose(out, (1, 0, 2))


def solution(mesh):
    in_specs = (
        P(("basin", "blk"), None, None),
        P(None, ("basin", "blk")),
        P(None, None, ("basin", "blk")),
        P(None, ("basin", "blk")),
        P(None, ("basin", "blk")),
        P(None, ("basin", "blk")),
        P(None, None, ("basin", "blk")),
        P(("basin", "blk")),
        P(None, None, ("basin", "blk")),
    )
    out_specs = P(("basin", "blk"), None, None)
    return jax.shard_map(local, mesh=mesh, in_specs=in_specs, out_specs=out_specs, check_vma=False)
```

```python
import functools

import jax
import jax.numpy as jnp
from jax import lax
from jax.experimental import pallas as pl
from jax.experimental.pallas import tpu as pltpu
from jax.sharding import PartitionSpec as P

NSTEP = 2
F32 = jnp.float32
BF16 = jnp.bfloat16


def padded(levels):
    return -(-levels // 8) * 8


def whole_rows(levels):
    return levels // 16 * 16


def message_rows(levels, nedge):
    return levels * nedge + 16


def direction(slot, parity):
    return lax.bitwise_xor(parity, jnp.int32(2 - slot)) if slot else 2


def has_partner(slot, at, count):
    first = lax.bitwise_and(at + slot // 2, jnp.int32(1)) == 1
    return jnp.where(first, at + 1 < count, at > 0)


def pack_chunk(parity, lo, levels, send, weights, rows_of, slots, outs):
    whole = whole_rows(levels)
    nedge = send.shape[1]
    rest = levels - whole
    share = 8 // rest if rest else 0
    for slot, out in zip(slots, outs):
        d = direction(slot, parity)
        if lo < whole:
            for e in range(nedge):
                k = slot * nedge + e
                value = rows_of(send[d, e], lo, 16) * weights[lo : lo + 16, k : k + 1]
                out[e * whole + lo : e * whole + lo + 16, :] = value.astype(BF16)
            continue
        sub = lax.broadcasted_iota(jnp.int32, (8, out.shape[1]), 0)
        parts = []
        for first in range(0, nedge, share or nedge):
            part = None
            for q in range(share):
                k = slot * nedge + first + q
                value = rows_of(send[d, first + q], lo, 8) * weights[lo : lo + 8, k : k + 1]
                if q:
                    value = pltpu.roll(value, q * rest, 0)
                part = value if part is None else jnp.where(sub >= q * rest, value, part)
            if share:
                parts.append(part)
        table = jnp.broadcast_to(weights[0:16, 3 * nedge + slot : 3 * nedge + slot + 1], (16, out.shape[1]))
        out[nedge * whole :, :] = jnp.concatenate(parts + [table], axis=0).astype(BF16)


def vertical(vt_ref, exs, out):
    cols, rows, _ = vt_ref.shape
    pad = jnp.zeros((64 - rows, out.shape[1]), F32)

    def column(j, _):
        at = pl.ds(pl.multiple_of(j * rows, 8), rows)
        x = jnp.concatenate([exs[at, :], pad], axis=0).astype(BF16)
        out[at, :] = jnp.dot(vt_ref[j][:, 0:64], x, preferred_element_type=F32)
        return _

    lax.fori_loop(0, cols, column, 0, unroll=16)


def add_edges(edges, levels, nedge, vt_ref, total):
    whole = whole_rows(levels)
    rest = levels - whole
    share = 8 // rest if rest else 0
    rows = vt_ref.shape[1]
    group = max(share, 4)
    pad = jnp.zeros((8, total.shape[1]), F32)
    for ref in edges:
        table = ref[levels * nedge :, :].astype(F32).astype(jnp.int32)
        tails = ref[whole * nedge : levels * nedge, :].astype(F32) if rest else None
        for first in range(0, nedge, group):
            targets = [table[e, 0] for e in range(first, first + group)]
            products = []
            for e, j in zip(range(first, first + group), targets):
                x = ref[e * whole : (e + 1) * whole, :]
                if rest:
                    tail = tails[e // share * 8 : e // share * 8 + 8]
                    if e % share:
                        tail = pltpu.roll(tail, 8 - e % share * rest, 0)
                    x = jnp.concatenate([x, jnp.concatenate([tail, pad], axis=0).astype(BF16)], axis=0)
                products.append(jnp.dot(vt_ref[j][:, 0 : x.shape[0]], x, preferred_element_type=F32))
            for j, part in zip(targets, products):
                at = pl.ds(pl.multiple_of(j * rows, 8), rows)
                total[at, :] = total[at, :] + part


def gather_kernel(
    blk, c_h, send_h, recv_h, edge_h, nbr_h, nw_h, sw_h, wet_h,
    s0, s1, s2, c_v, nbr_v, nw_v, sw_v, wet_v, wts_o,
    cf, wts, recv_v, edge_v, send_s, sems,
):
    levels, cols, width = c_h.shape
    nedge = edge_h.shape[1]
    pitch = cols + 8
    bounds = [(lo, min(lo + 16, levels)) for lo in range(0, levels, 16)]
    pairs = [(send_h, send_s), (recv_h, recv_v), (edge_h, edge_v)]
    pairs += [(c_h.at[pl.ds(lo, hi - lo)], c_v.at[pl.ds(lo, hi - lo)]) for lo, hi in bounds]
    pairs += [(nbr_h, nbr_v), (nw_h, nw_v), (sw_h, sw_v), (wet_h, wet_v)]
    copies = [pltpu.make_async_copy(a, b, sems.at[i]) for i, (a, b) in enumerate(pairs)]
    for copy in copies:
        copy.start()
    parity = lax.bitwise_and(lax.axis_index(blk), jnp.int32(1))
    wts[...] = jnp.zeros_like(wts)
    for copy in copies[:3]:
        copy.wait()
    for slot in range(3):
        d = direction(slot, parity)
        weight = edge_v[d]
        if slot:
            weight = jnp.where(has_partner(slot, lax.axis_index(blk), lax.axis_size(blk)), weight, 0.0)
        wts[slot * nedge : (slot + 1) * nedge, 0:levels] = weight
        wts[3 * nedge + slot : 3 * nedge + slot + 1, 0:nedge] = recv_v[pl.ds(d, 1), :].astype(F32)
    weights = wts[...].T
    wts_o[...] = weights
    rows_of = lambda s, lo, n: cf[pl.ds(lo * pitch + s, n, stride=pitch), :]
    for i, (lo, hi) in enumerate(bounds):
        copies[3 + i].wait()
        for l in range(lo, hi):
            cf[l * pitch : l * pitch + cols, :] = c_v[l].astype(F32)
        pack_chunk(parity, lo, levels, send_s, weights, rows_of, (0, 1, 2), (s0, s1, s2))
    if levels % 16 == 0:
        pack_chunk(parity, levels, levels, send_s, weights, rows_of, (0, 1, 2), (s0, s1, s2))
    for copy in copies[3 + len(bounds) :]:
        copy.wait()


def column_operator(nbr_ref, nw_ref, sw_ref, a_ref, merged):
    levels = nw_ref.shape[0]
    cols = nbr_ref.shape[1]
    nbr = nbr_ref.shape[0]
    lane = lax.broadcasted_iota(jnp.int32, (8, cols), 1)
    sub = lax.broadcasted_iota(jnp.int32, (8, cols), 0)
    target = jnp.where(sub == nbr, lane, -1)
    for n in range(nbr):
        target = jnp.where(sub == n, nbr_ref[n : n + 1, :], target)
    same = [(target == nbr_ref[n : n + 1, :]).astype(F32) for n in range(nbr)]
    same.append((target == lane).astype(F32))
    for l in range(levels):
        total = same[nbr] * sw_ref[l : l + 1, :]
        for n in range(nbr):
            total = total + same[n] * nw_ref[l, n : n + 1, :]
        merged[l] = total
    half = 16
    for jt in range(cols // half):
        j = lax.broadcasted_iota(jnp.int32, (half, cols), 0) + jt * half
        hits = [j == nbr_ref[n : n + 1, :] for n in range(nbr)]
        hits.append(j == lax.broadcasted_iota(jnp.int32, (half, cols), 1))

        def fill(p, _):
            for i in range(2):
                value = jnp.zeros((half, cols), F32)
                for n in range(nbr, -1, -1):
                    value = jnp.where(hits[n], merged[p * 2 + i, n : n + 1, :], value)
                a_ref[p, jt * half : (jt + 1) * half, i * cols : (i + 1) * cols] = value.astype(BF16)
            return _

        lax.fori_loop(0, levels // 2, fill, 0, unroll=5)


def level_products(a_ref, state_of, exs, rows):
    pairs, cols, _ = a_ref.shape
    width = exs.shape[1]
    zero = jnp.zeros((cols, width), BF16)
    for p in range(pairs):
        left = jnp.concatenate([state_of(2 * p), zero], axis=1)
        right = jnp.concatenate([zero, state_of(2 * p + 1)], axis=1)
        both = jnp.dot(a_ref[p], jnp.concatenate([left, right], axis=0), preferred_element_type=F32)
        exs[pl.ds(2 * p, cols, stride=rows), :] = both[:, 0:width]
        exs[pl.ds(2 * p + 1, cols, stride=rows), :] = both[:, width:]
    for l in range(2 * pairs, rows):
        exs[pl.ds(l, cols, stride=rows), :] = jnp.zeros((cols, width), F32)


def operator_kernel(
    c_ref, nbr_ref, nw_ref, sw_ref, wet_ref, v_h, a_ref, state_ref, vt_ref, exs, merged, vf, vts, v_ref, sem
):
    levels, cols, width = c_ref.shape
    rows = padded(levels)
    load = pltpu.make_async_copy(v_h, v_ref, sem)
    load.start()
    column_operator(nbr_ref, nw_ref, sw_ref, a_ref, merged)
    level_products(a_ref, lambda l: c_ref[l], exs, rows)
    level = lax.broadcasted_iota(jnp.int32, (levels, cols), 0)
    wet = wet_ref[...]
    load.wait()
    vf[...] = jnp.zeros_like(vf)
    for m in range(levels):
        keep = jnp.maximum(level, m) < wet
        vf[m * rows : m * rows + levels, :] = jnp.where(keep, v_ref[m].astype(F32), 0.0)
    for l in range(rows):
        block = vf[pl.ds(l, rows, stride=rows), :]
        block = jnp.concatenate([block, jnp.zeros((128 - rows, cols), F32)], axis=0)
        vts[pl.ds(l, cols, stride=rows), :] = block.T
    vt_ref[...] = vts[...].reshape(cols, rows, 128).astype(BF16)
    vertical(vt_ref, exs, state_ref)


def arrived_kernel(levels, nedge, r0, r2, local_ref, vt_ref, total):
    add_edges((r0, r2), levels, nedge, vt_ref, total)


def send_kernel(blk, levels, r1, local_ref, vt_ref, wts_ref, send_h, state, s0, s1, s2, send_s, sem):
    copy = pltpu.make_async_copy(send_h, send_s, sem)
    copy.start()
    add_edges((r1,), levels, send_h.shape[1], vt_ref, state)
    copy.wait()
    pack_state(blk, levels, send_s, wts_ref, state, vt_ref.shape[1], (0, 1, 2), (s0, s1, s2))


def pack_state(blk, levels, send, weights, state, rows, slots, outs):
    parity = lax.bitwise_and(lax.axis_index(blk), jnp.int32(1))
    rows_of = lambda s, lo, n: state[pl.ds(pl.multiple_of(s * rows + lo, 8), n), :]
    for lo in range(0, levels + 1, 16):
        pack_chunk(parity, lo, levels, send, weights, rows_of, slots, outs)


def middle_kernel(cs, a_ref, vt_ref, out_ref, exs):
    cols, rows, _ = vt_ref.shape
    level_products(a_ref, lambda l: cs[pl.ds(l, cols, stride=rows), :].astype(BF16), exs, rows)
    vertical(vt_ref, exs, out_ref)


def last_kernel(nedge, r1, local_ref, vt_ref, out_h, total, out_v, sems):
    levels, cols, width = out_h.shape
    rows = vt_ref.shape[1]
    add_edges((r1,), levels, nedge, vt_ref, total)
    bounds = [0, *range(4, levels, 8), levels]
    copies = []
    for i, (lo, hi) in enumerate(zip(bounds, bounds[1:])):
        for l in range(lo, hi):
            out_v[l] = total[pl.ds(l, cols, stride=rows), :].astype(BF16)
        copies.append(pltpu.make_async_copy(out_v.at[pl.ds(lo, hi - lo)], out_h.at[pl.ds(lo, hi - lo)], sems.at[i]))
        copies[-1].start()
    for copy in copies:
        copy.wait()


VM = pl.BlockSpec(memory_space=pltpu.VMEM)
HB = pl.BlockSpec(memory_space=pltpu.HBM)
DMA = pltpu.SemaphoreType.DMA


def call(kernel, ins, specs, outs, out_specs, scratch, limit, flops=0, aliases=None):
    size = sum(x.size * x.dtype.itemsize for x in (*ins, *outs))
    return pl.pallas_call(
        kernel,
        out_shape=outs,
        in_specs=specs,
        out_specs=out_specs,
        scratch_shapes=scratch,
        input_output_aliases=aliases or {},
        compiler_params=pltpu.CompilerParams(vmem_limit_bytes=limit * 2**20),
        cost_estimate=pl.CostEstimate(flops=flops, bytes_accessed=size, transcendentals=0),
    )(*ins)


def odd_or_even(value, first, blk, basin):
    n, b = lax.axis_size(blk), lax.axis_size(basin)
    partner = {i: i + 1 for i in range(first, n - 1, 2)}
    partner |= {j: i for i, j in partner.items()}
    across = lambda g: g ^ 1 if g ^ 1 < b else g
    route = [(g * n + i, g * n + partner[i] if i in partner else across(g) * n + i) for g in range(b) for i in range(n)]
    return lax.ppermute(value, (basin, blk), route)


def along_basin(value, basin):
    b = lax.axis_size(basin)
    return lax.ppermute(value, basin, [(i, (i + 1) % b) for i in range(b)])


def local(tracers, nbr_cols, nbr_wts, self_wts, send_cols, recv_cols, edge_wts, wet_levels, vert_inv):
    cols, levels, width = tracers.shape
    rows = padded(levels)
    nedge = send_cols.shape[1]
    shape = jax.ShapeDtypeStruct
    by_level = jnp.transpose(tracers, (1, 0, 2))
    nbr_by_level = jnp.transpose(nbr_wts, (1, 0, 2))
    edge_by_entry = jnp.transpose(edge_wts, (0, 2, 1))
    wet = wet_levels.reshape(1, cols)
    in_hbm = lambda x: pltpu.with_memory_space_constraint(x, pltpu.HBM)
    send_h = in_hbm(send_cols)
    loads = [by_level, nbr_cols, nbr_by_level, self_wts, wet]
    same = lambda x: shape(x.shape, x.dtype)
    message = shape((message_rows(levels, nedge), width), BF16)
    columns = shape((cols * rows, width), F32)
    flat = pltpu.VMEM(columns.shape, F32)
    send_table = pltpu.SMEM(send_cols.shape, jnp.int32)

    first = call(
        functools.partial(gather_kernel, "blk"),
        (in_hbm(by_level), send_h, *map(in_hbm, (recv_cols, edge_by_entry, *loads[1:]))),
        [HB] * 8,
        [message] * 3 + [same(x) for x in loads] + [shape((128, 128), F32)],
        [VM] * 9,
        [
            pltpu.VMEM((rows * (cols + 8), width), F32),
            pltpu.VMEM((128, 128), F32), pltpu.VMEM(recv_cols.shape, jnp.int32), pltpu.VMEM(edge_by_entry.shape, F32),
            send_table, DMA((7 + -(-levels // 16),)),
        ],
        16,
    )
    (to_next, to_odd, to_even), loads, wts = first[:3], first[3:8], first[8]
    operator_flops = 2 * levels * cols * cols * width
    vertical_flops = 2 * cols * rows * rows * width

    edge_flops = nedge * 2 * rows * rows * width

    def arrived(along, even, partial):
        return call(
            functools.partial(arrived_kernel, levels, nedge), (along, even, partial, vt), [VM] * 4, [columns], [VM], [], 16,
            flops=2 * edge_flops, aliases={2: 0},
        )[0]

    along = along_basin(to_next, "basin")
    odd = odd_or_even(to_odd, 1, "blk", "basin")
    even = odd_or_even(to_even, 0, "blk", "basin")
    operator, partial, vt = call(
        operator_kernel, (*loads, in_hbm(vert_inv)), [VM] * 5 + [HB],
        [shape((levels // 2, cols, 2 * cols), BF16), columns, shape((cols, rows, 128), BF16)], [VM] * 3,
        [flat, pltpu.VMEM((levels, 8, cols), F32), pltpu.VMEM((rows * rows, cols), F32), pltpu.VMEM((cols * rows, 128), F32),
         pltpu.VMEM(vert_inv.shape, BF16), DMA],
        32, flops=operator_flops + vertical_flops,
    )
    state, to_next, to_odd, to_even = call(
        functools.partial(send_kernel, "blk", levels),
        (odd, arrived(along, even, partial), vt, wts, send_h), [VM] * 4 + [HB],
        [columns] + [message] * 3, [VM] * 4, [send_table, DMA], 16, flops=edge_flops, aliases={1: 0},
    )
    along = along_basin(to_next, "basin")
    odd = odd_or_even(to_odd, 1, "blk", "basin")
    even = odd_or_even(to_even, 0, "blk", "basin")
    (partial,) = call(
        middle_kernel, (state, operator, vt), [VM] * 3, [columns], [VM], [flat], 32, flops=operator_flops + vertical_flops,
    )
    out, _ = call(
        functools.partial(last_kernel, nedge), (odd, arrived(along, even, partial), vt), [VM] * 3,
        [shape((levels, cols, width), BF16), columns], [HB, VM],
        [pltpu.VMEM((levels, cols, width), BF16), DMA((1 + -(-levels // 8),))], 16, flops=edge_flops, aliases={1: 1},
    )
    return jnp.transpose(out, (1, 0, 2))


def solution(mesh):
    in_specs = (
        P(("basin", "blk"), None, None),
        P(None, ("basin", "blk")),
        P(None, None, ("basin", "blk")),
        P(None, ("basin", "blk")),
        P(None, ("basin", "blk")),
        P(None, ("basin", "blk")),
        P(None, None, ("basin", "blk")),
        P(("basin", "blk")),
        P(None, None, ("basin", "blk")),
    )
    out_specs = P(("basin", "blk"), None, None)
    return jax.shard_map(local, mesh=mesh, in_specs=in_specs, out_specs=out_specs, check_vma=False)
```

```python
import functools

import jax
import jax.numpy as jnp
from jax import lax
from jax.experimental import pallas as pl
from jax.experimental.pallas import tpu as pltpu
from jax.sharding import PartitionSpec as P

NSTEP = 2
F32 = jnp.float32
BF16 = jnp.bfloat16


def padded(levels):
    return -(-levels // 8) * 8


def whole_rows(levels):
    return levels // 16 * 16


def message_rows(levels, nedge):
    return levels * nedge + 16


def direction(slot, parity):
    return lax.bitwise_xor(parity, jnp.int32(2 - slot)) if slot else 2


def has_partner(slot, at, count):
    first = lax.bitwise_and(at + slot // 2, jnp.int32(1)) == 1
    return jnp.where(first, at + 1 < count, at > 0)


def pack_chunk(lo, levels, nedge, source, weights, rows_of, slots, outs):
    whole = whole_rows(levels)
    rest = levels - whole
    share = 8 // rest if rest else 0
    for slot, out in zip(slots, outs):
        if lo < whole:
            for e in range(nedge):
                k = slot * nedge + e
                value = rows_of(source(slot, e), lo, 16) * weights[lo : lo + 16, k : k + 1]
                out[e * whole + lo : e * whole + lo + 16, :] = value.astype(BF16)
            continue
        sub = lax.broadcasted_iota(jnp.int32, (8, out.shape[1]), 0)
        parts = []
        for first in range(0, nedge, share or nedge):
            part = None
            for q in range(share):
                k = slot * nedge + first + q
                value = rows_of(source(slot, first + q), lo, 8) * weights[lo : lo + 8, k : k + 1]
                if q:
                    value = pltpu.roll(value, q * rest, 0)
                part = value if part is None else jnp.where(sub >= q * rest, value, part)
            if share:
                parts.append(part)
        if out.shape[0] > levels * nedge:
            parts.append(jnp.broadcast_to(weights[0:16, 3 * nedge + slot : 3 * nedge + slot + 1], (16, out.shape[1])))
        if parts:
            out[nedge * whole :, :] = jnp.concatenate(parts, axis=0).astype(BF16)


def vertical(vt_ref, exs, out):
    cols, rows, _ = vt_ref.shape
    pad = jnp.zeros((64 - rows, out.shape[1]), F32)

    def column(j, _):
        at = pl.ds(pl.multiple_of(j * rows, 8), rows)
        x = jnp.concatenate([exs[at, :], pad], axis=0).astype(BF16)
        out[at, :] = jnp.dot(vt_ref[j][:, 0:64], x, preferred_element_type=F32)
        return _

    lax.fori_loop(0, cols, column, 0, unroll=16)


def add_edges(edges, levels, nedge, vt_ref, total):
    whole = whole_rows(levels)
    rest = levels - whole
    share = 8 // rest if rest else 0
    rows = vt_ref.shape[1]
    group = max(share, 4)
    pad = jnp.zeros((8, total.shape[1]), F32)
    for ref, first_ref in edges:
        table = first_ref[levels * nedge :, :].astype(F32).astype(jnp.int32)
        tails = ref[whole * nedge : levels * nedge, :].astype(F32) if rest else None
        for first in range(0, nedge, group):
            targets = [table[e, 0] for e in range(first, first + group)]
            products = []
            for e, j in zip(range(first, first + group), targets):
                x = ref[e * whole : (e + 1) * whole, :]
                if rest:
                    tail = tails[e // share * 8 : e // share * 8 + 8]
                    if e % share:
                        tail = pltpu.roll(tail, 8 - e % share * rest, 0)
                    x = jnp.concatenate([x, jnp.concatenate([tail, pad], axis=0).astype(BF16)], axis=0)
                products.append(jnp.dot(vt_ref[j][:, 0 : x.shape[0]], x, preferred_element_type=F32))
            for j, part in zip(targets, products):
                at = pl.ds(pl.multiple_of(j * rows, 8), rows)
                total[at, :] = total[at, :] + part


def gather_kernel(
    blk, c_h, send_h, recv_h, edge_h, nbr_h, nw_h, sw_h, wet_h,
    s0, s1, s2, c_v, nbr_v, nw_v, sw_v, wet_v, wts_o,
    cf, wts, recv_v, edge_v, send_v, send_s, sems,
):
    levels, cols, width = c_h.shape
    nedge = edge_h.shape[1]
    pitch = cols + 8
    bounds = [(lo, min(lo + 16, levels)) for lo in range(0, levels, 16)]
    pairs = [(send_h, send_s), (send_h, send_v), (recv_h, recv_v), (edge_h, edge_v)]
    pairs += [(c_h.at[pl.ds(lo, hi - lo)], c_v.at[pl.ds(lo, hi - lo)]) for lo, hi in bounds]
    pairs += [(nbr_h, nbr_v), (nw_h, nw_v), (sw_h, sw_v), (wet_h, wet_v)]
    copies = [pltpu.make_async_copy(a, b, sems.at[i]) for i, (a, b) in enumerate(pairs)]
    for copy in copies:
        copy.start()
    parity = lax.bitwise_and(lax.axis_index(blk), jnp.int32(1))
    wts[...] = jnp.zeros_like(wts)
    for copy in copies[:4]:
        copy.wait()
    for slot in range(3):
        d = direction(slot, parity)
        weight = edge_v[d]
        if slot:
            weight = jnp.where(has_partner(slot, lax.axis_index(blk), lax.axis_size(blk)), weight, 0.0)
        wts[slot * nedge : (slot + 1) * nedge, 0:levels] = weight
        wts[3 * nedge + slot : 3 * nedge + slot + 1, 0:nedge] = recv_v[pl.ds(d, 1), :].astype(F32)
        wts[3 * nedge + 3 + slot : 3 * nedge + 4 + slot, 0:nedge] = send_v[pl.ds(d, 1), :].astype(F32)
    weights = wts[...].T
    wts_o[...] = weights
    source = lambda slot, e: send_s[direction(slot, parity), e]
    rows_of = lambda s, lo, n: cf[pl.ds(lo * pitch + s, n, stride=pitch), :]
    for i, (lo, hi) in enumerate(bounds):
        copies[4 + i].wait()
        for l in range(lo, hi):
            cf[l * pitch : l * pitch + cols, :] = c_v[l].astype(F32)
        pack_chunk(lo, levels, nedge, source, weights, rows_of, (0, 1, 2), (s0, s1, s2))
    if levels % 16 == 0:
        pack_chunk(levels, levels, nedge, source, weights, rows_of, (0, 1, 2), (s0, s1, s2))
    for copy in copies[4 + len(bounds) :]:
        copy.wait()


def column_operator(nbr_ref, nw_ref, sw_ref, a_ref, merged):
    levels = nw_ref.shape[0]
    cols = nbr_ref.shape[1]
    nbr = nbr_ref.shape[0]
    lane = lax.broadcasted_iota(jnp.int32, (8, cols), 1)
    sub = lax.broadcasted_iota(jnp.int32, (8, cols), 0)
    target = jnp.where(sub == nbr, lane, -1)
    for n in range(nbr):
        target = jnp.where(sub == n, nbr_ref[n : n + 1, :], target)
    same = [(target == nbr_ref[n : n + 1, :]).astype(F32) for n in range(nbr)]
    same.append((target == lane).astype(F32))
    for l in range(levels):
        total = same[nbr] * sw_ref[l : l + 1, :]
        for n in range(nbr):
            total = total + same[n] * nw_ref[l, n : n + 1, :]
        merged[l] = total
    half = 16
    for jt in range(cols // half):
        j = lax.broadcasted_iota(jnp.int32, (half, cols), 0) + jt * half
        hits = [j == nbr_ref[n : n + 1, :] for n in range(nbr)]
        hits.append(j == lax.broadcasted_iota(jnp.int32, (half, cols), 1))

        def fill(p, _):
            for i in range(2):
                value = jnp.zeros((half, cols), F32)
                for n in range(nbr, -1, -1):
                    value = jnp.where(hits[n], merged[p * 2 + i, n : n + 1, :], value)
                a_ref[p, jt * half : (jt + 1) * half, i * cols : (i + 1) * cols] = value.astype(BF16)
            return _

        lax.fori_loop(0, levels // 2, fill, 0, unroll=5)


def level_products(a_ref, state_of, exs, rows):
    pairs, cols, _ = a_ref.shape
    width = exs.shape[1]
    zero = jnp.zeros((cols, width), BF16)
    for p in range(pairs):
        left = jnp.concatenate([state_of(2 * p), zero], axis=1)
        right = jnp.concatenate([zero, state_of(2 * p + 1)], axis=1)
        both = jnp.dot(a_ref[p], jnp.concatenate([left, right], axis=0), preferred_element_type=F32)
        exs[pl.ds(2 * p, cols, stride=rows), :] = both[:, 0:width]
        exs[pl.ds(2 * p + 1, cols, stride=rows), :] = both[:, width:]
    for l in range(2 * pairs, rows):
        exs[pl.ds(l, cols, stride=rows), :] = jnp.zeros((cols, width), F32)


def operator_kernel(
    c_ref, nbr_ref, nw_ref, sw_ref, wet_ref, v_h, a_ref, state_ref, vt_ref, exs, merged, vf, vts, v_ref, sem
):
    levels, cols, width = c_ref.shape
    rows = padded(levels)
    load = pltpu.make_async_copy(v_h, v_ref, sem)
    load.start()
    column_operator(nbr_ref, nw_ref, sw_ref, a_ref, merged)
    level_products(a_ref, lambda l: c_ref[l], exs, rows)
    level = lax.broadcasted_iota(jnp.int32, (levels, cols), 0)
    wet = wet_ref[...]
    load.wait()
    vf[...] = jnp.zeros_like(vf)
    for m in range(levels):
        keep = jnp.maximum(level, m) < wet
        vf[m * rows : m * rows + levels, :] = jnp.where(keep, v_ref[m].astype(F32), 0.0)
    for l in range(rows):
        block = vf[pl.ds(l, rows, stride=rows), :]
        block = jnp.concatenate([block, jnp.zeros((128 - rows, cols), F32)], axis=0)
        vts[pl.ds(l, cols, stride=rows), :] = block.T
    vt_ref[...] = vts[...].reshape(cols, rows, 128).astype(BF16)
    vertical(vt_ref, exs, state_ref)


def arrived_kernel(levels, nedge, r0, r2, t0, t2, local_ref, vt_ref, total):
    add_edges(((r0, t0), (r2, t2)), levels, nedge, vt_ref, total)


def send_kernel(levels, nedge, r1, local_ref, vt_ref, wts_ref, state, s0, s1, s2):
    rows = vt_ref.shape[1]
    add_edges(((r1, r1),), levels, nedge, vt_ref, state)
    tables = [wts_ref[0:nedge, 3 * nedge + 3 + slot : 3 * nedge + 4 + slot].astype(jnp.int32) for slot in range(3)]
    source = lambda slot, e: tables[slot][e, 0]
    rows_of = lambda s, lo, n: state[pl.ds(pl.multiple_of(s * rows + lo, 8), n), :]
    for lo in range(0, levels + 1, 16):
        pack_chunk(lo, levels, nedge, source, wts_ref, rows_of, (0, 1, 2), (s0, s1, s2))


def middle_kernel(cs, a_ref, vt_ref, out_ref, exs):
    cols, rows, _ = vt_ref.shape
    level_products(a_ref, lambda l: cs[pl.ds(l, cols, stride=rows), :].astype(BF16), exs, rows)
    vertical(vt_ref, exs, out_ref)


def last_kernel(nedge, r1, t1, local_ref, vt_ref, out_h, total, out_v, sems):
    levels, cols, width = out_h.shape
    rows = vt_ref.shape[1]
    add_edges(((r1, t1),), levels, nedge, vt_ref, total)
    bounds = [0, *range(4, levels, 8), levels]
    copies = []
    for i, (lo, hi) in enumerate(zip(bounds, bounds[1:])):
        for l in range(lo, hi):
            out_v[l] = total[pl.ds(l, cols, stride=rows), :].astype(BF16)
        copies.append(pltpu.make_async_copy(out_v.at[pl.ds(lo, hi - lo)], out_h.at[pl.ds(lo, hi - lo)], sems.at[i]))
        copies[-1].start()
    for copy in copies:
        copy.wait()


VM = pl.BlockSpec(memory_space=pltpu.VMEM)
HB = pl.BlockSpec(memory_space=pltpu.HBM)
DMA = pltpu.SemaphoreType.DMA


def call(kernel, ins, specs, outs, out_specs, scratch, limit, flops=0, aliases=None):
    size = sum(x.size * x.dtype.itemsize for x in (*ins, *outs))
    return pl.pallas_call(
        kernel,
        out_shape=outs,
        in_specs=specs,
        out_specs=out_specs,
        scratch_shapes=scratch,
        input_output_aliases=aliases or {},
        compiler_params=pltpu.CompilerParams(vmem_limit_bytes=limit * 2**20),
        cost_estimate=pl.CostEstimate(flops=flops, bytes_accessed=size, transcendentals=0),
    )(*ins)


def odd_or_even(value, first, blk, basin):
    n, b = lax.axis_size(blk), lax.axis_size(basin)
    partner = {i: i + 1 for i in range(first, n - 1, 2)}
    partner |= {j: i for i, j in partner.items()}
    across = lambda g: g ^ 1 if g ^ 1 < b else g
    route = [(g * n + i, g * n + partner[i] if i in partner else across(g) * n + i) for g in range(b) for i in range(n)]
    return lax.ppermute(value, (basin, blk), route)


def along_basin(value, basin):
    b = lax.axis_size(basin)
    return lax.ppermute(value, basin, [(i, (i + 1) % b) for i in range(b)])


def local(tracers, nbr_cols, nbr_wts, self_wts, send_cols, recv_cols, edge_wts, wet_levels, vert_inv):
    cols, levels, width = tracers.shape
    rows = padded(levels)
    nedge = send_cols.shape[1]
    shape = jax.ShapeDtypeStruct
    by_level = jnp.transpose(tracers, (1, 0, 2))
    nbr_by_level = jnp.transpose(nbr_wts, (1, 0, 2))
    edge_by_entry = jnp.transpose(edge_wts, (0, 2, 1))
    wet = wet_levels.reshape(1, cols)
    in_hbm = lambda x: pltpu.with_memory_space_constraint(x, pltpu.HBM)
    send_h = in_hbm(send_cols)
    loads = [by_level, nbr_cols, nbr_by_level, self_wts, wet]
    same = lambda x: shape(x.shape, x.dtype)
    message = shape((message_rows(levels, nedge), width), BF16)
    columns = shape((cols * rows, width), F32)
    flat = pltpu.VMEM(columns.shape, F32)

    first = call(
        functools.partial(gather_kernel, "blk"),
        (in_hbm(by_level), send_h, *map(in_hbm, (recv_cols, edge_by_entry, *loads[1:]))),
        [HB] * 8,
        [message] * 3 + [same(x) for x in loads] + [shape((128, 128), F32)],
        [VM] * 9,
        [
            pltpu.VMEM((rows * (cols + 8), width), F32),
            pltpu.VMEM((128, 128), F32), pltpu.VMEM(recv_cols.shape, jnp.int32), pltpu.VMEM(edge_by_entry.shape, F32),
            pltpu.VMEM(send_cols.shape, jnp.int32), pltpu.SMEM(send_cols.shape, jnp.int32), DMA((8 + -(-levels // 16),)),
        ],
        16,
    )
    (to_next, to_odd, to_even), loads, wts = first[:3], first[3:8], first[8]
    operator_flops = 2 * levels * cols * cols * width
    vertical_flops = 2 * cols * rows * rows * width

    edge_flops = nedge * 2 * rows * rows * width

    def arrived(along, even, along_table, even_table, partial):
        return call(
            functools.partial(arrived_kernel, levels, nedge), (along, even, along_table, even_table, partial, vt), [VM] * 6,
            [columns], [VM], [], 16, flops=2 * edge_flops, aliases={4: 0},
        )[0]

    along = along_basin(to_next, "basin")
    odd = odd_or_even(to_odd, 1, "blk", "basin")
    even = odd_or_even(to_even, 0, "blk", "basin")
    operator, partial, vt = call(
        operator_kernel, (*loads, in_hbm(vert_inv)), [VM] * 5 + [HB],
        [shape((levels // 2, cols, 2 * cols), BF16), columns, shape((cols, rows, 128), BF16)], [VM] * 3,
        [flat, pltpu.VMEM((levels, 8, cols), F32), pltpu.VMEM((rows * rows, cols), F32), pltpu.VMEM((cols * rows, 128), F32),
         pltpu.VMEM(vert_inv.shape, BF16), DMA],
        32, flops=operator_flops + vertical_flops,
    )
    state, to_next, to_odd, to_even = call(
        functools.partial(send_kernel, levels, nedge),
        (odd, arrived(along, even, along, even, partial), vt, wts), [VM] * 4,
        [columns] + [shape((levels * nedge, width), BF16)] * 3, [VM] * 4, [], 16, flops=edge_flops, aliases={1: 0},
    )
    tables = (along, odd, even)
    along = along_basin(to_next, "basin")
    odd = odd_or_even(to_odd, 1, "blk", "basin")
    even = odd_or_even(to_even, 0, "blk", "basin")
    (partial,) = call(
        middle_kernel, (state, operator, vt), [VM] * 3, [columns], [VM], [flat], 32, flops=operator_flops + vertical_flops,
    )
    out, _ = call(
        functools.partial(last_kernel, nedge), (odd, tables[1], arrived(along, even, tables[0], tables[2], partial), vt), [VM] * 4,
        [shape((levels, cols, width), BF16), columns], [HB, VM],
        [pltpu.VMEM((levels, cols, width), BF16), DMA((1 + -(-levels // 8),))], 16, flops=edge_flops, aliases={2: 1},
    )
    return jnp.transpose(out, (1, 0, 2))


def solution(mesh):
    in_specs = (
        P(("basin", "blk"), None, None),
        P(None, ("basin", "blk")),
        P(None, None, ("basin", "blk")),
        P(None, ("basin", "blk")),
        P(None, ("basin", "blk")),
        P(None, ("basin", "blk")),
        P(None, None, ("basin", "blk")),
        P(("basin", "blk")),
        P(None, None, ("basin", "blk")),
    )
    out_specs = P(("basin", "blk"), None, None)
    return jax.shard_map(local, mesh=mesh, in_specs=in_specs, out_specs=out_specs, check_vma=False)
```

```python
import functools

import jax
import jax.numpy as jnp
from jax import lax
from jax.experimental import pallas as pl
from jax.experimental.pallas import tpu as pltpu
from jax.sharding import PartitionSpec as P

NSTEP = 2
F32 = jnp.float32
BF16 = jnp.bfloat16


def padded(levels):
    return -(-levels // 8) * 8


def whole_rows(levels):
    return levels // 16 * 16


def message_rows(levels, nedge):
    return levels * nedge + 16


def direction(slot, parity):
    return lax.bitwise_xor(parity, jnp.int32(2 - slot)) if slot else 2


def has_partner(slot, at, count):
    first = lax.bitwise_and(at + slot // 2, jnp.int32(1)) == 1
    return jnp.where(first, at + 1 < count, at > 0)


def source_columns(weights, nedge):
    tables = [weights[0:nedge, 3 * nedge + 3 + slot : 3 * nedge + 4 + slot].astype(jnp.int32) for slot in range(3)]
    columns = [[table[e, 0] for e in range(nedge)] for table in tables]
    return lambda slot, e: columns[slot][e]


def pack_chunk(lo, levels, nedge, source, weights, rows_of, slots, outs):
    whole = whole_rows(levels)
    rest = levels - whole
    share = 8 // rest if rest else 0
    for slot, out in zip(slots, outs):
        if lo < whole:
            for e in range(nedge):
                k = slot * nedge + e
                value = rows_of(source(slot, e), lo, 16) * weights[lo : lo + 16, k : k + 1]
                out[e * whole + lo : e * whole + lo + 16, :] = value.astype(BF16)
            continue
        sub = lax.broadcasted_iota(jnp.int32, (8, out.shape[1]), 0)
        parts = []
        for first in range(0, nedge, share or nedge):
            part = None
            for q in range(share):
                k = slot * nedge + first + q
                value = rows_of(source(slot, first + q), lo, 8) * weights[lo : lo + 8, k : k + 1]
                if q:
                    value = pltpu.roll(value, q * rest, 0)
                part = value if part is None else jnp.where(sub >= q * rest, value, part)
            if share:
                parts.append(part)
        if out.shape[0] > levels * nedge:
            parts.append(jnp.broadcast_to(weights[0:16, 3 * nedge + slot : 3 * nedge + slot + 1], (16, out.shape[1])))
        if parts:
            out[nedge * whole :, :] = jnp.concatenate(parts, axis=0).astype(BF16)


def vertical(vt_ref, exs, out):
    cols, rows, _ = vt_ref.shape
    pad = jnp.zeros((64 - rows, out.shape[1]), F32)

    def column(j, _):
        at = pl.ds(pl.multiple_of(j * rows, 8), rows)
        x = jnp.concatenate([exs[at, :], pad], axis=0).astype(BF16)
        out[at, :] = jnp.dot(vt_ref[j][:, 0:64], x, preferred_element_type=F32)
        return _

    lax.fori_loop(0, cols, column, 0, unroll=16)


def add_edges(edges, levels, nedge, vt_ref, total):
    whole = whole_rows(levels)
    rest = levels - whole
    share = 8 // rest if rest else 0
    rows = vt_ref.shape[1]
    group = max(share, 4)
    pad = jnp.zeros((8, total.shape[1]), F32)
    for ref, first_ref in edges:
        table = first_ref[levels * nedge :, :].astype(F32).astype(jnp.int32)
        tails = ref[whole * nedge : levels * nedge, :].astype(F32) if rest else None
        for first in range(0, nedge, group):
            targets = [table[e, 0] for e in range(first, first + group)]
            products = []
            for e, j in zip(range(first, first + group), targets):
                x = ref[e * whole : (e + 1) * whole, :]
                if rest:
                    tail = tails[e // share * 8 : e // share * 8 + 8]
                    if e % share:
                        tail = pltpu.roll(tail, 8 - e % share * rest, 0)
                    x = jnp.concatenate([x, jnp.concatenate([tail, pad], axis=0).astype(BF16)], axis=0)
                products.append(jnp.dot(vt_ref[j][:, 0 : x.shape[0]], x, preferred_element_type=F32))
            for j, part in zip(targets, products):
                at = pl.ds(pl.multiple_of(j * rows, 8), rows)
                total[at, :] = total[at, :] + part


def gather_kernel(
    blk, c_h, send_h, recv_h, edge_h, nbr_h, nw_h, sw_h, wet_h,
    s0, s1, s2, c_v, nbr_v, nw_v, sw_v, wet_v, wts_o,
    cf, wts, recv_v, edge_v, send_v, sems,
):
    levels, cols, width = c_h.shape
    nedge = edge_h.shape[1]
    pitch = cols + 8
    bounds = [(lo, min(lo + 16, levels)) for lo in range(0, levels, 16)]
    pairs = [(send_h, send_v), (recv_h, recv_v), (edge_h, edge_v)]
    pairs += [(c_h.at[pl.ds(lo, hi - lo)], c_v.at[pl.ds(lo, hi - lo)]) for lo, hi in bounds]
    pairs += [(nbr_h, nbr_v), (nw_h, nw_v), (sw_h, sw_v), (wet_h, wet_v)]
    copies = [pltpu.make_async_copy(a, b, sems.at[i]) for i, (a, b) in enumerate(pairs)]
    for copy in copies:
        copy.start()
    parity = lax.bitwise_and(lax.axis_index(blk), jnp.int32(1))
    wts[...] = jnp.zeros_like(wts)
    for copy in copies[:3]:
        copy.wait()
    for slot in range(3):
        d = direction(slot, parity)
        weight = edge_v[d]
        if slot:
            weight = jnp.where(has_partner(slot, lax.axis_index(blk), lax.axis_size(blk)), weight, 0.0)
        wts[slot * nedge : (slot + 1) * nedge, 0:levels] = weight
        wts[3 * nedge + slot : 3 * nedge + slot + 1, 0:nedge] = recv_v[pl.ds(d, 1), :].astype(F32)
        wts[3 * nedge + 3 + slot : 3 * nedge + 4 + slot, 0:nedge] = send_v[pl.ds(d, 1), :].astype(F32)
    weights = wts[...].T
    wts_o[...] = weights
    source = source_columns(weights, nedge)
    rows_of = lambda s, lo, n: cf[pl.ds(lo * pitch + s, n, stride=pitch), :]
    for i, (lo, hi) in enumerate(bounds):
        copies[3 + i].wait()
        for l in range(lo, hi):
            cf[l * pitch : l * pitch + cols, :] = c_v[l].astype(F32)
        pack_chunk(lo, levels, nedge, source, weights, rows_of, (0, 1, 2), (s0, s1, s2))
    if levels % 16 == 0:
        pack_chunk(levels, levels, nedge, source, weights, rows_of, (0, 1, 2), (s0, s1, s2))
    for copy in copies[3 + len(bounds) :]:
        copy.wait()


def column_operator(nbr_ref, nw_ref, sw_ref, a_ref, merged):
    levels = nw_ref.shape[0]
    cols = nbr_ref.shape[1]
    nbr = nbr_ref.shape[0]
    lane = lax.broadcasted_iota(jnp.int32, (8, cols), 1)
    sub = lax.broadcasted_iota(jnp.int32, (8, cols), 0)
    target = jnp.where(sub == nbr, lane, -1)
    for n in range(nbr):
        target = jnp.where(sub == n, nbr_ref[n : n + 1, :], target)
    same = [(target == nbr_ref[n : n + 1, :]).astype(F32) for n in range(nbr)]
    same.append((target == lane).astype(F32))
    for l in range(levels):
        total = same[nbr] * sw_ref[l : l + 1, :]
        for n in range(nbr):
            total = total + same[n] * nw_ref[l, n : n + 1, :]
        merged[l] = total
    half = 16
    for jt in range(cols // half):
        j = lax.broadcasted_iota(jnp.int32, (half, cols), 0) + jt * half
        hits = [j == nbr_ref[n : n + 1, :] for n in range(nbr)]
        hits.append(j == lax.broadcasted_iota(jnp.int32, (half, cols), 1))

        def fill(p, _):
            for i in range(2):
                value = jnp.zeros((half, cols), F32)
                for n in range(nbr, -1, -1):
                    value = jnp.where(hits[n], merged[p * 2 + i, n : n + 1, :], value)
                a_ref[p, jt * half : (jt + 1) * half, i * cols : (i + 1) * cols] = value.astype(BF16)
            return _

        lax.fori_loop(0, levels // 2, fill, 0, unroll=5)


def level_products(a_ref, state_of, exs, rows):
    pairs, cols, _ = a_ref.shape
    width = exs.shape[1]
    zero = jnp.zeros((cols, width), BF16)
    for p in range(pairs):
        left = jnp.concatenate([state_of(2 * p), zero], axis=1)
        right = jnp.concatenate([zero, state_of(2 * p + 1)], axis=1)
        both = jnp.dot(a_ref[p], jnp.concatenate([left, right], axis=0), preferred_element_type=F32)
        exs[pl.ds(2 * p, cols, stride=rows), :] = both[:, 0:width]
        exs[pl.ds(2 * p + 1, cols, stride=rows), :] = both[:, width:]
    for l in range(2 * pairs, rows):
        exs[pl.ds(l, cols, stride=rows), :] = jnp.zeros((cols, width), F32)


def operator_kernel(
    c_ref, nbr_ref, nw_ref, sw_ref, wet_ref, v_h, a_ref, state_ref, vt_ref, exs, merged, vf, vts, v_ref, sem
):
    levels, cols, width = c_ref.shape
    rows = padded(levels)
    load = pltpu.make_async_copy(v_h, v_ref, sem)
    load.start()
    column_operator(nbr_ref, nw_ref, sw_ref, a_ref, merged)
    level_products(a_ref, lambda l: c_ref[l], exs, rows)
    level = lax.broadcasted_iota(jnp.int32, (levels, cols), 0)
    wet = wet_ref[...]
    load.wait()
    vf[...] = jnp.zeros_like(vf)
    for m in range(levels):
        keep = jnp.maximum(level, m) < wet
        vf[m * rows : m * rows + levels, :] = jnp.where(keep, v_ref[m].astype(F32), 0.0)
    for l in range(rows):
        block = vf[pl.ds(l, rows, stride=rows), :]
        block = jnp.concatenate([block, jnp.zeros((128 - rows, cols), F32)], axis=0)
        vts[pl.ds(l, cols, stride=rows), :] = block.T
    vt_ref[...] = vts[...].reshape(cols, rows, 128).astype(BF16)
    vertical(vt_ref, exs, state_ref)


def arrived_kernel(levels, nedge, r0, r2, t0, t2, local_ref, vt_ref, total):
    add_edges(((r0, t0), (r2, t2)), levels, nedge, vt_ref, total)


def send_kernel(levels, nedge, r1, local_ref, vt_ref, wts_ref, state, s0, s1, s2):
    rows = vt_ref.shape[1]
    add_edges(((r1, r1),), levels, nedge, vt_ref, state)
    source = source_columns(wts_ref, nedge)
    rows_of = lambda s, lo, n: state[pl.ds(pl.multiple_of(s * rows + lo, 8), n), :]
    for lo in range(0, levels + 1, 16):
        pack_chunk(lo, levels, nedge, source, wts_ref, rows_of, (0, 1, 2), (s0, s1, s2))


def middle_kernel(cs, a_ref, vt_ref, out_ref, exs):
    cols, rows, _ = vt_ref.shape
    level_products(a_ref, lambda l: cs[pl.ds(l, cols, stride=rows), :].astype(BF16), exs, rows)
    vertical(vt_ref, exs, out_ref)


def last_kernel(nedge, r1, t1, local_ref, vt_ref, out_h, total, out_v, sems):
    levels, cols, width = out_h.shape
    rows = vt_ref.shape[1]
    add_edges(((r1, t1),), levels, nedge, vt_ref, total)
    bounds = [0, *range(4, levels, 8), levels]
    copies = []
    for i, (lo, hi) in enumerate(zip(bounds, bounds[1:])):
        for l in range(lo, hi):
            out_v[l] = total[pl.ds(l, cols, stride=rows), :].astype(BF16)
        copies.append(pltpu.make_async_copy(out_v.at[pl.ds(lo, hi - lo)], out_h.at[pl.ds(lo, hi - lo)], sems.at[i]))
        copies[-1].start()
    for copy in copies:
        copy.wait()


VM = pl.BlockSpec(memory_space=pltpu.VMEM)
HB = pl.BlockSpec(memory_space=pltpu.HBM)
DMA = pltpu.SemaphoreType.DMA


def call(kernel, ins, specs, outs, out_specs, scratch, limit, flops=0, aliases=None):
    size = sum(x.size * x.dtype.itemsize for x in (*ins, *outs))
    return pl.pallas_call(
        kernel,
        out_shape=outs,
        in_specs=specs,
        out_specs=out_specs,
        scratch_shapes=scratch,
        input_output_aliases=aliases or {},
        compiler_params=pltpu.CompilerParams(vmem_limit_bytes=limit * 2**20),
        cost_estimate=pl.CostEstimate(flops=flops, bytes_accessed=size, transcendentals=0),
    )(*ins)


def odd_or_even(value, first, blk, basin):
    n, b = lax.axis_size(blk), lax.axis_size(basin)
    partner = {i: i + 1 for i in range(first, n - 1, 2)}
    partner |= {j: i for i, j in partner.items()}
    across = lambda g: g ^ 1 if g ^ 1 < b else g
    route = [(g * n + i, g * n + partner[i] if i in partner else across(g) * n + i) for g in range(b) for i in range(n)]
    return lax.ppermute(value, (basin, blk), route)


def along_basin(value, basin):
    b = lax.axis_size(basin)
    return lax.ppermute(value, basin, [(i, (i + 1) % b) for i in range(b)])


def local(tracers, nbr_cols, nbr_wts, self_wts, send_cols, recv_cols, edge_wts, wet_levels, vert_inv):
    cols, levels, width = tracers.shape
    rows = padded(levels)
    nedge = send_cols.shape[1]
    shape = jax.ShapeDtypeStruct
    by_level = jnp.transpose(tracers, (1, 0, 2))
    nbr_by_level = jnp.transpose(nbr_wts, (1, 0, 2))
    edge_by_entry = jnp.transpose(edge_wts, (0, 2, 1))
    wet = wet_levels.reshape(1, cols)
    in_hbm = lambda x: pltpu.with_memory_space_constraint(x, pltpu.HBM)
    send_h = in_hbm(send_cols)
    loads = [by_level, nbr_cols, nbr_by_level, self_wts, wet]
    same = lambda x: shape(x.shape, x.dtype)
    message = shape((message_rows(levels, nedge), width), BF16)
    columns = shape((cols * rows, width), F32)
    flat = pltpu.VMEM(columns.shape, F32)

    first = call(
        functools.partial(gather_kernel, "blk"),
        (in_hbm(by_level), send_h, *map(in_hbm, (recv_cols, edge_by_entry, *loads[1:]))),
        [HB] * 8,
        [message] * 3 + [same(x) for x in loads] + [shape((128, 128), F32)],
        [VM] * 9,
        [
            pltpu.VMEM((rows * (cols + 8), width), F32),
            pltpu.VMEM((128, 128), F32), pltpu.VMEM(recv_cols.shape, jnp.int32), pltpu.VMEM(edge_by_entry.shape, F32),
            pltpu.VMEM(send_cols.shape, jnp.int32), DMA((7 + -(-levels // 16),)),
        ],
        16,
    )
    (to_next, to_odd, to_even), loads, wts = first[:3], first[3:8], first[8]
    operator_flops = 2 * levels * cols * cols * width
    vertical_flops = 2 * cols * rows * rows * width

    edge_flops = nedge * 2 * rows * rows * width

    def arrived(along, even, along_table, even_table, partial):
        return call(
            functools.partial(arrived_kernel, levels, nedge), (along, even, along_table, even_table, partial, vt), [VM] * 6,
            [columns], [VM], [], 16, flops=2 * edge_flops, aliases={4: 0},
        )[0]

    along = along_basin(to_next, "basin")
    odd = odd_or_even(to_odd, 1, "blk", "basin")
    even = odd_or_even(to_even, 0, "blk", "basin")
    operator, partial, vt = call(
        operator_kernel, (*loads, in_hbm(vert_inv)), [VM] * 5 + [HB],
        [shape((levels // 2, cols, 2 * cols), BF16), columns, shape((cols, rows, 128), BF16)], [VM] * 3,
        [flat, pltpu.VMEM((levels, 8, cols), F32), pltpu.VMEM((rows * rows, cols), F32), pltpu.VMEM((cols * rows, 128), F32),
         pltpu.VMEM(vert_inv.shape, BF16), DMA],
        32, flops=operator_flops + vertical_flops,
    )
    state, to_next, to_odd, to_even = call(
        functools.partial(send_kernel, levels, nedge),
        (odd, arrived(along, even, along, even, partial), vt, wts), [VM] * 4,
        [columns] + [shape((levels * nedge, width), BF16)] * 3, [VM] * 4, [], 16, flops=edge_flops, aliases={1: 0},
    )
    tables = (along, odd, even)
    along = along_basin(to_next, "basin")
    odd = odd_or_even(to_odd, 1, "blk", "basin")
    even = odd_or_even(to_even, 0, "blk", "basin")
    (partial,) = call(
        middle_kernel, (state, operator, vt), [VM] * 3, [columns], [VM], [flat], 32, flops=operator_flops + vertical_flops,
    )
    out, _ = call(
        functools.partial(last_kernel, nedge), (odd, tables[1], arrived(along, even, tables[0], tables[2], partial), vt), [VM] * 4,
        [shape((levels, cols, width), BF16), columns], [HB, VM],
        [pltpu.VMEM((levels, cols, width), BF16), DMA((1 + -(-levels // 8),))], 16, flops=edge_flops, aliases={2: 1},
    )
    return jnp.transpose(out, (1, 0, 2))


def solution(mesh):
    in_specs = (
        P(("basin", "blk"), None, None),
        P(None, ("basin", "blk")),
        P(None, None, ("basin", "blk")),
        P(None, ("basin", "blk")),
        P(None, ("basin", "blk")),
        P(None, ("basin", "blk")),
        P(None, None, ("basin", "blk")),
        P(("basin", "blk")),
        P(None, None, ("basin", "blk")),
    )
    out_specs = P(("basin", "blk"), None, None)
    return jax.shard_map(local, mesh=mesh, in_specs=in_specs, out_specs=out_specs, check_vma=False)
```

```python
import functools

import jax
import jax.numpy as jnp
from jax import lax
from jax.experimental import pallas as pl
from jax.experimental.pallas import tpu as pltpu
from jax.sharding import PartitionSpec as P

NSTEP = 2
F32 = jnp.float32
BF16 = jnp.bfloat16


def padded(levels):
    return -(-levels // 8) * 8


def whole_rows(levels):
    return levels // 16 * 16


def message_rows(levels, nedge):
    return levels * nedge + 16


def direction(slot, parity):
    return lax.bitwise_xor(parity, jnp.int32(2 - slot)) if slot else 2


def has_partner(slot, at, count):
    first = lax.bitwise_and(at + slot // 2, jnp.int32(1)) == 1
    return jnp.where(first, at + 1 < count, at > 0)


def source_columns(weights, nedge):
    tables = [weights[0:nedge, 3 * nedge + 3 + slot : 3 * nedge + 4 + slot].astype(jnp.int32) for slot in range(3)]
    columns = [[table[e, 0] for e in range(nedge)] for table in tables]
    return lambda slot, e: columns[slot][e]


def pack_chunk(lo, levels, nedge, source, weights, rows_of, slots, outs):
    whole = whole_rows(levels)
    rest = levels - whole
    share = 8 // rest if rest else 0
    for slot, out in zip(slots, outs):
        if lo < whole:
            for e in range(nedge):
                k = slot * nedge + e
                value = rows_of(source(slot, e), lo, 16) * weights[lo : lo + 16, k : k + 1]
                out[e * whole + lo : e * whole + lo + 16, :] = value.astype(BF16)
            continue
        sub = lax.broadcasted_iota(jnp.int32, (8, out.shape[1]), 0)
        parts = []
        for first in range(0, nedge, share or nedge):
            part = None
            for q in range(share):
                k = slot * nedge + first + q
                value = rows_of(source(slot, first + q), lo, 8) * weights[lo : lo + 8, k : k + 1]
                if q:
                    value = pltpu.roll(value, q * rest, 0)
                part = value if part is None else jnp.where(sub >= q * rest, value, part)
            if share:
                parts.append(part)
        if out.shape[0] > levels * nedge:
            parts.append(jnp.broadcast_to(weights[0:16, 3 * nedge + slot : 3 * nedge + slot + 1], (16, out.shape[1])))
        if parts:
            out[nedge * whole :, :] = jnp.concatenate(parts, axis=0).astype(BF16)


def vertical(vt_ref, exs, out):
    cols, rows, _ = vt_ref.shape
    pad = jnp.zeros((64 - rows, out.shape[1]), F32)

    def column(j, _):
        at = pl.ds(pl.multiple_of(j * rows, 8), rows)
        x = jnp.concatenate([exs[at, :], pad], axis=0).astype(BF16)
        out[at, :] = jnp.dot(vt_ref[j][:, 0:64], x, preferred_element_type=F32)
        return _

    lax.fori_loop(0, cols, column, 0, unroll=16)


def add_edges(edges, levels, nedge, vt_ref, total, place=None):
    whole = whole_rows(levels)
    rest = levels - whole
    share = 8 // rest if rest else 0
    rows = vt_ref.shape[1]
    group = max(share, 4)
    pad = jnp.zeros((8, total.shape[1]), F32)
    for ref, first_ref in edges:
        table = first_ref[levels * nedge :, :].astype(F32).astype(jnp.int32)
        tails = ref[whole * nedge : levels * nedge, :].astype(F32) if rest else None
        for first in range(0, nedge, group):
            targets = [table[e, 0] for e in range(first, first + group)]
            products = []
            for e, j in zip(range(first, first + group), targets):
                x = ref[e * whole : (e + 1) * whole, :]
                if rest:
                    tail = tails[e // share * 8 : e // share * 8 + 8]
                    if e % share:
                        tail = pltpu.roll(tail, 8 - e % share * rest, 0)
                    x = jnp.concatenate([x, jnp.concatenate([tail, pad], axis=0).astype(BF16)], axis=0)
                products.append(jnp.dot(vt_ref[j][:, 0 : x.shape[0]], x, preferred_element_type=F32))
            for j, part in zip(targets, products):
                at = place(j) if place else pl.ds(pl.multiple_of(j * rows, 8), rows)
                total[at, :] = total[at, :] + part


def gather_kernel(
    blk, c_h, send_h, recv_h, edge_h, nbr_h, nw_h, sw_h, wet_h,
    s0, s1, s2, c_v, nbr_v, nw_v, sw_v, wet_v, wts_o,
    cf, wts, recv_v, edge_v, send_v, sems,
):
    levels, cols, width = c_h.shape
    nedge = edge_h.shape[1]
    pitch = cols + 8
    bounds = [(lo, min(lo + 16, levels)) for lo in range(0, levels, 16)]
    pairs = [(send_h, send_v), (recv_h, recv_v), (edge_h, edge_v)]
    pieces = [(lo, min(lo + 4, levels)) for lo in range(0, levels, 4)]
    pairs += [(c_h.at[pl.ds(lo, hi - lo)], c_v.at[pl.ds(lo, hi - lo)]) for lo, hi in pieces]
    pairs += [(nbr_h, nbr_v), (nw_h, nw_v), (sw_h, sw_v), (wet_h, wet_v)]
    copies = [pltpu.make_async_copy(a, b, sems.at[i]) for i, (a, b) in enumerate(pairs)]
    for copy in copies:
        copy.start()
    parity = lax.bitwise_and(lax.axis_index(blk), jnp.int32(1))
    wts[...] = jnp.zeros_like(wts)
    for copy in copies[:3]:
        copy.wait()
    for slot in range(3):
        d = direction(slot, parity)
        weight = edge_v[d]
        if slot:
            weight = jnp.where(has_partner(slot, lax.axis_index(blk), lax.axis_size(blk)), weight, 0.0)
        wts[slot * nedge : (slot + 1) * nedge, 0:levels] = weight
        wts[3 * nedge + slot : 3 * nedge + slot + 1, 0:nedge] = recv_v[pl.ds(d, 1), :].astype(F32)
        wts[3 * nedge + 3 + slot : 3 * nedge + 4 + slot, 0:nedge] = send_v[pl.ds(d, 1), :].astype(F32)
    weights = wts[...].T
    wts_o[...] = weights
    source = source_columns(weights, nedge)
    rows_of = lambda s, lo, n: cf[pl.ds(lo * pitch + s, n, stride=pitch), :]
    for lo, hi in bounds:
        for i, (first, last) in enumerate(pieces):
            if lo <= first < hi:
                copies[3 + i].wait()
                for l in range(first, last):
                    cf[l * pitch : l * pitch + cols, :] = c_v[l].astype(F32)
        pack_chunk(lo, levels, nedge, source, weights, rows_of, (0, 1, 2), (s0, s1, s2))
    if levels % 16 == 0:
        pack_chunk(levels, levels, nedge, source, weights, rows_of, (0, 1, 2), (s0, s1, s2))
    for copy in copies[3 + len(pieces) :]:
        copy.wait()


def column_operator(nbr_ref, nw_ref, sw_ref, a_ref, merged):
    levels = nw_ref.shape[0]
    cols = nbr_ref.shape[1]
    nbr = nbr_ref.shape[0]
    lane = lax.broadcasted_iota(jnp.int32, (8, cols), 1)
    sub = lax.broadcasted_iota(jnp.int32, (8, cols), 0)
    target = jnp.where(sub == nbr, lane, -1)
    for n in range(nbr):
        target = jnp.where(sub == n, nbr_ref[n : n + 1, :], target)
    same = [(target == nbr_ref[n : n + 1, :]).astype(F32) for n in range(nbr)]
    same.append((target == lane).astype(F32))
    for l in range(levels):
        total = same[nbr] * sw_ref[l : l + 1, :]
        for n in range(nbr):
            total = total + same[n] * nw_ref[l, n : n + 1, :]
        merged[l] = total
    half = 16
    for jt in range(cols // half):
        j = lax.broadcasted_iota(jnp.int32, (half, cols), 0) + jt * half
        hits = [j == nbr_ref[n : n + 1, :] for n in range(nbr)]
        hits.append(j == lax.broadcasted_iota(jnp.int32, (half, cols), 1))

        def fill(p, _):
            for i in range(2):
                value = jnp.zeros((half, cols), F32)
                for n in range(nbr, -1, -1):
                    value = jnp.where(hits[n], merged[p * 2 + i, n : n + 1, :], value)
                a_ref[p, jt * half : (jt + 1) * half, i * cols : (i + 1) * cols] = value.astype(BF16)
            return _

        lax.fori_loop(0, levels // 2, fill, 0, unroll=5)


def level_products(a_ref, state_of, exs, rows):
    pairs, cols, _ = a_ref.shape
    width = exs.shape[1]
    zero = jnp.zeros((cols, width), BF16)
    for p in range(pairs):
        left = jnp.concatenate([state_of(2 * p), zero], axis=1)
        right = jnp.concatenate([zero, state_of(2 * p + 1)], axis=1)
        both = jnp.dot(a_ref[p], jnp.concatenate([left, right], axis=0), preferred_element_type=F32)
        exs[pl.ds(2 * p, cols, stride=rows), :] = both[:, 0:width]
        exs[pl.ds(2 * p + 1, cols, stride=rows), :] = both[:, width:]
    for l in range(2 * pairs, rows):
        exs[pl.ds(l, cols, stride=rows), :] = jnp.zeros((cols, width), F32)


def operator_kernel(
    c_ref, nbr_ref, nw_ref, sw_ref, wet_ref, v_h, a_ref, state_ref, vt_ref, exs, merged, vf, vts, v_ref, sem
):
    levels, cols, width = c_ref.shape
    rows = padded(levels)
    load = pltpu.make_async_copy(v_h, v_ref, sem)
    load.start()
    column_operator(nbr_ref, nw_ref, sw_ref, a_ref, merged)
    level_products(a_ref, lambda l: c_ref[l], exs, rows)
    level = lax.broadcasted_iota(jnp.int32, (levels, cols), 0)
    wet = wet_ref[...]
    load.wait()
    vf[...] = jnp.zeros_like(vf)
    for m in range(levels):
        keep = jnp.maximum(level, m) < wet
        vf[m * rows : m * rows + levels, :] = jnp.where(keep, v_ref[m].astype(F32), 0.0)
    for l in range(rows):
        block = vf[pl.ds(l, rows, stride=rows), :]
        block = jnp.concatenate([block, jnp.zeros((128 - rows, cols), F32)], axis=0)
        vts[pl.ds(l, cols, stride=rows), :] = block.T
    vt_ref[...] = vts[...].reshape(cols, rows, 128).astype(BF16)
    vertical(vt_ref, exs, state_ref)


def arrived_kernel(levels, nedge, r0, r2, t0, t2, local_ref, vt_ref, total):
    add_edges(((r0, t0), (r2, t2)), levels, nedge, vt_ref, total)


def turned_kernel(levels, nedge, r0, r2, t0, t2, local_ref, vt_ref, total, by_level):
    cols, rows, _ = vt_ref.shape
    pitch = cols + 8
    add_edges(((r0, t0), (r2, t2)), levels, nedge, vt_ref, total)
    for l in range(rows):
        by_level[l * pitch : l * pitch + cols, :] = total[pl.ds(l, cols, stride=rows), :]


def send_kernel(levels, nedge, r1, local_ref, vt_ref, wts_ref, state, s0, s1, s2):
    rows = vt_ref.shape[1]
    add_edges(((r1, r1),), levels, nedge, vt_ref, state)
    source = source_columns(wts_ref, nedge)
    rows_of = lambda s, lo, n: state[pl.ds(pl.multiple_of(s * rows + lo, 8), n), :]
    for lo in range(0, levels + 1, 16):
        pack_chunk(lo, levels, nedge, source, wts_ref, rows_of, (0, 1, 2), (s0, s1, s2))


def middle_kernel(cs, a_ref, vt_ref, out_ref, exs):
    cols, rows, _ = vt_ref.shape
    level_products(a_ref, lambda l: cs[pl.ds(l, cols, stride=rows), :].astype(BF16), exs, rows)
    vertical(vt_ref, exs, out_ref)


def last_kernel(nedge, r1, t1, local_ref, vt_ref, out_h, by_level, out_v, sems):
    levels, cols, width = out_h.shape
    rows = vt_ref.shape[1]
    pitch = cols + 8
    add_edges(((r1, t1),), levels, nedge, vt_ref, by_level, lambda j: pl.ds(j, rows, stride=pitch))
    bounds = [0, *range(4, levels, 8), levels]
    copies = []
    for i, (lo, hi) in enumerate(zip(bounds, bounds[1:])):
        for l in range(lo, hi):
            out_v[l] = by_level[l * pitch : l * pitch + cols, :].astype(BF16)
        copies.append(pltpu.make_async_copy(out_v.at[pl.ds(lo, hi - lo)], out_h.at[pl.ds(lo, hi - lo)], sems.at[i]))
        copies[-1].start()
    for copy in copies:
        copy.wait()


VM = pl.BlockSpec(memory_space=pltpu.VMEM)
HB = pl.BlockSpec(memory_space=pltpu.HBM)
DMA = pltpu.SemaphoreType.DMA


def call(kernel, ins, specs, outs, out_specs, scratch, limit, flops=0, aliases=None):
    size = sum(x.size * x.dtype.itemsize for x in (*ins, *outs))
    return pl.pallas_call(
        kernel,
        out_shape=outs,
        in_specs=specs,
        out_specs=out_specs,
        scratch_shapes=scratch,
        input_output_aliases=aliases or {},
        compiler_params=pltpu.CompilerParams(vmem_limit_bytes=limit * 2**20),
        cost_estimate=pl.CostEstimate(flops=flops, bytes_accessed=size, transcendentals=0),
    )(*ins)


def odd_or_even(value, first, blk, basin):
    n, b = lax.axis_size(blk), lax.axis_size(basin)
    partner = {i: i + 1 for i in range(first, n - 1, 2)}
    partner |= {j: i for i, j in partner.items()}
    across = lambda g: g ^ 1 if g ^ 1 < b else g
    route = [(g * n + i, g * n + partner[i] if i in partner else across(g) * n + i) for g in range(b) for i in range(n)]
    return lax.ppermute(value, (basin, blk), route)


def along_basin(value, basin):
    b = lax.axis_size(basin)
    return lax.ppermute(value, basin, [(i, (i + 1) % b) for i in range(b)])


def local(tracers, nbr_cols, nbr_wts, self_wts, send_cols, recv_cols, edge_wts, wet_levels, vert_inv):
    cols, levels, width = tracers.shape
    rows = padded(levels)
    nedge = send_cols.shape[1]
    shape = jax.ShapeDtypeStruct
    by_level = jnp.transpose(tracers, (1, 0, 2))
    nbr_by_level = jnp.transpose(nbr_wts, (1, 0, 2))
    edge_by_entry = jnp.transpose(edge_wts, (0, 2, 1))
    wet = wet_levels.reshape(1, cols)
    in_hbm = lambda x: pltpu.with_memory_space_constraint(x, pltpu.HBM)
    send_h = in_hbm(send_cols)
    loads = [by_level, nbr_cols, nbr_by_level, self_wts, wet]
    same = lambda x: shape(x.shape, x.dtype)
    message = shape((message_rows(levels, nedge), width), BF16)
    columns = shape((cols * rows, width), F32)
    flat = pltpu.VMEM(columns.shape, F32)

    first = call(
        functools.partial(gather_kernel, "blk"),
        (in_hbm(by_level), send_h, *map(in_hbm, (recv_cols, edge_by_entry, *loads[1:]))),
        [HB] * 8,
        [message] * 3 + [same(x) for x in loads] + [shape((128, 128), F32)],
        [VM] * 9,
        [
            pltpu.VMEM((rows * (cols + 8), width), F32),
            pltpu.VMEM((128, 128), F32), pltpu.VMEM(recv_cols.shape, jnp.int32), pltpu.VMEM(edge_by_entry.shape, F32),
            pltpu.VMEM(send_cols.shape, jnp.int32), DMA((7 + -(-levels // 4),)),
        ],
        16,
    )
    (to_next, to_odd, to_even), loads, wts = first[:3], first[3:8], first[8]
    operator_flops = 2 * levels * cols * cols * width
    vertical_flops = 2 * cols * rows * rows * width

    edge_flops = nedge * 2 * rows * rows * width

    along = along_basin(to_next, "basin")
    odd = odd_or_even(to_odd, 1, "blk", "basin")
    even = odd_or_even(to_even, 0, "blk", "basin")
    operator, partial, vt = call(
        operator_kernel, (*loads, in_hbm(vert_inv)), [VM] * 5 + [HB],
        [shape((levels // 2, cols, 2 * cols), BF16), columns, shape((cols, rows, 128), BF16)], [VM] * 3,
        [flat, pltpu.VMEM((levels, 8, cols), F32), pltpu.VMEM((rows * rows, cols), F32), pltpu.VMEM((cols * rows, 128), F32),
         pltpu.VMEM(vert_inv.shape, BF16), DMA],
        32, flops=operator_flops + vertical_flops,
    )
    (partial,) = call(
        functools.partial(arrived_kernel, levels, nedge), (along, even, along, even, partial, vt), [VM] * 6,
        [columns], [VM], [], 16, flops=2 * edge_flops, aliases={4: 0},
    )
    state, to_next, to_odd, to_even = call(
        functools.partial(send_kernel, levels, nedge),
        (odd, partial, vt, wts), [VM] * 4,
        [columns] + [shape((levels * nedge, width), BF16)] * 3, [VM] * 4, [], 16, flops=edge_flops, aliases={1: 0},
    )
    tables = (along, odd, even)
    along = along_basin(to_next, "basin")
    odd = odd_or_even(to_odd, 1, "blk", "basin")
    even = odd_or_even(to_even, 0, "blk", "basin")
    (partial,) = call(
        middle_kernel, (state, operator, vt), [VM] * 3, [columns], [VM], [flat], 32, flops=operator_flops + vertical_flops,
    )
    turned = shape((rows * (cols + 8), width), F32)
    _, by_level = call(
        functools.partial(turned_kernel, levels, nedge), (along, even, tables[0], tables[2], partial, vt), [VM] * 6,
        [columns, turned], [VM] * 2, [], 16, flops=2 * edge_flops, aliases={4: 0},
    )
    out, _ = call(
        functools.partial(last_kernel, nedge), (odd, tables[1], by_level, vt), [VM] * 4,
        [shape((levels, cols, width), BF16), turned], [HB, VM],
        [pltpu.VMEM((levels, cols, width), BF16), DMA((1 + -(-levels // 8),))], 16, flops=edge_flops, aliases={2: 1},
    )
    return jnp.transpose(out, (1, 0, 2))


def solution(mesh):
    in_specs = (
        P(("basin", "blk"), None, None),
        P(None, ("basin", "blk")),
        P(None, None, ("basin", "blk")),
        P(None, ("basin", "blk")),
        P(None, ("basin", "blk")),
        P(None, ("basin", "blk")),
        P(None, None, ("basin", "blk")),
        P(("basin", "blk")),
        P(None, None, ("basin", "blk")),
    )
    out_specs = P(("basin", "blk"), None, None)
    return jax.shard_map(local, mesh=mesh, in_specs=in_specs, out_specs=out_specs, check_vma=False)
```

```python
import functools

import jax
import jax.numpy as jnp
from jax import lax
from jax.experimental import pallas as pl
from jax.experimental.pallas import tpu as pltpu
from jax.sharding import PartitionSpec as P

NSTEP = 2
F32 = jnp.float32
BF16 = jnp.bfloat16


def padded(levels):
    return -(-levels // 8) * 8


def whole_rows(levels):
    return levels // 16 * 16


def message_rows(levels, nedge):
    return levels * nedge + 16


def direction(slot, parity):
    return lax.bitwise_xor(parity, jnp.int32(2 - slot)) if slot else 2


def has_partner(slot, at, count):
    first = lax.bitwise_and(at + slot // 2, jnp.int32(1)) == 1
    return jnp.where(first, at + 1 < count, at > 0)


def source_columns(weights, nedge):
    tables = [weights[0:nedge, 3 * nedge + 3 + slot : 3 * nedge + 4 + slot].astype(jnp.int32) for slot in range(3)]
    columns = [[table[e, 0] for e in range(nedge)] for table in tables]
    return lambda slot, e: columns[slot][e]


def pack_chunk(lo, levels, nedge, source, weights, rows_of, slots, outs):
    whole = whole_rows(levels)
    rest = levels - whole
    share = 8 // rest if rest else 0
    for slot, out in zip(slots, outs):
        if lo < whole:
            for e in range(nedge):
                k = slot * nedge + e
                value = rows_of(source(slot, e), lo, 16) * weights[lo : lo + 16, k : k + 1]
                out[e * whole + lo : e * whole + lo + 16, :] = value.astype(BF16)
            continue
        sub = lax.broadcasted_iota(jnp.int32, (8, out.shape[1]), 0)
        parts = []
        for first in range(0, nedge, share or nedge):
            part = None
            for q in range(share):
                k = slot * nedge + first + q
                value = rows_of(source(slot, first + q), lo, 8) * weights[lo : lo + 8, k : k + 1]
                if q:
                    value = pltpu.roll(value, q * rest, 0)
                part = value if part is None else jnp.where(sub >= q * rest, value, part)
            if share:
                parts.append(part)
        if out.shape[0] > levels * nedge:
            parts.append(jnp.broadcast_to(weights[0:16, 3 * nedge + slot : 3 * nedge + slot + 1], (16, out.shape[1])))
        if parts:
            out[nedge * whole :, :] = jnp.concatenate(parts, axis=0).astype(BF16)


def vertical(vt_ref, exs, out):
    cols, rows, _ = vt_ref.shape
    pad = jnp.zeros((64 - rows, out.shape[1]), F32)

    def column(j, _):
        at = pl.ds(pl.multiple_of(j * rows, 8), rows)
        x = jnp.concatenate([exs[at, :], pad], axis=0).astype(BF16)
        out[at, :] = jnp.dot(vt_ref[j][:, 0:64], x, preferred_element_type=F32)
        return _

    lax.fori_loop(0, cols, column, 0, unroll=16)


def add_edges(edges, levels, nedge, vt_ref, total):
    whole = whole_rows(levels)
    rest = levels - whole
    share = 8 // rest if rest else 0
    rows = vt_ref.shape[1]
    group = max(share, 4)
    pad = jnp.zeros((8, total.shape[1]), F32)
    for ref, first_ref in edges:
        table = first_ref[levels * nedge :, :].astype(F32).astype(jnp.int32)
        tails = ref[whole * nedge : levels * nedge, :].astype(F32) if rest else None
        for first in range(0, nedge, group):
            targets = [table[e, 0] for e in range(first, first + group)]
            products = []
            for e, j in zip(range(first, first + group), targets):
                x = ref[e * whole : (e + 1) * whole, :]
                if rest:
                    tail = tails[e // share * 8 : e // share * 8 + 8]
                    if e % share:
                        tail = pltpu.roll(tail, 8 - e % share * rest, 0)
                    x = jnp.concatenate([x, jnp.concatenate([tail, pad], axis=0).astype(BF16)], axis=0)
                products.append(jnp.dot(vt_ref[j][:, 0 : x.shape[0]], x, preferred_element_type=F32))
            for j, part in zip(targets, products):
                at = pl.ds(pl.multiple_of(j * rows, 8), rows)
                total[at, :] = total[at, :] + part


def gather_kernel(
    blk, c_h, send_h, recv_h, edge_h, nbr_h, nw_h, sw_h, wet_h,
    s0, s1, s2, c_v, nbr_v, nw_v, sw_v, wet_v, wts_o,
    cf, wts, recv_v, edge_v, send_v, sems,
):
    levels, cols, width = c_h.shape
    nedge = edge_h.shape[1]
    pitch = cols + 8
    whole = whole_rows(levels)
    bounds = [(lo, lo + 16 if lo + 16 < whole else levels) for lo in range(0, whole, 16)]
    pairs = [(c_h.at[pl.ds(lo, hi - lo)], c_v.at[pl.ds(lo, hi - lo)]) for lo, hi in bounds]
    tracer_copies = len(pairs)
    pairs += [(send_h, send_v), (recv_h, recv_v), (edge_h, edge_v)]
    pairs += [(nbr_h, nbr_v), (nw_h, nw_v), (sw_h, sw_v), (wet_h, wet_v)]
    copies = [pltpu.make_async_copy(a, b, sems.at[i]) for i, (a, b) in enumerate(pairs)]
    for copy in copies:
        copy.start()
    parity = lax.bitwise_and(lax.axis_index(blk), jnp.int32(1))
    wts[...] = jnp.zeros_like(wts)
    for copy in copies[tracer_copies : tracer_copies + 3]:
        copy.wait()
    for slot in range(3):
        d = direction(slot, parity)
        weight = edge_v[d]
        if slot:
            weight = jnp.where(has_partner(slot, lax.axis_index(blk), lax.axis_size(blk)), weight, 0.0)
        wts[slot * nedge : (slot + 1) * nedge, 0:levels] = weight
        wts[3 * nedge + slot : 3 * nedge + slot + 1, 0:nedge] = recv_v[pl.ds(d, 1), :].astype(F32)
        wts[3 * nedge + 3 + slot : 3 * nedge + 4 + slot, 0:nedge] = send_v[pl.ds(d, 1), :].astype(F32)
    weights = wts[...].T
    wts_o[...] = weights
    source = source_columns(weights, nedge)
    rows_of = lambda s, lo, n: cf[pl.ds(lo * pitch + s, n, stride=pitch), :]
    for i, (lo, hi) in enumerate(bounds):
        copies[i].wait()
        for l in range(lo, hi):
            cf[l * pitch : l * pitch + cols, :] = c_v[l].astype(F32)
        pack_chunk(lo, levels, nedge, source, weights, rows_of, (0, 1, 2), (s0, s1, s2))
    pack_chunk(whole, levels, nedge, source, weights, rows_of, (0, 1, 2), (s0, s1, s2))
    for copy in copies[tracer_copies + 3 :]:
        copy.wait()


def column_operator(nbr_ref, nw_ref, sw_ref, a_ref, merged):
    levels = nw_ref.shape[0]
    cols = nbr_ref.shape[1]
    nbr = nbr_ref.shape[0]
    lane = lax.broadcasted_iota(jnp.int32, (8, cols), 1)
    sub = lax.broadcasted_iota(jnp.int32, (8, cols), 0)
    target = jnp.where(sub == nbr, lane, -1)
    for n in range(nbr):
        target = jnp.where(sub == n, nbr_ref[n : n + 1, :], target)
    same = [(target == nbr_ref[n : n + 1, :]).astype(F32) for n in range(nbr)]
    same.append((target == lane).astype(F32))
    for l in range(levels):
        total = same[nbr] * sw_ref[l : l + 1, :]
        for n in range(nbr):
            total = total + same[n] * nw_ref[l, n : n + 1, :]
        merged[l] = total
    half = 16
    for jt in range(cols // half):
        j = lax.broadcasted_iota(jnp.int32, (half, cols), 0) + jt * half
        hits = [j == nbr_ref[n : n + 1, :] for n in range(nbr)]
        hits.append(j == lax.broadcasted_iota(jnp.int32, (half, cols), 1))

        def fill(p, _):
            for i in range(2):
                value = jnp.zeros((half, cols), F32)
                for n in range(nbr, -1, -1):
                    value = jnp.where(hits[n], merged[p * 2 + i, n : n + 1, :], value)
                a_ref[p, jt * half : (jt + 1) * half, i * cols : (i + 1) * cols] = value.astype(BF16)
            return _

        lax.fori_loop(0, levels // 2, fill, 0, unroll=5)


def level_products(a_ref, state_of, exs, rows):
    pairs, cols, _ = a_ref.shape
    width = exs.shape[1]
    zero = jnp.zeros((cols, width), BF16)
    for p in range(pairs):
        left = jnp.concatenate([state_of(2 * p), zero], axis=1)
        right = jnp.concatenate([zero, state_of(2 * p + 1)], axis=1)
        both = jnp.dot(a_ref[p], jnp.concatenate([left, right], axis=0), preferred_element_type=F32)
        exs[pl.ds(2 * p, cols, stride=rows), :] = both[:, 0:width]
        exs[pl.ds(2 * p + 1, cols, stride=rows), :] = both[:, width:]
    for l in range(2 * pairs, rows):
        exs[pl.ds(l, cols, stride=rows), :] = jnp.zeros((cols, width), F32)


def operator_kernel(
    c_ref, nbr_ref, nw_ref, sw_ref, wet_ref, v_h, a_ref, state_ref, vt_ref, exs, merged, vf, vts, v_ref, sem
):
    levels, cols, width = c_ref.shape
    rows = padded(levels)
    load = pltpu.make_async_copy(v_h, v_ref, sem)
    load.start()
    column_operator(nbr_ref, nw_ref, sw_ref, a_ref, merged)
    level_products(a_ref, lambda l: c_ref[l], exs, rows)
    level = lax.broadcasted_iota(jnp.int32, (levels, cols), 0)
    wet = wet_ref[...]
    load.wait()
    vf[...] = jnp.zeros_like(vf)
    for m in range(levels):
        keep = jnp.maximum(level, m) < wet
        vf[m * rows : m * rows + levels, :] = jnp.where(keep, v_ref[m].astype(F32), 0.0)
    for l in range(rows):
        block = vf[pl.ds(l, rows, stride=rows), :]
        block = jnp.concatenate([block, jnp.zeros((128 - rows, cols), F32)], axis=0)
        vts[pl.ds(l, cols, stride=rows), :] = block.T
    vt_ref[...] = vts[...].reshape(cols, rows, 128).astype(BF16)
    vertical(vt_ref, exs, state_ref)


def arrived_kernel(levels, nedge, r0, r2, t0, t2, local_ref, vt_ref, total):
    add_edges(((r0, t0), (r2, t2)), levels, nedge, vt_ref, total)


def send_kernel(levels, nedge, r1, local_ref, vt_ref, wts_ref, state, s0, s1, s2):
    rows = vt_ref.shape[1]
    add_edges(((r1, r1),), levels, nedge, vt_ref, state)
    source = source_columns(wts_ref, nedge)
    rows_of = lambda s, lo, n: state[pl.ds(pl.multiple_of(s * rows + lo, 8), n), :]
    for lo in range(0, levels + 1, 16):
        pack_chunk(lo, levels, nedge, source, wts_ref, rows_of, (0, 1, 2), (s0, s1, s2))


def middle_kernel(cs, a_ref, vt_ref, out_ref, exs):
    cols, rows, _ = vt_ref.shape
    level_products(a_ref, lambda l: cs[pl.ds(l, cols, stride=rows), :].astype(BF16), exs, rows)
    vertical(vt_ref, exs, out_ref)


def last_kernel(nedge, r1, t1, local_ref, vt_ref, out_h, total, out_v, sems):
    levels, cols, width = out_h.shape
    rows = vt_ref.shape[1]
    add_edges(((r1, t1),), levels, nedge, vt_ref, total)
    bounds = [0, *range(4, levels, 8), levels]
    copies = []
    for i, (lo, hi) in enumerate(zip(bounds, bounds[1:])):
        for l in range(lo, hi):
            out_v[l] = total[pl.ds(l, cols, stride=rows), :].astype(BF16)
        copies.append(pltpu.make_async_copy(out_v.at[pl.ds(lo, hi - lo)], out_h.at[pl.ds(lo, hi - lo)], sems.at[i]))
        copies[-1].start()
    for copy in copies:
        copy.wait()


VM = pl.BlockSpec(memory_space=pltpu.VMEM)
HB = pl.BlockSpec(memory_space=pltpu.HBM)
DMA = pltpu.SemaphoreType.DMA


def call(kernel, ins, specs, outs, out_specs, scratch, limit, flops=0, aliases=None):
    size = sum(x.size * x.dtype.itemsize for x in (*ins, *outs))
    return pl.pallas_call(
        kernel,
        out_shape=outs,
        in_specs=specs,
        out_specs=out_specs,
        scratch_shapes=scratch,
        input_output_aliases=aliases or {},
        compiler_params=pltpu.CompilerParams(vmem_limit_bytes=limit * 2**20),
        cost_estimate=pl.CostEstimate(flops=flops, bytes_accessed=size, transcendentals=0),
    )(*ins)


def odd_or_even(value, first, blk, basin):
    n, b = lax.axis_size(blk), lax.axis_size(basin)
    partner = {i: i + 1 for i in range(first, n - 1, 2)}
    partner |= {j: i for i, j in partner.items()}
    across = lambda g: g ^ 1 if g ^ 1 < b else g
    route = [(g * n + i, g * n + partner[i] if i in partner else across(g) * n + i) for g in range(b) for i in range(n)]
    return lax.ppermute(value, (basin, blk), route)


def along_basin(value, basin):
    b = lax.axis_size(basin)
    return lax.ppermute(value, basin, [(i, (i + 1) % b) for i in range(b)])


def local(tracers, nbr_cols, nbr_wts, self_wts, send_cols, recv_cols, edge_wts, wet_levels, vert_inv):
    cols, levels, width = tracers.shape
    rows = padded(levels)
    nedge = send_cols.shape[1]
    shape = jax.ShapeDtypeStruct
    by_level = jnp.transpose(tracers, (1, 0, 2))
    nbr_by_level = jnp.transpose(nbr_wts, (1, 0, 2))
    edge_by_entry = jnp.transpose(edge_wts, (0, 2, 1))
    wet = wet_levels.reshape(1, cols)
    in_hbm = lambda x: pltpu.with_memory_space_constraint(x, pltpu.HBM)
    send_h = in_hbm(send_cols)
    loads = [by_level, nbr_cols, nbr_by_level, self_wts, wet]
    same = lambda x: shape(x.shape, x.dtype)
    message = shape((message_rows(levels, nedge), width), BF16)
    columns = shape((cols * rows, width), F32)
    flat = pltpu.VMEM(columns.shape, F32)

    first = call(
        functools.partial(gather_kernel, "blk"),
        (in_hbm(by_level), send_h, *map(in_hbm, (recv_cols, edge_by_entry, *loads[1:]))),
        [HB] * 8,
        [message] * 3 + [same(x) for x in loads] + [shape((128, 128), F32)],
        [VM] * 9,
        [
            pltpu.VMEM((rows * (cols + 8), width), F32),
            pltpu.VMEM((128, 128), F32), pltpu.VMEM(recv_cols.shape, jnp.int32), pltpu.VMEM(edge_by_entry.shape, F32),
            pltpu.VMEM(send_cols.shape, jnp.int32), DMA((7 + -(-levels // 16),)),
        ],
        16,
    )
    (to_next, to_odd, to_even), loads, wts = first[:3], first[3:8], first[8]
    operator_flops = 2 * levels * cols * cols * width
    vertical_flops = 2 * cols * rows * rows * width

    edge_flops = nedge * 2 * rows * rows * width

    def arrived(along, even, along_table, even_table, partial):
        return call(
            functools.partial(arrived_kernel, levels, nedge), (along, even, along_table, even_table, partial, vt), [VM] * 6,
            [columns], [VM], [], 16, flops=2 * edge_flops, aliases={4: 0},
        )[0]

    along = along_basin(to_next, "basin")
    odd = odd_or_even(to_odd, 1, "blk", "basin")
    even = odd_or_even(to_even, 0, "blk", "basin")
    operator, partial, vt = call(
        operator_kernel, (*loads, in_hbm(vert_inv)), [VM] * 5 + [HB],
        [shape((levels // 2, cols, 2 * cols), BF16), columns, shape((cols, rows, 128), BF16)], [VM] * 3,
        [flat, pltpu.VMEM((levels, 8, cols), F32), pltpu.VMEM((rows * rows, cols), F32), pltpu.VMEM((cols * rows, 128), F32),
         pltpu.VMEM(vert_inv.shape, BF16), DMA],
        32, flops=operator_flops + vertical_flops,
    )
    state, to_next, to_odd, to_even = call(
        functools.partial(send_kernel, levels, nedge),
        (odd, arrived(along, even, along, even, partial), vt, wts), [VM] * 4,
        [columns] + [shape((levels * nedge, width), BF16)] * 3, [VM] * 4, [], 16, flops=edge_flops, aliases={1: 0},
    )
    tables = (along, odd, even)
    along = along_basin(to_next, "basin")
    odd = odd_or_even(to_odd, 1, "blk", "basin")
    even = odd_or_even(to_even, 0, "blk", "basin")
    (partial,) = call(
        middle_kernel, (state, operator, vt), [VM] * 3, [columns], [VM], [flat], 32, flops=operator_flops + vertical_flops,
    )
    out, _ = call(
        functools.partial(last_kernel, nedge), (odd, tables[1], arrived(along, even, tables[0], tables[2], partial), vt), [VM] * 4,
        [shape((levels, cols, width), BF16), columns], [HB, VM],
        [pltpu.VMEM((levels, cols, width), BF16), DMA((1 + -(-levels // 8),))], 16, flops=edge_flops, aliases={2: 1},
    )
    return jnp.transpose(out, (1, 0, 2))


def solution(mesh):
    in_specs = (
        P(("basin", "blk"), None, None),
        P(None, ("basin", "blk")),
        P(None, None, ("basin", "blk")),
        P(None, ("basin", "blk")),
        P(None, ("basin", "blk")),
        P(None, ("basin", "blk")),
        P(None, None, ("basin", "blk")),
        P(("basin", "blk")),
        P(None, None, ("basin", "blk")),
    )
    out_specs = P(("basin", "blk"), None, None)
    return jax.shard_map(local, mesh=mesh, in_specs=in_specs, out_specs=out_specs, check_vma=False)
```

```python
import functools

import jax
import jax.numpy as jnp
from jax import lax
from jax.experimental import pallas as pl
from jax.experimental.pallas import tpu as pltpu
from jax.sharding import PartitionSpec as P

NSTEP = 2
F32 = jnp.float32
BF16 = jnp.bfloat16


def padded(levels):
    return -(-levels // 8) * 8


def whole_rows(levels):
    return levels // 16 * 16


def message_rows(levels, nedge):
    return levels * nedge + 16


def direction(slot, parity):
    return lax.bitwise_xor(parity, jnp.int32(2 - slot)) if slot else 2


def has_partner(slot, at, count):
    first = lax.bitwise_and(at + slot // 2, jnp.int32(1)) == 1
    return jnp.where(first, at + 1 < count, at > 0)


def source_columns(weights, nedge):
    tables = [weights[0:nedge, 3 * nedge + 3 + slot : 3 * nedge + 4 + slot].astype(jnp.int32) for slot in range(3)]
    columns = [[table[e, 0] for e in range(nedge)] for table in tables]
    return lambda slot, e: columns[slot][e]


def pack_chunk(lo, levels, nedge, source, weights, rows_of, slots, outs):
    whole = whole_rows(levels)
    rest = levels - whole
    share = 8 // rest if rest else 0
    for slot, out in zip(slots, outs):
        if lo < whole:
            for e in range(nedge):
                k = slot * nedge + e
                value = rows_of(source(slot, e), lo, 16) * weights[lo : lo + 16, k : k + 1]
                out[e * whole + lo : e * whole + lo + 16, :] = value.astype(BF16)
            continue
        sub = lax.broadcasted_iota(jnp.int32, (8, out.shape[1]), 0)
        parts = []
        for first in range(0, nedge, share or nedge):
            part = None
            for q in range(share):
                k = slot * nedge + first + q
                value = rows_of(source(slot, first + q), lo, 8) * weights[lo : lo + 8, k : k + 1]
                if q:
                    value = pltpu.roll(value, q * rest, 0)
                part = value if part is None else jnp.where(sub >= q * rest, value, part)
            if share:
                parts.append(part)
        if out.shape[0] > levels * nedge:
            parts.append(jnp.broadcast_to(weights[0:16, 3 * nedge + slot : 3 * nedge + slot + 1], (16, out.shape[1])))
        if parts:
            out[nedge * whole :, :] = jnp.concatenate(parts, axis=0).astype(BF16)


def vertical(vt_ref, exs, out):
    cols, rows, _ = vt_ref.shape
    pad = jnp.zeros((64 - rows, out.shape[1]), F32)

    def column(j, _):
        at = pl.ds(pl.multiple_of(j * rows, 8), rows)
        x = jnp.concatenate([exs[at, :], pad], axis=0).astype(BF16)
        out[at, :] = jnp.dot(vt_ref[j][:, 0:64], x, preferred_element_type=F32)
        return _

    lax.fori_loop(0, cols, column, 0, unroll=16)


def add_edges(edges, levels, nedge, vt_ref, total):
    whole = whole_rows(levels)
    rest = levels - whole
    share = 8 // rest if rest else 0
    rows = vt_ref.shape[1]
    group = max(share, 4)
    pad = jnp.zeros((8, total.shape[1]), F32)
    for ref, first_ref in edges:
        table = first_ref[levels * nedge :, :].astype(F32).astype(jnp.int32)
        tails = ref[whole * nedge : levels * nedge, :].astype(F32) if rest else None
        for first in range(0, nedge, group):
            targets = [table[e, 0] for e in range(first, first + group)]
            products = []
            for e, j in zip(range(first, first + group), targets):
                x = ref[e * whole : (e + 1) * whole, :]
                if rest:
                    tail = tails[e // share * 8 : e // share * 8 + 8]
                    if e % share:
                        tail = pltpu.roll(tail, 8 - e % share * rest, 0)
                    x = jnp.concatenate([x, jnp.concatenate([tail, pad], axis=0).astype(BF16)], axis=0)
                products.append(jnp.dot(vt_ref[j][:, 0 : x.shape[0]], x, preferred_element_type=F32))
            for j, part in zip(targets, products):
                at = pl.ds(pl.multiple_of(j * rows, 8), rows)
                total[at, :] = total[at, :] + part


def gather_kernel(
    blk, c_h, send_h, recv_h, edge_h, s0, s1, s2, c_v, wts_o,
    cf, wts, recv_v, edge_v, send_v, sems,
):
    levels, cols, width = c_h.shape
    nedge = edge_h.shape[1]
    pitch = cols + 8
    bounds = [(lo, min(lo + 16, levels)) for lo in range(0, levels, 16)]
    pairs = [(send_h, send_v), (recv_h, recv_v), (edge_h, edge_v)]
    pairs += [(c_h.at[pl.ds(lo, hi - lo)], c_v.at[pl.ds(lo, hi - lo)]) for lo, hi in bounds]
    copies = [pltpu.make_async_copy(a, b, sems.at[i]) for i, (a, b) in enumerate(pairs)]
    for copy in copies:
        copy.start()
    parity = lax.bitwise_and(lax.axis_index(blk), jnp.int32(1))
    wts[...] = jnp.zeros_like(wts)
    for copy in copies[:3]:
        copy.wait()
    for slot in range(3):
        d = direction(slot, parity)
        weight = edge_v[d]
        if slot:
            weight = jnp.where(has_partner(slot, lax.axis_index(blk), lax.axis_size(blk)), weight, 0.0)
        wts[slot * nedge : (slot + 1) * nedge, 0:levels] = weight
        wts[3 * nedge + slot : 3 * nedge + slot + 1, 0:nedge] = recv_v[pl.ds(d, 1), :].astype(F32)
        wts[3 * nedge + 3 + slot : 3 * nedge + 4 + slot, 0:nedge] = send_v[pl.ds(d, 1), :].astype(F32)
    weights = wts[...].T
    wts_o[...] = weights
    source = source_columns(weights, nedge)
    rows_of = lambda s, lo, n: cf[pl.ds(lo * pitch + s, n, stride=pitch), :]
    for i, (lo, hi) in enumerate(bounds):
        copies[3 + i].wait()
        for l in range(lo, hi):
            cf[l * pitch : l * pitch + cols, :] = c_v[l].astype(F32)
        pack_chunk(lo, levels, nedge, source, weights, rows_of, (0, 1, 2), (s0, s1, s2))
    if levels % 16 == 0:
        pack_chunk(levels, levels, nedge, source, weights, rows_of, (0, 1, 2), (s0, s1, s2))


def column_operator(nbr_ref, nw_ref, sw_ref, a_ref, merged):
    levels = nw_ref.shape[0]
    cols = nbr_ref.shape[1]
    nbr = nbr_ref.shape[0]
    lane = lax.broadcasted_iota(jnp.int32, (8, cols), 1)
    sub = lax.broadcasted_iota(jnp.int32, (8, cols), 0)
    target = jnp.where(sub == nbr, lane, -1)
    for n in range(nbr):
        target = jnp.where(sub == n, nbr_ref[n : n + 1, :], target)
    same = [(target == nbr_ref[n : n + 1, :]).astype(F32) for n in range(nbr)]
    same.append((target == lane).astype(F32))
    for l in range(levels):
        total = same[nbr] * sw_ref[l : l + 1, :]
        for n in range(nbr):
            total = total + same[n] * nw_ref[l, n : n + 1, :]
        merged[l] = total
    half = 16
    for jt in range(cols // half):
        j = lax.broadcasted_iota(jnp.int32, (half, cols), 0) + jt * half
        hits = [j == nbr_ref[n : n + 1, :] for n in range(nbr)]
        hits.append(j == lax.broadcasted_iota(jnp.int32, (half, cols), 1))

        def fill(p, _):
            for i in range(2):
                value = jnp.zeros((half, cols), F32)
                for n in range(nbr, -1, -1):
                    value = jnp.where(hits[n], merged[p * 2 + i, n : n + 1, :], value)
                a_ref[p, jt * half : (jt + 1) * half, i * cols : (i + 1) * cols] = value.astype(BF16)
            return _

        lax.fori_loop(0, levels // 2, fill, 0, unroll=5)


def level_products(a_ref, state_of, exs, rows):
    pairs, cols, _ = a_ref.shape
    width = exs.shape[1]
    zero = jnp.zeros((cols, width), BF16)
    for p in range(pairs):
        left = jnp.concatenate([state_of(2 * p), zero], axis=1)
        right = jnp.concatenate([zero, state_of(2 * p + 1)], axis=1)
        both = jnp.dot(a_ref[p], jnp.concatenate([left, right], axis=0), preferred_element_type=F32)
        exs[pl.ds(2 * p, cols, stride=rows), :] = both[:, 0:width]
        exs[pl.ds(2 * p + 1, cols, stride=rows), :] = both[:, width:]
    for l in range(2 * pairs, rows):
        exs[pl.ds(l, cols, stride=rows), :] = jnp.zeros((cols, width), F32)


def operator_kernel(
    c_ref, nbr_h, nw_h, sw_h, wet_h, v_h, a_ref, state_ref, vt_ref,
    exs, merged, vf, vts, nbr_ref, nw_ref, sw_ref, wet_ref, v_ref, sems
):
    levels, cols, width = c_ref.shape
    rows = padded(levels)
    pairs = [(nbr_h, nbr_ref), (nw_h, nw_ref), (sw_h, sw_ref), (wet_h, wet_ref), (v_h, v_ref)]
    copies = [pltpu.make_async_copy(a, b, sems.at[i]) for i, (a, b) in enumerate(pairs)]
    for copy in copies:
        copy.start()
    for copy in copies[:4]:
        copy.wait()
    column_operator(nbr_ref, nw_ref, sw_ref, a_ref, merged)
    level_products(a_ref, lambda l: c_ref[l], exs, rows)
    level = lax.broadcasted_iota(jnp.int32, (levels, cols), 0)
    wet = wet_ref[...]
    copies[4].wait()
    vf[...] = jnp.zeros_like(vf)
    for m in range(levels):
        keep = jnp.maximum(level, m) < wet
        vf[m * rows : m * rows + levels, :] = jnp.where(keep, v_ref[m].astype(F32), 0.0)
    for l in range(rows):
        block = vf[pl.ds(l, rows, stride=rows), :]
        block = jnp.concatenate([block, jnp.zeros((128 - rows, cols), F32)], axis=0)
        vts[pl.ds(l, cols, stride=rows), :] = block.T
    vt_ref[...] = vts[...].reshape(cols, rows, 128).astype(BF16)
    vertical(vt_ref, exs, state_ref)


def arrived_kernel(levels, nedge, r0, r2, t0, t2, local_ref, vt_ref, total):
    add_edges(((r0, t0), (r2, t2)), levels, nedge, vt_ref, total)


def send_kernel(levels, nedge, r1, local_ref, vt_ref, wts_ref, state, s0, s1, s2):
    rows = vt_ref.shape[1]
    add_edges(((r1, r1),), levels, nedge, vt_ref, state)
    source = source_columns(wts_ref, nedge)
    rows_of = lambda s, lo, n: state[pl.ds(pl.multiple_of(s * rows + lo, 8), n), :]
    for lo in range(0, levels + 1, 16):
        pack_chunk(lo, levels, nedge, source, wts_ref, rows_of, (0, 1, 2), (s0, s1, s2))


def middle_kernel(cs, a_ref, vt_ref, out_ref, exs):
    cols, rows, _ = vt_ref.shape
    level_products(a_ref, lambda l: cs[pl.ds(l, cols, stride=rows), :].astype(BF16), exs, rows)
    vertical(vt_ref, exs, out_ref)


def last_kernel(nedge, r1, t1, local_ref, vt_ref, out_h, total, out_v, sems):
    levels, cols, width = out_h.shape
    rows = vt_ref.shape[1]
    add_edges(((r1, t1),), levels, nedge, vt_ref, total)
    bounds = [0, *range(4, levels, 8), levels]
    copies = []
    for i, (lo, hi) in enumerate(zip(bounds, bounds[1:])):
        for l in range(lo, hi):
            out_v[l] = total[pl.ds(l, cols, stride=rows), :].astype(BF16)
        copies.append(pltpu.make_async_copy(out_v.at[pl.ds(lo, hi - lo)], out_h.at[pl.ds(lo, hi - lo)], sems.at[i]))
        copies[-1].start()
    for copy in copies:
        copy.wait()


VM = pl.BlockSpec(memory_space=pltpu.VMEM)
HB = pl.BlockSpec(memory_space=pltpu.HBM)
DMA = pltpu.SemaphoreType.DMA


def call(kernel, ins, specs, outs, out_specs, scratch, limit, flops=0, aliases=None):
    size = sum(x.size * x.dtype.itemsize for x in (*ins, *outs))
    return pl.pallas_call(
        kernel,
        out_shape=outs,
        in_specs=specs,
        out_specs=out_specs,
        scratch_shapes=scratch,
        input_output_aliases=aliases or {},
        compiler_params=pltpu.CompilerParams(vmem_limit_bytes=limit * 2**20),
        cost_estimate=pl.CostEstimate(flops=flops, bytes_accessed=size, transcendentals=0),
    )(*ins)


def odd_or_even(value, first, blk, basin):
    n, b = lax.axis_size(blk), lax.axis_size(basin)
    partner = {i: i + 1 for i in range(first, n - 1, 2)}
    partner |= {j: i for i, j in partner.items()}
    across = lambda g: g ^ 1 if g ^ 1 < b else g
    route = [(g * n + i, g * n + partner[i] if i in partner else across(g) * n + i) for g in range(b) for i in range(n)]
    return lax.ppermute(value, (basin, blk), route)


def along_basin(value, basin):
    b = lax.axis_size(basin)
    return lax.ppermute(value, basin, [(i, (i + 1) % b) for i in range(b)])


def local(tracers, nbr_cols, nbr_wts, self_wts, send_cols, recv_cols, edge_wts, wet_levels, vert_inv):
    cols, levels, width = tracers.shape
    rows = padded(levels)
    nedge = send_cols.shape[1]
    shape = jax.ShapeDtypeStruct
    by_level = jnp.transpose(tracers, (1, 0, 2))
    nbr_by_level = jnp.transpose(nbr_wts, (1, 0, 2))
    edge_by_entry = jnp.transpose(edge_wts, (0, 2, 1))
    wet = wet_levels.reshape(1, cols)
    in_hbm = lambda x: pltpu.with_memory_space_constraint(x, pltpu.HBM)
    send_h = in_hbm(send_cols)
    loads = [nbr_cols, nbr_by_level, self_wts, wet]
    same = lambda x: shape(x.shape, x.dtype)
    message = shape((message_rows(levels, nedge), width), BF16)
    columns = shape((cols * rows, width), F32)
    flat = pltpu.VMEM(columns.shape, F32)

    first = call(
        functools.partial(gather_kernel, "blk"),
        (in_hbm(by_level), send_h, *map(in_hbm, (recv_cols, edge_by_entry))),
        [HB] * 4,
        [message] * 3 + [same(by_level), shape((128, 128), F32)],
        [VM] * 5,
        [
            pltpu.VMEM((rows * (cols + 8), width), F32),
            pltpu.VMEM((128, 128), F32), pltpu.VMEM(recv_cols.shape, jnp.int32), pltpu.VMEM(edge_by_entry.shape, F32),
            pltpu.VMEM(send_cols.shape, jnp.int32), DMA((3 + -(-levels // 16),)),
        ],
        16,
    )
    *messages, state, wts = first
    to_next, to_odd, to_even = messages
    operator_flops = 2 * levels * cols * cols * width
    vertical_flops = 2 * cols * rows * rows * width

    edge_flops = nedge * 2 * rows * rows * width

    def arrived(along, even, along_table, even_table, partial):
        return call(
            functools.partial(arrived_kernel, levels, nedge), (along, even, along_table, even_table, partial, vt), [VM] * 6,
            [columns], [VM], [], 16, flops=2 * edge_flops, aliases={4: 0},
        )[0]

    along = along_basin(to_next, "basin")
    odd = odd_or_even(to_odd, 1, "blk", "basin")
    even = odd_or_even(to_even, 0, "blk", "basin")
    operator, partial, vt = call(
        operator_kernel, (state, *map(in_hbm, (*loads, vert_inv))), [VM] + [HB] * 5,
        [shape((levels // 2, cols, 2 * cols), BF16), columns, shape((cols, rows, 128), BF16)], [VM] * 3,
        [flat, pltpu.VMEM((levels, 8, cols), F32), pltpu.VMEM((rows * rows, cols), F32), pltpu.VMEM((cols * rows, 128), F32),
         *[pltpu.VMEM(x.shape, x.dtype) for x in (*loads, vert_inv)], DMA((5,))],
        32, flops=operator_flops + vertical_flops,
    )
    state, to_next, to_odd, to_even = call(
        functools.partial(send_kernel, levels, nedge),
        (odd, arrived(along, even, along, even, partial), vt, wts), [VM] * 4,
        [columns] + [shape((levels * nedge, width), BF16)] * 3, [VM] * 4, [], 16, flops=edge_flops, aliases={1: 0},
    )
    tables = (along, odd, even)
    along = along_basin(to_next, "basin")
    odd = odd_or_even(to_odd, 1, "blk", "basin")
    even = odd_or_even(to_even, 0, "blk", "basin")
    (partial,) = call(
        middle_kernel, (state, operator, vt), [VM] * 3, [columns], [VM], [flat], 32, flops=operator_flops + vertical_flops,
    )
    out, _ = call(
        functools.partial(last_kernel, nedge), (odd, tables[1], arrived(along, even, tables[0], tables[2], partial), vt), [VM] * 4,
        [shape((levels, cols, width), BF16), columns], [HB, VM],
        [pltpu.VMEM((levels, cols, width), BF16), DMA((1 + -(-levels // 8),))], 16, flops=edge_flops, aliases={2: 1},
    )
    return jnp.transpose(out, (1, 0, 2))


def solution(mesh):
    in_specs = (
        P(("basin", "blk"), None, None),
        P(None, ("basin", "blk")),
        P(None, None, ("basin", "blk")),
        P(None, ("basin", "blk")),
        P(None, ("basin", "blk")),
        P(None, ("basin", "blk")),
        P(None, None, ("basin", "blk")),
        P(("basin", "blk")),
        P(None, None, ("basin", "blk")),
    )
    out_specs = P(("basin", "blk"), None, None)
    return jax.shard_map(local, mesh=mesh, in_specs=in_specs, out_specs=out_specs, check_vma=False)
```

```python
import functools

import jax
import jax.numpy as jnp
from jax import lax
from jax.experimental import pallas as pl
from jax.experimental.pallas import tpu as pltpu
from jax.sharding import PartitionSpec as P

NSTEP = 2
F32 = jnp.float32
BF16 = jnp.bfloat16


def padded(levels):
    return -(-levels // 8) * 8


def whole_rows(levels):
    return levels // 16 * 16


def message_rows(levels, nedge):
    return levels * nedge + 16


def direction(slot, parity):
    return lax.bitwise_xor(parity, jnp.int32(2 - slot)) if slot else 2


def has_partner(slot, at, count):
    first = lax.bitwise_and(at + slot // 2, jnp.int32(1)) == 1
    return jnp.where(first, at + 1 < count, at > 0)


def source_columns(weights, nedge):
    tables = [weights[0:nedge, 3 * nedge + 3 + slot : 3 * nedge + 4 + slot].astype(jnp.int32) for slot in range(3)]
    columns = [[table[e, 0] for e in range(nedge)] for table in tables]
    return lambda slot, e: columns[slot][e]


def pack_chunk(lo, levels, nedge, source, weights, rows_of, slots, outs):
    whole = whole_rows(levels)
    rest = levels - whole
    share = 8 // rest if rest else 0
    for slot, out in zip(slots, outs):
        if lo < whole:
            for e in range(nedge):
                k = slot * nedge + e
                value = rows_of(source(slot, e), lo, 16) * weights[lo : lo + 16, k : k + 1]
                out[e * whole + lo : e * whole + lo + 16, :] = value.astype(BF16)
            continue
        sub = lax.broadcasted_iota(jnp.int32, (8, out.shape[1]), 0)
        parts = []
        for first in range(0, nedge, share or nedge):
            part = None
            for q in range(share):
                k = slot * nedge + first + q
                value = rows_of(source(slot, first + q), lo, 8) * weights[lo : lo + 8, k : k + 1]
                if q:
                    value = pltpu.roll(value, q * rest, 0)
                part = value if part is None else jnp.where(sub >= q * rest, value, part)
            if share:
                parts.append(part)
        if out.shape[0] > levels * nedge:
            parts.append(jnp.broadcast_to(weights[0:16, 3 * nedge + slot : 3 * nedge + slot + 1], (16, out.shape[1])))
        if parts:
            out[nedge * whole :, :] = jnp.concatenate(parts, axis=0).astype(BF16)


def vertical(vt_ref, exs, out):
    cols, rows, _ = vt_ref.shape
    pad = jnp.zeros((64 - rows, out.shape[1]), F32)

    def column(j, _):
        at = pl.ds(pl.multiple_of(j * rows, 8), rows)
        x = jnp.concatenate([exs[at, :], pad], axis=0).astype(BF16)
        out[at, :] = jnp.dot(vt_ref[j][:, 0:64], x, preferred_element_type=F32)
        return _

    lax.fori_loop(0, cols, column, 0, unroll=16)


def add_edges(edges, levels, nedge, vt_ref, total):
    whole = whole_rows(levels)
    rest = levels - whole
    share = 8 // rest if rest else 0
    rows = vt_ref.shape[1]
    group = max(share, 4)
    pad = jnp.zeros((8, total.shape[1]), F32)
    for ref, first_ref in edges:
        table = first_ref[levels * nedge :, :].astype(F32).astype(jnp.int32)
        tails = ref[whole * nedge : levels * nedge, :].astype(F32) if rest else None
        for first in range(0, nedge, group):
            targets = [table[e, 0] for e in range(first, first + group)]
            products = []
            for e, j in zip(range(first, first + group), targets):
                x = ref[e * whole : (e + 1) * whole, :]
                if rest:
                    tail = tails[e // share * 8 : e // share * 8 + 8]
                    if e % share:
                        tail = pltpu.roll(tail, 8 - e % share * rest, 0)
                    x = jnp.concatenate([x, jnp.concatenate([tail, pad], axis=0).astype(BF16)], axis=0)
                products.append(jnp.dot(vt_ref[j][:, 0 : x.shape[0]], x, preferred_element_type=F32))
            for j, part in zip(targets, products):
                at = pl.ds(pl.multiple_of(j * rows, 8), rows)
                total[at, :] = total[at, :] + part


def gather_kernel(
    blk, c_h, send_h, recv_h, edge_h, nbr_h, nw_h, sw_h, wet_h,
    s0, s1, s2, c_v, nbr_v, nw_v, sw_v, wet_v, wts_o,
    cf, wts, recv_v, edge_v, send_v, sems,
):
    levels, cols, width = c_h.shape
    nedge = edge_h.shape[1]
    pitch = cols + 8
    whole = whole_rows(levels)
    bounds = [(lo, lo + 16 if lo + 16 < whole else levels) for lo in range(0, whole, 16)]
    pairs = [(send_h, send_v), (recv_h, recv_v), (edge_h, edge_v)]
    pairs += [(c_h.at[pl.ds(lo, hi - lo)], c_v.at[pl.ds(lo, hi - lo)]) for lo, hi in bounds]
    pairs += [(nbr_h, nbr_v), (nw_h, nw_v), (sw_h, sw_v), (wet_h, wet_v)]
    copies = [pltpu.make_async_copy(a, b, sems.at[i]) for i, (a, b) in enumerate(pairs)]
    for copy in copies:
        copy.start()
    parity = lax.bitwise_and(lax.axis_index(blk), jnp.int32(1))
    wts[...] = jnp.zeros_like(wts)
    for copy in copies[:3]:
        copy.wait()
    for slot in range(3):
        d = direction(slot, parity)
        weight = edge_v[d]
        if slot:
            weight = jnp.where(has_partner(slot, lax.axis_index(blk), lax.axis_size(blk)), weight, 0.0)
        wts[slot * nedge : (slot + 1) * nedge, 0:levels] = weight
        wts[3 * nedge + slot : 3 * nedge + slot + 1, 0:nedge] = recv_v[pl.ds(d, 1), :].astype(F32)
        wts[3 * nedge + 3 + slot : 3 * nedge + 4 + slot, 0:nedge] = send_v[pl.ds(d, 1), :].astype(F32)
    weights = wts[...].T
    wts_o[...] = weights
    source = source_columns(weights, nedge)
    rows_of = lambda s, lo, n: cf[pl.ds(lo * pitch + s, n, stride=pitch), :]
    for i, (lo, hi) in enumerate(bounds):
        copies[3 + i].wait()
        for l in range(lo, hi):
            cf[l * pitch : l * pitch + cols, :] = c_v[l].astype(F32)
        pack_chunk(lo, levels, nedge, source, weights, rows_of, (0, 1, 2), (s0, s1, s2))
    pack_chunk(whole, levels, nedge, source, weights, rows_of, (0, 1, 2), (s0, s1, s2))
    for copy in copies[3 + len(bounds) :]:
        copy.wait()


def column_operator(nbr_ref, nw_ref, sw_ref, a_ref, merged):
    levels = nw_ref.shape[0]
    cols = nbr_ref.shape[1]
    nbr = nbr_ref.shape[0]
    lane = lax.broadcasted_iota(jnp.int32, (8, cols), 1)
    sub = lax.broadcasted_iota(jnp.int32, (8, cols), 0)
    target = jnp.where(sub == nbr, lane, -1)
    for n in range(nbr):
        target = jnp.where(sub == n, nbr_ref[n : n + 1, :], target)
    same = [(target == nbr_ref[n : n + 1, :]).astype(F32) for n in range(nbr)]
    same.append((target == lane).astype(F32))
    for l in range(levels):
        total = same[nbr] * sw_ref[l : l + 1, :]
        for n in range(nbr):
            total = total + same[n] * nw_ref[l, n : n + 1, :]
        merged[l] = total
    half = 16
    for jt in range(cols // half):
        j = lax.broadcasted_iota(jnp.int32, (half, cols), 0) + jt * half
        hits = [j == nbr_ref[n : n + 1, :] for n in range(nbr)]
        hits.append(j == lax.broadcasted_iota(jnp.int32, (half, cols), 1))

        def fill(p, _):
            for i in range(2):
                value = jnp.zeros((half, cols), F32)
                for n in range(nbr, -1, -1):
                    value = jnp.where(hits[n], merged[p * 2 + i, n : n + 1, :], value)
                a_ref[p, jt * half : (jt + 1) * half, i * cols : (i + 1) * cols] = value.astype(BF16)
            return _

        lax.fori_loop(0, levels // 2, fill, 0, unroll=5)


def level_products(a_ref, state_of, exs, rows):
    pairs, cols, _ = a_ref.shape
    width = exs.shape[1]
    zero = jnp.zeros((cols, width), BF16)
    for p in range(pairs):
        left = jnp.concatenate([state_of(2 * p), zero], axis=1)
        right = jnp.concatenate([zero, state_of(2 * p + 1)], axis=1)
        both = jnp.dot(a_ref[p], jnp.concatenate([left, right], axis=0), preferred_element_type=F32)
        exs[pl.ds(2 * p, cols, stride=rows), :] = both[:, 0:width]
        exs[pl.ds(2 * p + 1, cols, stride=rows), :] = both[:, width:]
    for l in range(2 * pairs, rows):
        exs[pl.ds(l, cols, stride=rows), :] = jnp.zeros((cols, width), F32)


def operator_kernel(
    c_ref, nbr_ref, nw_ref, sw_ref, wet_ref, v_h, a_ref, state_ref, vt_ref, exs, merged, vf, vts, v_ref, sem
):
    levels, cols, width = c_ref.shape
    rows = padded(levels)
    load = pltpu.make_async_copy(v_h, v_ref, sem)
    load.start()
    column_operator(nbr_ref, nw_ref, sw_ref, a_ref, merged)
    level_products(a_ref, lambda l: c_ref[l], exs, rows)
    level = lax.broadcasted_iota(jnp.int32, (levels, cols), 0)
    wet = wet_ref[...]
    load.wait()
    vf[...] = jnp.zeros_like(vf)
    for m in range(levels):
        keep = jnp.maximum(level, m) < wet
        vf[m * rows : m * rows + levels, :] = jnp.where(keep, v_ref[m].astype(F32), 0.0)
    for l in range(rows):
        block = vf[pl.ds(l, rows, stride=rows), :]
        block = jnp.concatenate([block, jnp.zeros((128 - rows, cols), F32)], axis=0)
        vts[pl.ds(l, cols, stride=rows), :] = block.T
    vt_ref[...] = vts[...].reshape(cols, rows, 128).astype(BF16)
    vertical(vt_ref, exs, state_ref)


def arrived_kernel(levels, nedge, r0, r2, t0, t2, local_ref, vt_ref, total):
    add_edges(((r0, t0), (r2, t2)), levels, nedge, vt_ref, total)


def send_kernel(levels, nedge, r1, local_ref, vt_ref, wts_ref, state, s0, s1, s2):
    rows = vt_ref.shape[1]
    add_edges(((r1, r1),), levels, nedge, vt_ref, state)
    source = source_columns(wts_ref, nedge)
    rows_of = lambda s, lo, n: state[pl.ds(pl.multiple_of(s * rows + lo, 8), n), :]
    for lo in range(0, levels + 1, 16):
        pack_chunk(lo, levels, nedge, source, wts_ref, rows_of, (0, 1, 2), (s0, s1, s2))


def middle_kernel(cs, a_ref, vt_ref, out_ref, exs):
    cols, rows, _ = vt_ref.shape
    level_products(a_ref, lambda l: cs[pl.ds(l, cols, stride=rows), :].astype(BF16), exs, rows)
    vertical(vt_ref, exs, out_ref)


def last_kernel(nedge, r1, t1, local_ref, vt_ref, out_h, total, out_v, sems):
    levels, cols, width = out_h.shape
    rows = vt_ref.shape[1]
    add_edges(((r1, t1),), levels, nedge, vt_ref, total)
    bounds = [0, *range(8, levels - 8, 14), levels]
    copies = []
    for i, (lo, hi) in enumerate(zip(bounds, bounds[1:])):
        for l in range(lo, hi):
            out_v[l] = total[pl.ds(l, cols, stride=rows), :].astype(BF16)
        copies.append(pltpu.make_async_copy(out_v.at[pl.ds(lo, hi - lo)], out_h.at[pl.ds(lo, hi - lo)], sems.at[i]))
        copies[-1].start()
    for copy in copies:
        copy.wait()


VM = pl.BlockSpec(memory_space=pltpu.VMEM)
HB = pl.BlockSpec(memory_space=pltpu.HBM)
DMA = pltpu.SemaphoreType.DMA


def call(kernel, ins, specs, outs, out_specs, scratch, limit, flops=0, aliases=None):
    size = sum(x.size * x.dtype.itemsize for x in (*ins, *outs))
    return pl.pallas_call(
        kernel,
        out_shape=outs,
        in_specs=specs,
        out_specs=out_specs,
        scratch_shapes=scratch,
        input_output_aliases=aliases or {},
        compiler_params=pltpu.CompilerParams(vmem_limit_bytes=limit * 2**20),
        cost_estimate=pl.CostEstimate(flops=flops, bytes_accessed=size, transcendentals=0),
    )(*ins)


def odd_or_even(value, first, blk, basin):
    n, b = lax.axis_size(blk), lax.axis_size(basin)
    partner = {i: i + 1 for i in range(first, n - 1, 2)}
    partner |= {j: i for i, j in partner.items()}
    across = lambda g: g ^ 1 if g ^ 1 < b else g
    route = [(g * n + i, g * n + partner[i] if i in partner else across(g) * n + i) for g in range(b) for i in range(n)]
    return lax.ppermute(value, (basin, blk), route)


def along_basin(value, basin):
    b = lax.axis_size(basin)
    return lax.ppermute(value, basin, [(i, (i + 1) % b) for i in range(b)])


def local(tracers, nbr_cols, nbr_wts, self_wts, send_cols, recv_cols, edge_wts, wet_levels, vert_inv):
    cols, levels, width = tracers.shape
    rows = padded(levels)
    nedge = send_cols.shape[1]
    shape = jax.ShapeDtypeStruct
    by_level = jnp.transpose(tracers, (1, 0, 2))
    nbr_by_level = jnp.transpose(nbr_wts, (1, 0, 2))
    edge_by_entry = jnp.transpose(edge_wts, (0, 2, 1))
    wet = wet_levels.reshape(1, cols)
    in_hbm = lambda x: pltpu.with_memory_space_constraint(x, pltpu.HBM)
    send_h = in_hbm(send_cols)
    loads = [by_level, nbr_cols, nbr_by_level, self_wts, wet]
    same = lambda x: shape(x.shape, x.dtype)
    message = shape((message_rows(levels, nedge), width), BF16)
    columns = shape((cols * rows, width), F32)
    flat = pltpu.VMEM(columns.shape, F32)

    first = call(
        functools.partial(gather_kernel, "blk"),
        (in_hbm(by_level), send_h, *map(in_hbm, (recv_cols, edge_by_entry, *loads[1:]))),
        [HB] * 8,
        [message] * 3 + [same(x) for x in loads] + [shape((128, 128), F32)],
        [VM] * 9,
        [
            pltpu.VMEM((rows * (cols + 8), width), F32),
            pltpu.VMEM((128, 128), F32), pltpu.VMEM(recv_cols.shape, jnp.int32), pltpu.VMEM(edge_by_entry.shape, F32),
            pltpu.VMEM(send_cols.shape, jnp.int32), DMA((7 + -(-levels // 16),)),
        ],
        16,
    )
    (to_next, to_odd, to_even), loads, wts = first[:3], first[3:8], first[8]
    operator_flops = 2 * levels * cols * cols * width
    vertical_flops = 2 * cols * rows * rows * width

    edge_flops = nedge * 2 * rows * rows * width

    def arrived(along, even, along_table, even_table, partial):
        return call(
            functools.partial(arrived_kernel, levels, nedge), (along, even, along_table, even_table, partial, vt), [VM] * 6,
            [columns], [VM], [], 16, flops=2 * edge_flops, aliases={4: 0},
        )[0]

    along = along_basin(to_next, "basin")
    odd = odd_or_even(to_odd, 1, "blk", "basin")
    even = odd_or_even(to_even, 0, "blk", "basin")
    operator, partial, vt = call(
        operator_kernel, (*loads, in_hbm(vert_inv)), [VM] * 5 + [HB],
        [shape((levels // 2, cols, 2 * cols), BF16), columns, shape((cols, rows, 128), BF16)], [VM] * 3,
        [flat, pltpu.VMEM((levels, 8, cols), F32), pltpu.VMEM((rows * rows, cols), F32), pltpu.VMEM((cols * rows, 128), F32),
         pltpu.VMEM(vert_inv.shape, BF16), DMA],
        32, flops=operator_flops + vertical_flops,
    )
    state, to_next, to_odd, to_even = call(
        functools.partial(send_kernel, levels, nedge),
        (odd, arrived(along, even, along, even, partial), vt, wts), [VM] * 4,
        [columns] + [shape((levels * nedge, width), BF16)] * 3, [VM] * 4, [], 16, flops=edge_flops, aliases={1: 0},
    )
    tables = (along, odd, even)
    along = along_basin(to_next, "basin")
    odd = odd_or_even(to_odd, 1, "blk", "basin")
    even = odd_or_even(to_even, 0, "blk", "basin")
    (partial,) = call(
        middle_kernel, (state, operator, vt), [VM] * 3, [columns], [VM], [flat], 32, flops=operator_flops + vertical_flops,
    )
    out, _ = call(
        functools.partial(last_kernel, nedge), (odd, tables[1], arrived(along, even, tables[0], tables[2], partial), vt), [VM] * 4,
        [shape((levels, cols, width), BF16), columns], [HB, VM],
        [pltpu.VMEM((levels, cols, width), BF16), DMA((1 + -(-levels // 8),))], 16, flops=edge_flops, aliases={2: 1},
    )
    return jnp.transpose(out, (1, 0, 2))


def solution(mesh):
    in_specs = (
        P(("basin", "blk"), None, None),
        P(None, ("basin", "blk")),
        P(None, None, ("basin", "blk")),
        P(None, ("basin", "blk")),
        P(None, ("basin", "blk")),
        P(None, ("basin", "blk")),
        P(None, None, ("basin", "blk")),
        P(("basin", "blk")),
        P(None, None, ("basin", "blk")),
    )
    out_specs = P(("basin", "blk"), None, None)
    return jax.shard_map(local, mesh=mesh, in_specs=in_specs, out_specs=out_specs, check_vma=False)
```

```python
import functools

import jax
import jax.numpy as jnp
from jax import lax
from jax.experimental import pallas as pl
from jax.experimental.pallas import tpu as pltpu
from jax.sharding import PartitionSpec as P

NSTEP = 2
F32 = jnp.float32
BF16 = jnp.bfloat16


def padded(levels):
    return -(-levels // 8) * 8


def whole_rows(levels):
    return levels // 16 * 16


def message_rows(levels, nedge):
    return levels * nedge + 16


def direction(slot, parity):
    return lax.bitwise_xor(parity, jnp.int32(2 - slot)) if slot else 2


def has_partner(slot, at, count):
    first = lax.bitwise_and(at + slot // 2, jnp.int32(1)) == 1
    return jnp.where(first, at + 1 < count, at > 0)


def source_columns(weights, nedge):
    tables = [weights[0:nedge, 3 * nedge + 3 + slot : 3 * nedge + 4 + slot].astype(jnp.int32) for slot in range(3)]
    columns = [[table[e, 0] for e in range(nedge)] for table in tables]
    return lambda slot, e: columns[slot][e]


def pack_chunk(lo, levels, nedge, source, weights, rows_of, slots, outs):
    whole = whole_rows(levels)
    rest = levels - whole
    share = 8 // rest if rest else 0
    for slot, out in zip(slots, outs):
        if lo < whole:
            for e in range(nedge):
                k = slot * nedge + e
                value = rows_of(source(slot, e), lo, 16) * weights[lo : lo + 16, k : k + 1]
                out[e * whole + lo : e * whole + lo + 16, :] = value.astype(BF16)
            continue
        sub = lax.broadcasted_iota(jnp.int32, (8, out.shape[1]), 0)
        parts = []
        for first in range(0, nedge, share or nedge):
            part = None
            for q in range(share):
                k = slot * nedge + first + q
                value = rows_of(source(slot, first + q), lo, 8) * weights[lo : lo + 8, k : k + 1]
                if q:
                    value = pltpu.roll(value, q * rest, 0)
                part = value if part is None else jnp.where(sub >= q * rest, value, part)
            if share:
                parts.append(part)
        if out.shape[0] > levels * nedge:
            parts.append(jnp.broadcast_to(weights[0:16, 3 * nedge + slot : 3 * nedge + slot + 1], (16, out.shape[1])))
        if parts:
            out[nedge * whole :, :] = jnp.concatenate(parts, axis=0).astype(BF16)


def vertical(vt_ref, exs, out):
    cols, rows, _ = vt_ref.shape
    pad = jnp.zeros((64 - rows, out.shape[1]), F32)

    def column(j, _):
        at = pl.ds(pl.multiple_of(j * rows, 8), rows)
        x = jnp.concatenate([exs[at, :], pad], axis=0).astype(BF16)
        out[at, :] = jnp.dot(vt_ref[j][:, 0:64], x, preferred_element_type=F32)
        return _

    lax.fori_loop(0, cols, column, 0, unroll=16)


def add_edges(edges, levels, nedge, vt_ref, total):
    whole = whole_rows(levels)
    rest = levels - whole
    share = 8 // rest if rest else 0
    rows = vt_ref.shape[1]
    group = max(share, 4)
    pad = jnp.zeros((8, total.shape[1]), F32)
    for ref, first_ref in edges:
        table = first_ref[levels * nedge :, :].astype(F32).astype(jnp.int32)
        tails = ref[whole * nedge : levels * nedge, :].astype(F32) if rest else None
        for first in range(0, nedge, group):
            targets = [table[e, 0] for e in range(first, first + group)]
            products = []
            for e, j in zip(range(first, first + group), targets):
                x = ref[e * whole : (e + 1) * whole, :]
                if rest:
                    tail = tails[e // share * 8 : e // share * 8 + 8]
                    if e % share:
                        tail = pltpu.roll(tail, 8 - e % share * rest, 0)
                    x = jnp.concatenate([x, jnp.concatenate([tail, pad], axis=0).astype(BF16)], axis=0)
                products.append(jnp.dot(vt_ref[j][:, 0 : x.shape[0]], x, preferred_element_type=F32))
            for j, part in zip(targets, products):
                at = pl.ds(pl.multiple_of(j * rows, 8), rows)
                total[at, :] = total[at, :] + part


def gather_kernel(
    blk, c_h, send_h, recv_h, edge_h, nbr_h, nw_h, sw_h, wet_h,
    s0, s1, s2, c_v, nbr_v, nw_v, sw_v, wet_v, wts_o,
    cf, wts, recv_v, edge_v, send_v, sems,
):
    levels, cols, width = c_h.shape
    nedge = edge_h.shape[1]
    pitch = cols + 8
    whole = whole_rows(levels)
    bounds = [(lo, lo + 16 if lo + 16 < whole else levels) for lo in range(0, whole, 16)]
    pairs = [(send_h, send_v), (recv_h, recv_v), (edge_h, edge_v)]
    pairs += [(c_h.at[pl.ds(lo, hi - lo)], c_v.at[pl.ds(lo, hi - lo)]) for lo, hi in bounds]
    pairs += [(nbr_h, nbr_v), (nw_h, nw_v), (sw_h, sw_v), (wet_h, wet_v)]
    copies = [pltpu.make_async_copy(a, b, sems.at[i]) for i, (a, b) in enumerate(pairs)]
    for copy in copies:
        copy.start()
    parity = lax.bitwise_and(lax.axis_index(blk), jnp.int32(1))
    wts[...] = jnp.zeros_like(wts)
    for copy in copies[:3]:
        copy.wait()
    for slot in range(3):
        d = direction(slot, parity)
        weight = edge_v[d]
        if slot:
            weight = jnp.where(has_partner(slot, lax.axis_index(blk), lax.axis_size(blk)), weight, 0.0)
        wts[slot * nedge : (slot + 1) * nedge, 0:levels] = weight
        wts[3 * nedge + slot : 3 * nedge + slot + 1, 0:nedge] = recv_v[pl.ds(d, 1), :].astype(F32)
        wts[3 * nedge + 3 + slot : 3 * nedge + 4 + slot, 0:nedge] = send_v[pl.ds(d, 1), :].astype(F32)
    weights = wts[...].T
    wts_o[...] = weights
    source = source_columns(weights, nedge)
    rows_of = lambda s, lo, n: cf[pl.ds(lo * pitch + s, n, stride=pitch), :]
    for i, (lo, hi) in enumerate(bounds):
        copies[3 + i].wait()
        for l in range(lo, hi):
            cf[l * pitch : l * pitch + cols, :] = c_v[l].astype(F32)
        pack_chunk(lo, levels, nedge, source, weights, rows_of, (0, 1, 2), (s0, s1, s2))
    pack_chunk(whole, levels, nedge, source, weights, rows_of, (0, 1, 2), (s0, s1, s2))
    for copy in copies[3 + len(bounds) :]:
        copy.wait()


def column_operator(nbr_ref, nw_ref, sw_ref, a_ref, merged):
    levels = nw_ref.shape[0]
    cols = nbr_ref.shape[1]
    nbr = nbr_ref.shape[0]
    lane = lax.broadcasted_iota(jnp.int32, (8, cols), 1)
    sub = lax.broadcasted_iota(jnp.int32, (8, cols), 0)
    target = jnp.where(sub == nbr, lane, -1)
    for n in range(nbr):
        target = jnp.where(sub == n, nbr_ref[n : n + 1, :], target)
    same = [(target == nbr_ref[n : n + 1, :]).astype(F32) for n in range(nbr)]
    same.append((target == lane).astype(F32))
    for l in range(levels):
        total = same[nbr] * sw_ref[l : l + 1, :]
        for n in range(nbr):
            total = total + same[n] * nw_ref[l, n : n + 1, :]
        merged[l] = total
    half = 16
    for jt in range(cols // half):
        j = lax.broadcasted_iota(jnp.int32, (half, cols), 0) + jt * half
        hits = [j == nbr_ref[n : n + 1, :] for n in range(nbr)]
        hits.append(j == lax.broadcasted_iota(jnp.int32, (half, cols), 1))

        def fill(p, _):
            for i in range(2):
                value = jnp.zeros((half, cols), F32)
                for n in range(nbr, -1, -1):
                    value = jnp.where(hits[n], merged[p * 2 + i, n : n + 1, :], value)
                a_ref[p, jt * half : (jt + 1) * half, i * cols : (i + 1) * cols] = value.astype(BF16)
            return _

        lax.fori_loop(0, levels // 2, fill, 0, unroll=5)


def level_products(a_ref, state_of, exs, rows):
    pairs, cols, _ = a_ref.shape
    width = exs.shape[1]
    zero = jnp.zeros((cols, width), BF16)
    for p in range(pairs):
        left = jnp.concatenate([state_of(2 * p), zero], axis=1)
        right = jnp.concatenate([zero, state_of(2 * p + 1)], axis=1)
        both = jnp.dot(a_ref[p], jnp.concatenate([left, right], axis=0), preferred_element_type=F32)
        exs[pl.ds(2 * p, cols, stride=rows), :] = both[:, 0:width]
        exs[pl.ds(2 * p + 1, cols, stride=rows), :] = both[:, width:]
    for l in range(2 * pairs, rows):
        exs[pl.ds(l, cols, stride=rows), :] = jnp.zeros((cols, width), F32)


def operator_kernel(
    c_ref, nbr_ref, nw_ref, sw_ref, wet_ref, v_h, a_ref, state_ref, vt_ref, exs, merged, vf, vts, v_ref, sem
):
    levels, cols, width = c_ref.shape
    rows = padded(levels)
    load = pltpu.make_async_copy(v_h, v_ref, sem)
    load.start()
    column_operator(nbr_ref, nw_ref, sw_ref, a_ref, merged)
    level_products(a_ref, lambda l: c_ref[l], exs, rows)
    level = lax.broadcasted_iota(jnp.int32, (levels, cols), 0)
    wet = wet_ref[...]
    load.wait()
    vf[...] = jnp.zeros_like(vf)
    for m in range(levels):
        keep = jnp.maximum(level, m) < wet
        vf[m * rows : m * rows + levels, :] = jnp.where(keep, v_ref[m].astype(F32), 0.0)
    for l in range(rows):
        block = vf[pl.ds(l, rows, stride=rows), :]
        block = jnp.concatenate([block, jnp.zeros((128 - rows, cols), F32)], axis=0)
        vts[pl.ds(l, cols, stride=rows), :] = block.T
    vt_ref[...] = vts[...].reshape(cols, rows, 128).astype(BF16)
    vertical(vt_ref, exs, state_ref)


def arrived_kernel(levels, nedge, r0, r2, t0, t2, local_ref, vt_ref, total):
    add_edges(((r0, t0), (r2, t2)), levels, nedge, vt_ref, total)


def send_kernel(levels, nedge, r1, local_ref, vt_ref, wts_ref, state, s0, s1, s2):
    rows = vt_ref.shape[1]
    add_edges(((r1, r1),), levels, nedge, vt_ref, state)
    source = source_columns(wts_ref, nedge)
    rows_of = lambda s, lo, n: state[pl.ds(pl.multiple_of(s * rows + lo, 8), n), :]
    for lo in range(0, levels + 1, 16):
        pack_chunk(lo, levels, nedge, source, wts_ref, rows_of, (0, 1, 2), (s0, s1, s2))


def middle_kernel(cs, a_ref, vt_ref, out_ref, exs):
    cols, rows, _ = vt_ref.shape
    level_products(a_ref, lambda l: cs[pl.ds(l, cols, stride=rows), :].astype(BF16), exs, rows)
    vertical(vt_ref, exs, out_ref)


def last_kernel(nedge, r1, t1, local_ref, vt_ref, out_h, total, out_v, sems):
    levels, cols, width = out_h.shape
    rows = vt_ref.shape[1]
    add_edges(((r1, t1),), levels, nedge, vt_ref, total)
    bounds = [0, *range(4, levels, 8), levels]
    copies = []
    for i, (lo, hi) in enumerate(zip(bounds, bounds[1:])):
        for l in range(lo, hi):
            out_v[l] = total[pl.ds(l, cols, stride=rows), :].astype(BF16)
        copies.append(pltpu.make_async_copy(out_v.at[pl.ds(lo, hi - lo)], out_h.at[pl.ds(lo, hi - lo)], sems.at[i]))
        copies[-1].start()
    for copy in copies:
        copy.wait()


VM = pl.BlockSpec(memory_space=pltpu.VMEM)
HB = pl.BlockSpec(memory_space=pltpu.HBM)
DMA = pltpu.SemaphoreType.DMA


def call(kernel, ins, specs, outs, out_specs, scratch, limit, flops=0, aliases=None):
    size = sum(x.size * x.dtype.itemsize for x in (*ins, *outs))
    return pl.pallas_call(
        kernel,
        out_shape=outs,
        in_specs=specs,
        out_specs=out_specs,
        scratch_shapes=scratch,
        input_output_aliases=aliases or {},
        compiler_params=pltpu.CompilerParams(vmem_limit_bytes=limit * 2**20),
        cost_estimate=pl.CostEstimate(flops=flops, bytes_accessed=size, transcendentals=0),
    )(*ins)


def odd_or_even(value, first, blk, basin):
    n, b = lax.axis_size(blk), lax.axis_size(basin)
    partner = {i: i + 1 for i in range(first, n - 1, 2)}
    partner |= {j: i for i, j in partner.items()}
    across = lambda g: g ^ 1 if g ^ 1 < b else g
    route = [(g * n + i, g * n + partner[i] if i in partner else across(g) * n + i) for g in range(b) for i in range(n)]
    return lax.ppermute(value, (basin, blk), route)


def along_basin(value, basin):
    b = lax.axis_size(basin)
    return lax.ppermute(value, basin, [(i, (i + 1) % b) for i in range(b)])


def local(tracers, nbr_cols, nbr_wts, self_wts, send_cols, recv_cols, edge_wts, wet_levels, vert_inv):
    cols, levels, width = tracers.shape
    rows = padded(levels)
    nedge = send_cols.shape[1]
    shape = jax.ShapeDtypeStruct
    by_level = jnp.transpose(tracers, (1, 0, 2))
    nbr_by_level = jnp.transpose(nbr_wts, (1, 0, 2))
    edge_by_entry = jnp.transpose(edge_wts, (0, 2, 1))
    wet = wet_levels.reshape(1, cols)
    in_hbm = lambda x: pltpu.with_memory_space_constraint(x, pltpu.HBM)
    send_h = in_hbm(send_cols)
    loads = [by_level, nbr_cols, nbr_by_level, self_wts, wet]
    same = lambda x: shape(x.shape, x.dtype)
    message = shape((message_rows(levels, nedge), width), BF16)
    columns = shape((cols * rows, width), F32)
    flat = pltpu.VMEM(columns.shape, F32)

    first = call(
        functools.partial(gather_kernel, "blk"),
        (in_hbm(by_level), send_h, *map(in_hbm, (recv_cols, edge_by_entry, *loads[1:]))),
        [HB] * 8,
        [message] * 3 + [same(x) for x in loads] + [shape((128, 128), F32)],
        [VM] * 9,
        [
            pltpu.VMEM((rows * (cols + 8), width), F32),
            pltpu.VMEM((128, 128), F32), pltpu.VMEM(recv_cols.shape, jnp.int32), pltpu.VMEM(edge_by_entry.shape, F32),
            pltpu.VMEM(send_cols.shape, jnp.int32), DMA((7 + -(-levels // 16),)),
        ],
        16,
    )
    (to_next, to_odd, to_even), loads, wts = first[:3], first[3:8], first[8]
    operator_flops = 2 * levels * cols * cols * width
    vertical_flops = 2 * cols * rows * rows * width

    edge_flops = nedge * 2 * rows * rows * width

    def arrived(along, even, along_table, even_table, partial):
        return call(
            functools.partial(arrived_kernel, levels, nedge), (along, even, along_table, even_table, partial, vt), [VM] * 6,
            [columns], [VM], [], 16, flops=2 * edge_flops, aliases={4: 0},
        )[0]

    along = along_basin(to_next, "basin")
    odd = odd_or_even(to_odd, 1, "blk", "basin")
    even = odd_or_even(to_even, 0, "blk", "basin")
    operator, partial, vt = call(
        operator_kernel, (*loads, in_hbm(vert_inv)), [VM] * 5 + [HB],
        [shape((levels // 2, cols, 2 * cols), BF16), columns, shape((cols, rows, 128), BF16)], [VM] * 3,
        [flat, pltpu.VMEM((levels, 8, cols), F32), pltpu.VMEM((rows * rows, cols), F32), pltpu.VMEM((cols * rows, 128), F32),
         pltpu.VMEM(vert_inv.shape, BF16), DMA],
        32, flops=operator_flops + vertical_flops,
    )
    state, to_next, to_odd, to_even = call(
        functools.partial(send_kernel, levels, nedge),
        (odd, arrived(along, even, along, even, partial), vt, wts), [VM] * 4,
        [columns] + [shape((levels * nedge, width), BF16)] * 3, [VM] * 4, [], 16, flops=edge_flops, aliases={1: 0},
    )
    tables = (along, odd, even)
    along = along_basin(to_next, "basin")
    odd = odd_or_even(to_odd, 1, "blk", "basin")
    even = odd_or_even(to_even, 0, "blk", "basin")
    (partial,) = call(
        middle_kernel, (state, operator, vt), [VM] * 3, [columns], [VM], [flat], 32, flops=operator_flops + vertical_flops,
    )
    out, _ = call(
        functools.partial(last_kernel, nedge), (odd, tables[1], arrived(along, even, tables[0], tables[2], partial), vt), [VM] * 4,
        [shape((levels, cols, width), BF16), columns], [HB, VM],
        [pltpu.VMEM((levels, cols, width), BF16), DMA((1 + -(-levels // 8),))], 16, flops=edge_flops, aliases={2: 1},
    )
    return jnp.transpose(out, (1, 0, 2))


def solution(mesh):
    in_specs = (
        P(("basin", "blk"), None, None),
        P(None, ("basin", "blk")),
        P(None, None, ("basin", "blk")),
        P(None, ("basin", "blk")),
        P(None, ("basin", "blk")),
        P(None, ("basin", "blk")),
        P(None, None, ("basin", "blk")),
        P(("basin", "blk")),
        P(None, None, ("basin", "blk")),
    )
    out_specs = P(("basin", "blk"), None, None)
    return jax.shard_map(local, mesh=mesh, in_specs=in_specs, out_specs=out_specs, check_vma=False)
```
